32 devices in a mesh: section: 4 (over y, x), expert: 8 (over z, core).
Axes of the slice: x: 2, y: 2, z: 4, core: 2. Of those that a mesh axis runs over, the one named last changes fastest.
Arguments:
- forward_sent: bfloat16 [4, 512, 2048], P('section', 'expert'), may hold values from -6 to 6
- embedded: bfloat16 [512, 2048], P('expert'), may hold values from -6 to 6
- forward_routes: int32 [4, 512, 2], P('section', 'expert'), may hold values from 0 to 63, all different within a row; in each aligned block of 64 rows (0 to 63, 64 to 127, ..., all dimensions but the last counted through in order) at most 3 rows name the same one
- backward_sent: bfloat16 [4, 512, 2048], P('section', 'expert'), may hold values from -6 to 6
- loss_gradient: bfloat16 [512, 2048], P('expert'), may hold values from -6 to 6
- saved_inputs: bfloat16 [4, 512, 2048], P('section', 'expert'), may hold values from -6 to 6
- backward_routes: int32 [4, 512, 2], P('section', 'expert'), may hold values from 0 to 63, all different within a row; in each aligned block of 64 rows (0 to 63, 64 to 127, ..., all dimensions but the last counted through in order) at most 3 rows name the same one
- pre_activation: bfloat16 [4, 8, 64, 3, 1024], P('section', None, 'expert'), may hold values from -6 to 6
- norm_gain: bfloat16 [4, 2048], P('section'), may hold values from 0.099609375 to 1.8984375
- router: bfloat16 [4, 2048, 64], P('section'), may hold values from -0.125 to 0.125
- up_weight: bfloat16 [64, 2048, 1024], P('expert'), may hold values from -0.125 to 0.125
- down_weight: bfloat16 [64, 1024, 2048], P('expert'), may hold values from -0.1875 to 0.1875
Outputs:
- forward_output: bfloat16 [4, 512, 2048], P('section', 'expert')
- input_gradient: bfloat16 [4, 512, 2048], P('section', 'expert')
The draws below stay inside these ranges and needn't reach their ends.
Inputs may be any that keep to these rules, and one draw needn't show every extreme that they name: `forward_routes`: in each aligned block of 64 rows (one device's tokens at one section) no expert is named by more than 3 rows, a bound that some block reaches; the 2 entries of a row differ. `backward_routes`: in each aligned block of 64 rows (one device's tokens at one section) no expert is named by more than 3 rows, a bound that some block reaches; the 2 entries of a row differ.
All inputs are finite; a program needn't handle non-finite values.
Results may differ from the reference program's by a relative error of at most 0.0053.
Values may be sent and summed in bfloat16 or wider, within the bound.
No kernel may reach another device: no remote copies, remote signals or barrier semaphores. Data moves between devices by JAX's collectives and lax.ppermute only.
A program may use at most 128 MiB of HBM per device.

```python
import math
import jax
import jax.numpy as jnp
import numpy as np
from jax import lax

D = 2048
FF = 1024
EXPERTS = 64
TOP = 2
TOK_DEV = 64
CAP = 3
SECTIONS = 4
BLOCKS = 8
TOKENS = 512


def block_scale(key, shape, split, low, high):
    loudness = 1.0
    for position, blocks in split:
        steps = jax.random.uniform(jax.random.fold_in(jax.random.fold_in(key, 6), position), (blocks,), jnp.float32, low / len(split), high / len(split))
        loudness = loudness * jnp.repeat(jnp.exp(steps), shape[position] // blocks).reshape((-1,) + (1,) * (len(shape) - 1 - position))
    return loudness


def assign_block(key, own, number, rows, amount, top, reach, slope):
    order = jax.random.permutation(key, amount)
    crowded, usual = portions_of(amount, rows * top, reach, slope, True), portions_of(amount, rows * top, reach, slope, False)
    places = jnp.arange(amount)

    def named(tallies, turn):
        used = int((tallies > 0).sum())
        fixed = max(1, used // 4)
        moved = fixed + (places - fixed + turn * (used - fixed)) % max(1, amount - fixed)
        return jnp.zeros((amount,), jnp.int32).at[order[jnp.where(places < fixed, places, moved)]].set(jnp.asarray(tallies, jnp.int32))

    tallies = jnp.where(number % 4 == 0, named(crowded, number // 4), named(usual, number - number // 4 - 1))
    mixed = jax.random.permutation(jax.random.fold_in(own, 3), amount)
    source_of, sink = mixed[0:amount // 2 * 2:2], mixed[1:amount // 2 * 2:2]
    room = jnp.minimum(tallies[source_of] - 1, reach - tallies[sink]) // 2
    room = jnp.where((source_of == order[0]) | (sink == order[0]) | (tallies[sink] == 0), 0, jnp.maximum(room, 0))
    moved = jax.random.randint(jax.random.fold_in(own, 4), (amount // 2,), 0, 1 << 20) % (room + 1)
    tallies = tallies.at[source_of].add(-moved).at[sink].add(moved)
    labels = jnp.searchsorted(jnp.cumsum(tallies), jnp.arange(rows * top), side="right").astype(jnp.int32)
    grid = labels.reshape(top, rows).T
    grid = grid[jax.random.permutation(jax.random.fold_in(own, 1), rows)]
    turn = jax.random.randint(jax.random.fold_in(own, 2), (rows, 1), 0, top)
    return jnp.take_along_axis(grid, (jnp.arange(top)[None, :] + turn) % top, axis=1)


def portions_of(amount, total, limit, slope, full):
    loads = [(1 << 20) // math.isqrt(rank ** slope) + 1 for rank in range(1, amount + 1)]
    largest = limit if full else min(limit, max(-(-total // amount), total * loads[0] // sum(loads)))
    least = 1 if total - largest >= amount - 1 else 0
    holding, spare = [largest] + [least] * (amount - 1), total - largest - least * (amount - 1)
    while spare > 0:
        free = [i for i in range(1, amount) if holding[i] < largest] or [i for i in range(1, amount) if holding[i] < limit]
        whole, budget = sum([loads[i] for i in free]), spare
        for i in free:
            extra = min(limit - holding[i], max(1, budget * loads[i] // whole), spare)
            holding[i] = holding[i] + extra
            spare = spare - extra
    return np.array(holding)


def normal_values(rng, shape, spread, reach, cuts=(), kind=jnp.bfloat16):
    entries = spread * jax.random.normal(rng, shape, jnp.float32)
    if cuts:
        entries = entries * block_scale(rng, shape, cuts, -0.22, 0.18)
    return jnp.clip(entries, -reach, reach).astype(kind)


def setup_inputs(seed: int = 0) -> dict:
    arg_keys = jax.random.split(jax.random.key(seed), 13)
    forward_sent = normal_values(arg_keys[0], (SECTIONS, TOKENS, D), 1.0, 6.0, ((0, 4), (1, 8)))
    embedded = normal_values(arg_keys[1], (TOKENS, D), 1.0, 6.0, ((0, 8),))
    forward_routes_keys = jax.random.split(jax.random.fold_in(arg_keys[2], 1), SECTIONS * TOKENS // TOK_DEV)
    forward_routes_turns = jax.random.permutation(jax.random.fold_in(arg_keys[2], 3), SECTIONS * TOKENS // TOK_DEV)
    forward_routes = jax.vmap(lambda own, number: assign_block(jax.random.fold_in(arg_keys[2], 2), own, number, TOK_DEV, EXPERTS, TOP, CAP, 2))(forward_routes_keys, forward_routes_turns).reshape((SECTIONS, TOKENS, TOP))
    backward_sent = normal_values(arg_keys[3], (SECTIONS, TOKENS, D), 1.0, 6.0, ((0, 4), (1, 8)))
    loss_gradient = normal_values(arg_keys[4], (TOKENS, D), 1.0, 6.0, ((0, 8),))
    saved_inputs = normal_values(arg_keys[5], (SECTIONS, TOKENS, D), 1.0, 6.0, ((0, 4), (1, 8)))
    backward_routes_keys = jax.random.split(jax.random.fold_in(arg_keys[6], 1), SECTIONS * TOKENS // TOK_DEV)
    backward_routes_turns = jax.random.permutation(jax.random.fold_in(arg_keys[6], 3), SECTIONS * TOKENS // TOK_DEV)
    backward_routes = jax.vmap(lambda own, number: assign_block(jax.random.fold_in(arg_keys[6], 2), own, number, TOK_DEV, EXPERTS, TOP, CAP, 2))(backward_routes_keys, backward_routes_turns).reshape((SECTIONS, TOKENS, TOP))
    pre_activation = normal_values(arg_keys[7], (SECTIONS, BLOCKS, EXPERTS, CAP, FF), 1.0, 6.0, ((0, 4), (2, 8)))
    norm_gain = jnp.clip(1.0 + 0.18 * jax.random.normal(arg_keys[8], (SECTIONS, D), jnp.float32), 0.099609375, 1.8984375).astype(jnp.bfloat16)
    router = normal_values(arg_keys[9], (SECTIONS, D, EXPERTS), D ** -0.5, 0.125, ((0, 4),))
    up_weight = normal_values(arg_keys[10], (EXPERTS, D, FF), D ** -0.5, 0.125, ((0, 8),))
    down_weight = normal_values(arg_keys[11], (EXPERTS, FF, D), FF ** -0.5, 0.1875, ((0, 8),))
    return {"forward_sent": forward_sent, "embedded": embedded, "forward_routes": forward_routes, "backward_sent": backward_sent, "loss_gradient": loss_gradient, "saved_inputs": saved_inputs, "backward_routes": backward_routes, "pre_activation": pre_activation, "norm_gain": norm_gain, "router": router, "up_weight": up_weight, "down_weight": down_weight}


EPS = 1e-06
HIGH = lax.Precision.HIGHEST

def slot_targets(block_routes):
    flattened = block_routes.reshape(-1).astype(jnp.int32)
    onehot = (flattened[:, None] == jnp.arange(EXPERTS, dtype=jnp.int32)[None, :]).astype(jnp.int32)
    before = jnp.cumsum(onehot, axis=0) - onehot
    ranked = lax.optimization_barrier(jnp.sum(before * onehot, axis=1)).astype(jnp.int32)
    return (flattened * CAP + ranked).reshape(block_routes.shape)

def routing(tokens, gain_row, router_mat, routes):
    widened = tokens.astype(jnp.float32)
    inv_rms = lax.rsqrt(lax.optimization_barrier(jnp.mean(widened * widened, axis=-1)) + EPS)
    normed = (widened * inv_rms[:, None] * gain_row.astype(jnp.float32)).astype(jnp.bfloat16)
    logits = jnp.dot(normed.astype(jnp.float32), router_mat.astype(jnp.float32), precision=HIGH)
    chosen = jnp.take_along_axis(logits, routes, axis=1)
    exponent = jnp.exp(chosen)
    shares = exponent / lax.optimization_barrier(jnp.sum(exponent, axis=1, keepdims=True))
    rounded = lax.optimization_barrier(shares.astype(jnp.bfloat16)).astype(jnp.float32)
    targets = jax.vmap(slot_targets)(routes.reshape(BLOCKS, TOK_DEV, TOP))
    slot_table = (targets[..., None] == jnp.arange(EXPERTS * CAP, dtype=jnp.int32)).astype(jnp.float32)
    placing = lax.optimization_barrier(jnp.sum(slot_table, axis=2))
    mixing = lax.optimization_barrier(jnp.sum(slot_table * rounded.reshape(BLOCKS, TOK_DEV, TOP)[..., None], axis=2))
    return (widened, inv_rms, normed, shares, slot_table, placing, mixing)

def dispatch(placing, data):
    blocked = data.reshape(BLOCKS, TOK_DEV, D).astype(jnp.float32)
    sent_rows = jnp.einsum('jts,jtd->jsd', placing, blocked, precision=HIGH).astype(jnp.bfloat16)
    return sent_rows.reshape(BLOCKS, EXPERTS, CAP, D).transpose(1, 0, 2, 3)

def forward_section(tokens, routes, gain_row, router_mat, up_weight, down_weight):
    widened, inv_rms, normed, shares, slot_table, placing, mixing = routing(tokens, gain_row, router_mat, routes)
    per_expert = dispatch(placing, normed)

    def expert(operands):
        block_rows, up_mat, down_mat = operands
        flattened = block_rows.reshape(-1, D).astype(jnp.float32)
        pre_act = jnp.dot(flattened, up_mat.astype(jnp.float32), precision=HIGH)
        hidden = lax.optimization_barrier(jax.nn.silu(pre_act).astype(jnp.bfloat16)).astype(jnp.float32)
        result = jnp.dot(hidden, down_mat.astype(jnp.float32), precision=HIGH).astype(jnp.bfloat16)
        return result.reshape(BLOCKS, CAP, D)
    outputs = lax.map(expert, (per_expert, up_weight, down_weight))
    outputs = outputs.transpose(1, 0, 2, 3).reshape(BLOCKS, EXPERTS * CAP, D).astype(jnp.float32)
    expert_sum = jnp.einsum('jts,jsd->jtd', mixing, outputs, precision=HIGH).reshape(TOKENS, D)
    return (widened + expert_sum).astype(jnp.bfloat16)

def backward_section(tokens, upstream, routes, saved_pre, gain_row, router_mat, up_weight, down_weight):
    widened, inv_rms, normed, shares, slot_table, placing, mixing = routing(tokens, gain_row, router_mat, routes)
    per_expert = dispatch(placing, upstream)
    saved_view = saved_pre.transpose(1, 0, 2, 3)

    def expert(operands):
        block_rows, saved_block, up_mat, down_mat = operands
        grad_rows = block_rows.reshape(-1, D).astype(jnp.float32)
        pre_act = saved_block.reshape(-1, FF).astype(jnp.float32)
        hidden_grad = jnp.dot(grad_rows, down_mat.astype(jnp.float32).T, precision=HIGH)
        hidden_rounded = lax.optimization_barrier(jax.nn.silu(pre_act).astype(jnp.bfloat16)).astype(jnp.float32)
        inner_sums = lax.optimization_barrier(jnp.sum(hidden_grad * hidden_rounded, axis=-1)).astype(jnp.bfloat16)
        sigmoid_pre = jax.nn.sigmoid(pre_act)
        pre_grad = hidden_grad * sigmoid_pre * (1.0 + pre_act * (1.0 - sigmoid_pre))
        pre_grad = lax.optimization_barrier(pre_grad.astype(jnp.bfloat16)).astype(jnp.float32)
        input_rows = jnp.dot(pre_grad, up_mat.astype(jnp.float32).T, precision=HIGH).astype(jnp.bfloat16)
        return (input_rows.reshape(BLOCKS, CAP, D), inner_sums.reshape(BLOCKS, CAP))
    input_rows, inner_sums = lax.map(expert, (per_expert, saved_view, up_weight, down_weight))
    input_rows = input_rows.transpose(1, 0, 2, 3).reshape(BLOCKS, EXPERTS * CAP, D).astype(jnp.float32)
    inner_sums = inner_sums.transpose(1, 0, 2).reshape(BLOCKS, EXPERTS * CAP).astype(jnp.float32)
    normed_grad = jnp.einsum('jts,jsd->jtd', mixing, input_rows, precision=HIGH).reshape(TOKENS, D)
    route_sums = jnp.einsum('jtks,js->jtk', slot_table, inner_sums, precision=HIGH).reshape(TOKENS, TOP)
    chosen_grad = shares * (route_sums - lax.optimization_barrier(jnp.sum(shares * route_sums, axis=1, keepdims=True)))
    route_hits = (routes[..., None] == jnp.arange(EXPERTS, dtype=jnp.int32)).astype(jnp.float32)
    logit_grad = jnp.einsum('tk,tke->te', chosen_grad, route_hits, precision=HIGH)
    normed_grad = normed_grad + jnp.dot(logit_grad, router_mat.astype(jnp.float32).T, precision=HIGH)
    gained_grad = normed_grad * gain_row.astype(jnp.float32)
    input_grad = inv_rms[:, None] * gained_grad - widened * (inv_rms ** 3)[:, None] * lax.optimization_barrier(jnp.mean(widened * gained_grad, axis=-1, keepdims=True))
    return (upstream.astype(jnp.float32) + input_grad).astype(jnp.bfloat16)

def reference(forward_sent, embedded, forward_routes, backward_sent, loss_gradient, saved_inputs, backward_routes, pre_activation, norm_gain, router, up_weight, down_weight):
    section_input = jnp.concatenate([embedded[None], forward_sent[:-1]], axis=0)
    upstream = jnp.concatenate([backward_sent[1:], loss_gradient[None]], axis=0)

    def run_forward(operands):
        tokens, routes, gain_row, router_mat = operands
        return forward_section(tokens, routes, gain_row, router_mat, up_weight, down_weight)

    def run_backward(operands):
        tokens, grads, routes, saved_pre, gain_row, router_mat = operands
        return backward_section(tokens, grads, routes, saved_pre, gain_row, router_mat, up_weight, down_weight)
    forward_output = lax.map(run_forward, (section_input, forward_routes, norm_gain, router))
    input_gradient = lax.map(run_backward, (saved_inputs, upstream, backward_routes, pre_activation, norm_gain, router))
    return (forward_output, input_gradient)
```

```python
import functools

import jax
import jax.numpy as jnp
import numpy as np
from jax import lax
from jax.experimental import pallas as pl
from jax.experimental.pallas import tpu as pltpu
from jax.sharding import PartitionSpec as P

EPS = 1e-06
BF16 = jnp.bfloat16
F32 = jnp.float32
LANES = 128
ROWS = 16
VMEM_LIMIT = 48 * 1024 * 1024
NT = (((1,), (1,)), ((), ()))
TN = (((0,), (0,)), ((), ()))


def dot(a, b, dims=(((1,), (0,)), ((), ()))):
    return lax.dot_general(a, b, dims, preferred_element_type=F32)


def call(kernel, out_shape, cost, **kwargs):
    flops, moved = cost
    return pl.pallas_call(
        kernel,
        out_shape=out_shape,
        compiler_params=pltpu.CompilerParams(vmem_limit_bytes=VMEM_LIMIT),
        cost_estimate=pl.CostEstimate(flops=flops, bytes_accessed=moved, transcendentals=0),
        **kwargs,
    )


def full_spec(shape):
    return pl.BlockSpec(shape, lambda *_: (0,) * len(shape))


SMEM = pl.BlockSpec(memory_space=pltpu.SMEM)
VMEM = pl.BlockSpec(memory_space=pltpu.VMEM)


def rotate(block, axis, distance):
    size = lax.axis_size(axis)
    return lax.ppermute(block, axis, [(i, (i + distance) % size) for i in range(size)])


def expert_hits(routes, experts):
    count, top = routes.shape
    lane = lax.broadcasted_iota(jnp.int32, (count, experts), 1)
    return [(routes[:, k : k + 1] == lane).astype(F32) for k in range(top)]


def slot_tables(routes, experts, capacity):
    count, top = routes.shape
    hits = expert_hits(routes, experts)
    earlier = lax.broadcasted_iota(jnp.int32, (count, count), 1) < lax.broadcasted_iota(
        jnp.int32, (count, count), 0
    )
    before = dot(earlier.astype(F32).astype(BF16), sum(hits).astype(BF16))
    lane = lax.broadcasted_iota(jnp.int32, (count, experts * capacity), 1)
    tables = []
    for k in range(top):
        ranked = jnp.sum((before + sum(hits[:k], jnp.zeros_like(before))) * hits[k], 1, keepdims=True)
        target = routes[:, k : k + 1] * capacity + ranked.astype(jnp.int32)
        tables.append((lane == target).astype(F32))
    return tables, hits


def normalise(tokens, gain):
    widened = tokens.astype(F32)
    inv_rms = lax.rsqrt(jnp.mean(widened * widened, axis=-1, keepdims=True) + EPS)
    return widened, inv_rms, (widened * inv_rms * gain.astype(F32)).astype(BF16)


def route_shares(normed, router, hits):
    logits = dot(normed, router)
    exponents = [jnp.exp(jnp.sum(logits * hit, axis=1, keepdims=True)) for hit in hits]
    total = sum(exponents)
    return [exponent / total for exponent in exponents]


def forward_send_kernel(capacity, experts, pick, sent, first, gain, routes, tokens, normed, send):
    chosen = jnp.where(pick[0] == 1, first[...], sent[...])
    tokens[...] = chosen
    _, _, rows = normalise(chosen, gain[...])
    normed[...] = rows
    tables, _ = slot_tables(routes[...], experts, capacity)
    send[...] = dot(sum(tables).astype(BF16), rows, TN).astype(BF16)


def backward_send_kernel(capacity, experts, pick, arrived, last, routes, upstream, send):
    chosen = jnp.where(pick[0] == 1, last[...], arrived[...])
    upstream[...] = chosen
    tables, _ = slot_tables(routes[...], experts, capacity)
    send[...] = dot(sum(tables).astype(BF16), chosen, TN).astype(BF16)


def mixing_kernel(
    capacity, experts, normed, router_f, routes_f, saved, gain, router_b, routes_b,
    mixing_f, mixing_b, tables_b, shares_b,
):
    tables, hits = slot_tables(routes_f[...], experts, capacity)
    shares = route_shares(normed[...], router_f[...], hits)
    mixing_f[...] = sum(t * s.astype(BF16).astype(F32) for t, s in zip(tables, shares)).astype(BF16)
    tables, hits = slot_tables(routes_b[...], experts, capacity)
    _, _, rows = normalise(saved[...], gain[...])
    shares = route_shares(rows, router_b[...], hits)
    mixing_b[...] = sum(t * s.astype(BF16).astype(F32) for t, s in zip(tables, shares)).astype(BF16)
    for k in range(len(tables)):
        tables_b[k] = tables[k].astype(BF16)
        shares_b[k] = jnp.broadcast_to(shares[k], shares_b.shape[1:])


def forward_expert_kernel(padded, steps, recv, order, back_order, up, down, out, rows, total, results):
    expert, step = pl.program_id(0), pl.program_id(1)

    @pl.when((expert == 0) & (step == 0))
    def _():
        rows[...] = dot(order[...], recv[...]).astype(BF16)

    own = pl.ds(pl.multiple_of(expert * padded, ROWS), padded)
    pre_act = dot(rows[own, :], up[0])
    hidden = (pre_act / (1.0 + jnp.exp(-pre_act))).astype(BF16)
    part = dot(hidden, down[0])

    @pl.when(step == 0)
    def _():
        total[...] = part

    @pl.when(step > 0)
    def _():
        total[...] += part

    @pl.when(step == steps - 1)
    def _():
        results[own, :] = total[...].astype(BF16)

    @pl.when((expert == pl.num_programs(0) - 1) & (step == steps - 1))
    def _():
        out[...] = dot(back_order[...], results[...]).astype(BF16)


def backward_expert_kernel(
    padded, steps, recv, order, back_order, saved_pre, up, down, out, rows, total, inner, results
):
    expert, step = pl.program_id(0), pl.program_id(1)
    width = rows.shape[1]

    @pl.when((expert == 0) & (step == 0))
    def _():
        rows[...] = dot(order[...], recv[...]).astype(BF16)

    own = pl.ds(pl.multiple_of(expert * padded, ROWS), padded)
    hidden_grad = dot(rows[own, :], down[0], NT)
    pre = saved_pre[0].astype(F32)
    gate = 1.0 / (1.0 + jnp.exp(-pre))
    hidden = (pre * gate).astype(BF16).astype(F32)
    inner_part = jnp.sum(hidden_grad * hidden, axis=1, keepdims=True)
    pre_grad = (hidden_grad * gate * (1.0 + pre * (1.0 - gate))).astype(BF16)
    part = dot(pre_grad, up[0], NT)

    @pl.when(step == 0)
    def _():
        total[...] = part
        inner[...] = jnp.broadcast_to(inner_part, inner.shape)

    @pl.when(step > 0)
    def _():
        total[...] += part
        inner[...] += jnp.broadcast_to(inner_part, inner.shape)

    @pl.when(step == steps - 1)
    def _():
        results[own, :width] = total[...].astype(BF16)
        results[own, width:] = inner[...].astype(BF16)

    @pl.when((expert == pl.num_programs(0) - 1) & (step == steps - 1))
    def _():
        out[...] = dot(back_order[...], results[...]).astype(BF16)


def forward_combine_kernel(tokens, mixing, back, out):
    out[...] = (tokens[...].astype(F32) + dot(mixing[...], back[...])).astype(BF16)


def backward_combine_kernel(
    experts, saved, upstream, gain, router, routes, mixing, tables, shares, back, out
):
    width = saved.shape[1]
    widened = saved[...].astype(F32)
    inv_rms = lax.rsqrt(jnp.mean(widened * widened, axis=-1, keepdims=True) + EPS)
    hits = expert_hits(routes[...], experts)
    top = len(hits)
    share = [shares[k][:, :1] for k in range(top)]
    inner = [dot(tables[k], back[:, width:])[:, :1] for k in range(top)]
    mean = sum(share[k] * inner[k] for k in range(top))
    logit_grad = sum(share[k] * (inner[k] - mean) * hits[k] for k in range(top))
    high = logit_grad.astype(BF16)
    rest = logit_grad - high.astype(F32)
    middle = rest.astype(BF16)
    low = (rest - middle.astype(F32)).astype(BF16)
    normed_grad = dot(mixing[...], back[:, :width])
    for piece in (high, middle, low):
        normed_grad += dot(piece, router[...], NT)
    gained = normed_grad * gain[...].astype(F32)
    projected = jnp.mean(widened * gained, axis=-1, keepdims=True)
    grad = inv_rms * gained - widened * (inv_rms * inv_rms * inv_rms * projected)
    out[...] = (upstream[...].astype(F32) + grad).astype(BF16)


def row_order(sources, local, capacity, padded):
    table = np.zeros((local * padded, sources * local * capacity), np.float32)
    for expert in range(local):
        for source in range(sources):
            for slot in range(capacity):
                table[
                    expert * padded + source * capacity + slot,
                    (source * local + expert) * capacity + slot,
                ] = 1.0
    return table


def on_device(
    forward_sent,
    embedded,
    forward_routes,
    backward_sent,
    loss_gradient,
    saved_inputs,
    backward_routes,
    pre_activation,
    norm_gain,
    router,
    up_weight,
    down_weight,
):
    section = lax.axis_index("section")
    last = lax.axis_size("section") - 1
    sources = lax.axis_size("expert")
    experts = router.shape[2]
    capacity = pre_activation.shape[3]
    local, width, hidden = up_weight.shape
    count = embedded.shape[0]
    top = forward_routes.shape[2]
    slots = experts * capacity
    rows = sources * capacity
    padded = -(-rows // ROWS) * ROWS
    steps = 2
    chunk = hidden // steps
    at_last = (section == last).astype(jnp.int32).reshape(1)
    shape = jax.ShapeDtypeStruct

    routes_f = rotate(forward_routes[0], "section", -1)
    gain_f = rotate(norm_gain, "section", -1)
    arrived = rotate(backward_sent[0], "section", -1)
    router_f = rotate(router[0], "section", -1)

    tokens, normed, send_f = call(
        functools.partial(forward_send_kernel, capacity, experts),
        (shape((count, width), BF16), shape((count, width), BF16), shape((slots, width), BF16)),
        (2 * slots * count * width, 2 * (4 * count + slots) * width),
        in_specs=[SMEM, VMEM, VMEM, VMEM, VMEM],
    )(at_last, forward_sent[0], embedded, gain_f, routes_f)
    got_f = lax.all_to_all(send_f, "expert", split_axis=0, concat_axis=0, tiled=True)

    upstream, send_b = call(
        functools.partial(backward_send_kernel, capacity, experts),
        (shape((count, width), BF16), shape((slots, width), BF16)),
        (2 * slots * count * width, 2 * (3 * count + slots) * width),
        in_specs=[SMEM, VMEM, VMEM, VMEM],
    )(at_last, arrived, loss_gradient, backward_routes[0])
    got_b = lax.all_to_all(send_b, "expert", split_axis=0, concat_axis=0, tiled=True)

    mixing_f, mixing_b, tables_b, shares_b = call(
        functools.partial(mixing_kernel, capacity, experts),
        (
            shape((count, slots), BF16),
            shape((count, slots), BF16),
            shape((top, count, slots), BF16),
            shape((top, count, LANES), F32),
        ),
        (4 * count * width * experts, 4 * (count + LANES) * width),
    )(
        normed, router_f, routes_f, saved_inputs[0], norm_gain, router[0], backward_routes[0]
    )
    saved_pre = jnp.transpose(pre_activation[0], (1, 0, 2, 3)).reshape(local, rows, hidden)
    saved_pre = jnp.pad(saved_pre, ((0, 0), (0, padded - rows), (0, 0)))

    order = row_order(sources, local, capacity, padded)
    order, back_order = jnp.asarray(order, BF16), jnp.asarray(order.T, BF16)
    weight_specs = [
        pl.BlockSpec((1, width, chunk), lambda e, f: (e, 0, f)),
        pl.BlockSpec((1, chunk, width), lambda e, f: (e, f, 0)),
    ]
    expert_cost = (
        4 * local * padded * width * hidden,
        4 * local * width * hidden,
    )
    result_f = call(
        functools.partial(forward_expert_kernel, padded, steps),
        shape((slots, width), BF16),
        expert_cost,
        grid=(local, steps),
        in_specs=[
            full_spec((slots, width)),
            full_spec(order.shape),
            full_spec(back_order.shape),
            *weight_specs,
        ],
        out_specs=full_spec((slots, width)),
        scratch_shapes=[
            pltpu.VMEM((local * padded, width), BF16),
            pltpu.VMEM((padded, width), F32),
            pltpu.VMEM((local * padded, width), BF16),
        ],
    )(got_f, order, back_order, up_weight, down_weight)
    back_f = lax.all_to_all(result_f, "expert", split_axis=0, concat_axis=0, tiled=True)

    result_b = call(
        functools.partial(backward_expert_kernel, padded, steps),
        shape((slots, width + LANES), BF16),
        expert_cost,
        grid=(local, steps),
        in_specs=[
            full_spec((slots, width)),
            full_spec(order.shape),
            full_spec(back_order.shape),
            pl.BlockSpec((1, padded, chunk), lambda e, f: (e, 0, f)),
            *weight_specs,
        ],
        out_specs=full_spec((slots, width + LANES)),
        scratch_shapes=[
            pltpu.VMEM((local * padded, width), BF16),
            pltpu.VMEM((padded, width), F32),
            pltpu.VMEM((padded, LANES), F32),
            pltpu.VMEM((local * padded, width + LANES), BF16),
        ],
    )(got_b, order, back_order, saved_pre, up_weight, down_weight)
    back_b = lax.all_to_all(result_b, "expert", split_axis=0, concat_axis=0, tiled=True)

    output = call(
        forward_combine_kernel,
        shape((count, width), BF16),
        (2 * slots * count * width, 2 * (2 * count + slots) * width),
    )(tokens, mixing_f, back_f)
    forward_output = rotate(output, "section", 1)

    input_gradient = call(
        functools.partial(backward_combine_kernel, experts),
        shape((count, width), BF16),
        (2 * slots * count * width, 2 * (3 * count + slots) * width),
    )(
        saved_inputs[0], upstream, norm_gain, router[0], backward_routes[0],
        mixing_b, tables_b, shares_b, back_b,
    )
    return (forward_output[None], input_gradient[None])


def solution(mesh):
    return jax.shard_map(
        on_device,
        mesh=mesh,
        in_specs=(
            P("section", "expert", None),
            P("expert", None),
            P("section", "expert", None),
            P("section", "expert", None),
            P("expert", None),
            P("section", "expert", None),
            P("section", "expert", None),
            P("section", None, "expert", None, None),
            P("section", None),
            P("section", None, None),
            P("expert", None, None),
            P("expert", None, None),
        ),
        out_specs=(P("section", "expert", None), P("section", "expert", None)),
        check_vma=False,
    )
```

```python
import functools

import jax
import jax.numpy as jnp
import numpy as np
from jax import lax
from jax.experimental import pallas as pl
from jax.experimental.pallas import tpu as pltpu
from jax.sharding import PartitionSpec as P

EPS = 1e-06
BF16 = jnp.bfloat16
F32 = jnp.float32
LANES = 128
ROWS = 16
VMEM_LIMIT = 48 * 1024 * 1024
NT = (((1,), (1,)), ((), ()))
TN = (((0,), (0,)), ((), ()))


def dot(a, b, dims=(((1,), (0,)), ((), ()))):
    return lax.dot_general(a, b, dims, preferred_element_type=F32)


def call(kernel, out_shape, cost, **kwargs):
    flops, moved = cost
    return pl.pallas_call(
        kernel,
        out_shape=out_shape,
        compiler_params=pltpu.CompilerParams(vmem_limit_bytes=VMEM_LIMIT),
        cost_estimate=pl.CostEstimate(flops=flops, bytes_accessed=moved, transcendentals=0),
        **kwargs,
    )


def full_spec(shape):
    return pl.BlockSpec(shape, lambda *_: (0,) * len(shape))


SMEM = pl.BlockSpec(memory_space=pltpu.SMEM)
VMEM = pl.BlockSpec(memory_space=pltpu.VMEM)


def rotate(block, axis, distance):
    size = lax.axis_size(axis)
    return lax.ppermute(block, axis, [(i, (i + distance) % size) for i in range(size)])


def expert_hits(routes, experts):
    count, top = routes.shape
    lane = lax.broadcasted_iota(jnp.int32, (count, experts), 1)
    return [(routes[:, k : k + 1] == lane).astype(F32) for k in range(top)]


def slot_targets(routes, experts, capacity):
    count, top = routes.shape
    hits = expert_hits(routes, experts)
    earlier = lax.broadcasted_iota(jnp.int32, (count, count), 1) < lax.broadcasted_iota(
        jnp.int32, (count, count), 0
    )
    before = dot(earlier.astype(F32).astype(BF16), sum(hits).astype(BF16))
    targets = []
    for k in range(top):
        ranked = jnp.sum((before + sum(hits[:k], jnp.zeros_like(before))) * hits[k], 1, keepdims=True)
        targets.append(routes[:, k : k + 1] * capacity + ranked.astype(jnp.int32))
    return targets, hits


def slot_tables(routes, experts, capacity):
    targets, hits = slot_targets(routes, experts, capacity)
    lane = lax.broadcasted_iota(jnp.int32, (routes.shape[0], experts * capacity), 1)
    return [(lane == target).astype(F32) for target in targets], hits


def normalise(tokens, gain):
    widened = tokens.astype(F32)
    inv_rms = lax.rsqrt(jnp.mean(widened * widened, axis=-1, keepdims=True) + EPS)
    return widened, inv_rms, (widened * inv_rms * gain.astype(F32)).astype(BF16)


def route_shares(normed, router, hits):
    logits = dot(normed, router, NT)
    exponents = [jnp.exp(jnp.sum(logits * hit, axis=1, keepdims=True)) for hit in hits]
    total = sum(exponents)
    return [exponent / total for exponent in exponents]


def slot_keys_kernel(capacity, experts, block, routes_f, routes_b, keys_f, keys_b):
    slots = experts * capacity
    for routes, keys in ((routes_f, keys_f), (routes_b, keys_b)):
        lane = lax.broadcasted_iota(jnp.int32, keys.shape, 1)
        out = jnp.zeros(keys.shape, jnp.int32)
        for k, target in enumerate(slot_targets(routes[...], experts, capacity)[0]):
            out += jnp.where(lane == k, target + block[0] * slots, 0)
        keys[...] = out


def mixing_kernel(
    capacity, experts, tokens, gain_f, router_f, routes_f, saved, gain_b, router_b, routes_b,
    mixing_f, mixing_b, tables_b, shares_b,
):
    tables, hits = slot_tables(routes_f[...], experts, capacity)
    _, _, rows = normalise(tokens[...], gain_f[...])
    shares = route_shares(rows, router_f[...], hits)
    mixing_f[...] = sum(t * s.astype(BF16).astype(F32) for t, s in zip(tables, shares)).astype(BF16)
    tables, hits = slot_tables(routes_b[...], experts, capacity)
    _, _, rows = normalise(saved[...], gain_b[...])
    shares = route_shares(rows, router_b[...], hits)
    mixing_b[...] = sum(t * s.astype(BF16).astype(F32) for t, s in zip(tables, shares)).astype(BF16)
    for k in range(len(tables)):
        tables_b[k] = tables[k].astype(BF16)
        shares_b[k] = jnp.broadcast_to(shares[k], shares_b.shape[1:])


def send_rows_kernel(capacity, experts, routes, tokens, send):
    tables, _ = slot_tables(routes[...], experts, capacity)
    send[...] = dot(sum(tables).astype(BF16), tokens[...], TN).astype(BF16)


def picked_rows(offset, row_keys, keys, tokens):
    wanted = row_keys[...] + offset
    held = sum((keys[:, k : k + 1] == wanted).astype(F32) for k in range(keys.shape[1]))
    return dot(held.astype(BF16), tokens[...], TN)


def forward_expert_kernel(
    padded, steps, offset, row_keys, keys, tokens, gain, back_order, up, down,
    out, rows, total, results,
):
    expert, step = pl.program_id(0), pl.program_id(1)

    @pl.when((expert == 0) & (step == 0))
    def _():
        picked = picked_rows(offset[0], row_keys, keys, tokens)
        rows[...] = normalise(picked, gain[...])[2]

    own = pl.ds(pl.multiple_of(expert * padded, ROWS), padded)
    pre_act = dot(rows[own, :], up[0])
    hidden = (pre_act / (1.0 + jnp.exp(-pre_act))).astype(BF16)
    part = dot(hidden, down[0])

    @pl.when(step == 0)
    def _():
        total[...] = part

    @pl.when(step > 0)
    def _():
        total[...] += part

    @pl.when(step == steps - 1)
    def _():
        results[own, :] = total[...].astype(BF16)

    @pl.when((expert == pl.num_programs(0) - 1) & (step == steps - 1))
    def _():
        out[...] = dot(back_order[...], results[...]).astype(BF16)


def backward_expert_kernel(
    padded, steps, offset, row_keys, keys, upstream, back_order, saved_pre, up, down,
    out, rows, total, inner, results,
):
    expert, step = pl.program_id(0), pl.program_id(1)
    width = rows.shape[1]

    @pl.when((expert == 0) & (step == 0))
    def _():
        picked = picked_rows(offset[0], row_keys, keys, upstream)
        rows[...] = picked.astype(BF16)

    own = pl.ds(pl.multiple_of(expert * padded, ROWS), padded)
    hidden_grad = jnp.transpose(dot(down[0], rows[own, :], NT))
    pre = saved_pre[0].astype(F32)
    gate = 1.0 / (1.0 + jnp.exp(-pre))
    hidden = (pre * gate).astype(BF16).astype(F32)
    inner_part = jnp.sum(hidden_grad * hidden, axis=1, keepdims=True)
    pre_grad = (hidden_grad * gate * (1.0 + pre * (1.0 - gate))).astype(BF16)
    part = dot(up[0], pre_grad, NT)

    @pl.when(step == 0)
    def _():
        total[...] = part
        inner[...] = jnp.broadcast_to(inner_part, inner.shape)

    @pl.when(step > 0)
    def _():
        total[...] += part
        inner[...] += jnp.broadcast_to(inner_part, inner.shape)

    @pl.when(step == steps - 1)
    def _():
        results[own, :width] = jnp.transpose(total[...]).astype(BF16)
        results[own, width:] = inner[...].astype(BF16)

    @pl.when((expert == pl.num_programs(0) - 1) & (step == steps - 1))
    def _():
        out[...] = dot(back_order[...], results[...]).astype(BF16)


def forward_combine_kernel(tokens, mixing, back, out):
    out[...] = (tokens[...].astype(F32) + dot(mixing[...], back[...])).astype(BF16)


def backward_combine_kernel(
    experts, saved, upstream, gain, router, routes, mixing, tables, shares, back, out
):
    width = saved.shape[1]
    widened = saved[...].astype(F32)
    inv_rms = lax.rsqrt(jnp.mean(widened * widened, axis=-1, keepdims=True) + EPS)
    hits = expert_hits(routes[...], experts)
    top = len(hits)
    share = [shares[k][:, :1] for k in range(top)]
    inner = [dot(tables[k], back[:, width:])[:, :1] for k in range(top)]
    mean = sum(share[k] * inner[k] for k in range(top))
    logit_grad = sum(share[k] * (inner[k] - mean) * hits[k] for k in range(top))
    high = logit_grad.astype(BF16)
    rest = logit_grad - high.astype(F32)
    middle = rest.astype(BF16)
    low = (rest - middle.astype(F32)).astype(BF16)
    normed_grad = dot(mixing[...], back[:, :width])
    for piece in (high, middle, low):
        normed_grad += dot(piece, router[...])
    gained = normed_grad * gain[...].astype(F32)
    projected = jnp.mean(widened * gained, axis=-1, keepdims=True)
    grad = inv_rms * gained - widened * (inv_rms * inv_rms * inv_rms * projected)
    out[...] = (upstream[...].astype(F32) + grad).astype(BF16)


def row_order(sources, local, capacity, padded, slots):
    keys = np.full((1, local * padded), -sources * slots, np.int32)
    back = np.zeros((sources * local * capacity, local * padded), np.float32)
    for expert in range(local):
        for source in range(sources):
            for slot in range(capacity):
                row = expert * padded + source * capacity + slot
                keys[0, row] = source * slots + expert * capacity + slot
                back[(source * local + expert) * capacity + slot, row] = 1.0
    return keys, back


def on_device(
    forward_sent,
    embedded,
    forward_routes,
    backward_sent,
    loss_gradient,
    saved_inputs,
    backward_routes,
    pre_activation,
    norm_gain,
    router,
    up_weight,
    down_weight,
):
    section = lax.axis_index("section")
    last = lax.axis_size("section") - 1
    sources = lax.axis_size("expert")
    experts = router.shape[2]
    capacity = pre_activation.shape[3]
    local, width, hidden = up_weight.shape
    count = embedded.shape[0]
    top = forward_routes.shape[2]
    slots = experts * capacity
    rows = sources * capacity
    padded = -(-rows // ROWS) * ROWS
    steps = 2
    chunk = hidden // steps
    at_last = (section == last).astype(jnp.int32).reshape(1)
    shape = jax.ShapeDtypeStruct

    router_t = router[0].T
    arrived = rotate(backward_sent[0], "section", -1)
    tokens = jnp.where(section == last, embedded, forward_sent[0])
    routes_f = rotate(forward_routes[0], "section", -1)
    gain_f = rotate(norm_gain, "section", -1)
    router_f = rotate(router_t, "section", -1)
    upstream = jnp.where(section == last, loss_gradient, arrived)
    here = lax.axis_index("expert")
    if sources * count <= 4 * slots:
        got_f = lax.all_gather(tokens, "expert", axis=0, tiled=True)
        keys = call(
            functools.partial(slot_keys_kernel, capacity, experts),
            (shape((count, top), jnp.int32),) * 2,
            (4 * count * count * experts, 4 * count * LANES),
            in_specs=[SMEM, VMEM, VMEM],
        )(here.reshape(1), forward_routes[0], backward_routes[0])
        keys_f, keys_b = lax.all_gather(keys, "expert", axis=0, tiled=True)
        keys_f = rotate(keys_f, "section", -1)
        got_b = lax.all_gather(upstream, "expert", axis=0, tiled=True)
    else:
        got_f, got_b = [
            lax.all_to_all(
                call(
                    functools.partial(send_rows_kernel, capacity, experts),
                    shape((slots, width), BF16),
                    (2 * slots * count * width, 2 * (count + slots) * width),
                )(routes, data),
                "expert",
                split_axis=0,
                concat_axis=0,
                tiled=True,
            )
            for routes, data in ((routes_f, tokens), (backward_routes[0], upstream))
        ]
        place = jnp.arange(slots, dtype=jnp.int32)[:, None]
        share = local * capacity
        keys_f = keys_b = place // share * slots + here * share + place % share

    mixing_f, mixing_b, tables_b, shares_b = call(
        functools.partial(mixing_kernel, capacity, experts),
        (
            shape((count, slots), BF16),
            shape((count, slots), BF16),
            shape((top, count, slots), BF16),
            shape((top, count, LANES), F32),
        ),
        (4 * count * width * experts, 4 * (count + LANES) * width),
    )(
        tokens, gain_f, router_f, routes_f, saved_inputs[0], norm_gain, router_t, backward_routes[0]
    )
    saved_pre = jnp.transpose(pre_activation[0], (1, 0, 2, 3)).reshape(local, rows, hidden)
    saved_pre = jnp.pad(saved_pre, ((0, 0), (0, padded - rows), (0, 0)))

    row_keys, back_order = row_order(sources, local, capacity, padded, slots)
    back_order = jnp.asarray(back_order, BF16)
    offset = (here * (local * capacity)).reshape(1)
    weight_specs = [
        pl.BlockSpec((1, width, chunk), lambda e, f: (e, 0, f)),
        pl.BlockSpec((1, chunk, width), lambda e, f: (e, f, 0)),
    ]
    expert_cost = (
        4 * local * padded * width * hidden,
        4 * local * width * hidden,
    )
    result_f = call(
        functools.partial(forward_expert_kernel, padded, steps),
        shape((slots, width), BF16),
        expert_cost,
        grid=(local, steps),
        in_specs=[
            SMEM,
            full_spec(row_keys.shape),
            full_spec(keys_f.shape),
            full_spec(got_f.shape),
            full_spec(gain_f.shape),
            full_spec(back_order.shape),
            *weight_specs,
        ],
        out_specs=full_spec((slots, width)),
        scratch_shapes=[
            pltpu.VMEM((local * padded, width), BF16),
            pltpu.VMEM((padded, width), F32),
            pltpu.VMEM((local * padded, width), BF16),
        ],
    )(offset, row_keys, keys_f, got_f, gain_f, back_order, up_weight, down_weight)
    back_f = lax.all_to_all(result_f, "expert", split_axis=0, concat_axis=0, tiled=True)

    result_b = call(
        functools.partial(backward_expert_kernel, padded, steps),
        shape((slots, width + LANES), BF16),
        expert_cost,
        grid=(local, steps),
        in_specs=[
            SMEM,
            full_spec(row_keys.shape),
            full_spec(keys_b.shape),
            full_spec(got_b.shape),
            full_spec(back_order.shape),
            pl.BlockSpec((1, padded, chunk), lambda e, f: (e, 0, f)),
            *weight_specs,
        ],
        out_specs=full_spec((slots, width + LANES)),
        scratch_shapes=[
            pltpu.VMEM((local * padded, width), BF16),
            pltpu.VMEM((width, padded), F32),
            pltpu.VMEM((padded, LANES), F32),
            pltpu.VMEM((local * padded, width + LANES), BF16),
        ],
    )(offset, row_keys, keys_b, got_b, back_order, saved_pre, up_weight, down_weight)
    back_b = lax.all_to_all(result_b, "expert", split_axis=0, concat_axis=0, tiled=True)

    output = call(
        forward_combine_kernel,
        shape((count, width), BF16),
        (2 * slots * count * width, 2 * (2 * count + slots) * width),
    )(tokens, mixing_f, back_f)
    forward_output = rotate(output, "section", 1)

    input_gradient = call(
        functools.partial(backward_combine_kernel, experts),
        shape((count, width), BF16),
        (2 * slots * count * width, 2 * (3 * count + slots) * width),
    )(
        saved_inputs[0], upstream, norm_gain, router_t, backward_routes[0],
        mixing_b, tables_b, shares_b, back_b,
    )
    return (forward_output[None], input_gradient[None])


def solution(mesh):
    return jax.shard_map(
        on_device,
        mesh=mesh,
        in_specs=(
            P("section", "expert", None),
            P("expert", None),
            P("section", "expert", None),
            P("section", "expert", None),
            P("expert", None),
            P("section", "expert", None),
            P("section", "expert", None),
            P("section", None, "expert", None, None),
            P("section", None),
            P("section", None, None),
            P("expert", None, None),
            P("expert", None, None),
        ),
        out_specs=(P("section", "expert", None), P("section", "expert", None)),
        check_vma=False,
    )
```

```python
import functools

import jax
import jax.numpy as jnp
import numpy as np
from jax import lax
from jax.experimental import pallas as pl
from jax.experimental.pallas import tpu as pltpu
from jax.sharding import PartitionSpec as P

EPS = 1e-06
BF16 = jnp.bfloat16
F32 = jnp.float32
LANES = 128
ROWS = 16
VMEM_LIMIT = 48 * 1024 * 1024
NT = (((1,), (1,)), ((), ()))
TN = (((0,), (0,)), ((), ()))


def dot(a, b, dims=(((1,), (0,)), ((), ()))):
    return lax.dot_general(a, b, dims, preferred_element_type=F32)


def call(kernel, out_shape, cost, **kwargs):
    flops, moved = cost
    return pl.pallas_call(
        kernel,
        out_shape=out_shape,
        compiler_params=pltpu.CompilerParams(vmem_limit_bytes=VMEM_LIMIT),
        cost_estimate=pl.CostEstimate(flops=flops, bytes_accessed=moved, transcendentals=0),
        **kwargs,
    )


def full_spec(shape):
    return pl.BlockSpec(shape, lambda *_: (0,) * len(shape))


SMEM = pl.BlockSpec(memory_space=pltpu.SMEM)
VMEM = pl.BlockSpec(memory_space=pltpu.VMEM)


def from_behind(block, axis, distance):
    devices = range(lax.axis_size(axis))
    route = [(i - distance, i) for i in devices if i - distance in devices]
    return lax.ppermute(block, axis, route)


def exchange(rows):
    return lax.all_to_all(rows, "expert", split_axis=0, concat_axis=0, tiled=True)


def expert_hits(routes, experts):
    count, top = routes.shape
    lane = lax.broadcasted_iota(jnp.int32, (count, experts), 1)
    return [(routes[:, k : k + 1] == lane).astype(F32) for k in range(top)]


def slot_targets(routes, experts, capacity):
    count, top = routes.shape
    hits = expert_hits(routes, experts)
    earlier = lax.broadcasted_iota(jnp.int32, (count, count), 1) < lax.broadcasted_iota(
        jnp.int32, (count, count), 0
    )
    before = dot(earlier.astype(F32).astype(BF16), sum(hits).astype(BF16))
    targets = []
    for k in range(top):
        ranked = jnp.sum((before + sum(hits[:k], jnp.zeros_like(before))) * hits[k], 1, keepdims=True)
        targets.append(routes[:, k : k + 1] * capacity + ranked.astype(jnp.int32))
    return targets, hits


def tables_of(targets, row_keys):
    return [(row_keys == target).astype(F32) for target in targets]


def normalise(tokens, gain):
    widened = tokens.astype(F32)
    inv_rms = lax.rsqrt(jnp.mean(widened * widened, axis=-1, keepdims=True) + EPS)
    return widened, inv_rms, (widened * inv_rms * gain.astype(F32)).astype(BF16)


def route_shares(normed, router, hits):
    logits = dot(normed, router, NT)
    exponents = [jnp.exp(jnp.sum(logits * hit, axis=1, keepdims=True)) for hit in hits]
    total = sum(exponents)
    return [exponent / total for exponent in exponents]


def first_send_kernel(
    capacity, experts, place, arrived_f, arrived_b, embedded, loss, gain, routes_f, routes_b,
    row_keys, tokens, upstream, data, send,
):
    count = embedded.shape[0]
    slots = experts * capacity
    chosen = jnp.where(place[0] == 0, embedded[...], arrived_f[...])
    tokens[...] = chosen
    data[:count, :] = normalise(chosen, gain[...])[2]
    chosen = jnp.where(place[0] == place[1], loss[...], arrived_b[...])
    upstream[...] = chosen
    data[count:, :] = chosen
    targets_f, _ = slot_targets(routes_f[...], experts, capacity)
    targets_b, _ = slot_targets(routes_b[...], experts, capacity)
    keys = row_keys[0:1, :]
    table_f = sum(tables_of(targets_f, keys))
    table_b = sum(tables_of([t + slots for t in targets_b], keys))
    table = jnp.concatenate([table_f, table_b], axis=0).astype(BF16)
    send[...] = dot(table, data[...], TN).astype(BF16)


def mixing_kernel(
    capacity, experts, data, saved, gain, router, routes_f, routes_b, row_keys,
    mixing_f, mixing_b, tables_b, shares_b, *sends,
):
    count = saved.shape[0]
    slots = experts * capacity
    targets_f, hits = slot_targets(routes_f[...], experts, capacity)
    shares_f = route_shares(data[:count, :], router[...], hits)
    targets_b, hits = slot_targets(routes_b[...], experts, capacity)
    targets_b = [t + slots for t in targets_b]
    _, _, rows = normalise(saved[...], gain[...])
    own_shares = route_shares(rows, router[...], hits)
    for k, share in enumerate(own_shares):
        shares_b[k] = jnp.broadcast_to(share, shares_b.shape[1:])
    for part in range(mixing_f.shape[0]):
        keys = row_keys[part : part + 1, :]
        found_f, found_b = tables_of(targets_f, keys), tables_of(targets_b, keys)
        mixing_f[part] = sum(
            t * s.astype(BF16).astype(F32) for t, s in zip(found_f, shares_f)
        ).astype(BF16)
        mixing_b[part] = sum(
            t * s.astype(BF16).astype(F32) for t, s in zip(found_b, own_shares)
        ).astype(BF16)
        for k, table in enumerate(found_b):
            tables_b[part, k] = table.astype(BF16)
        if part > 0:
            table = jnp.concatenate([sum(found_f), sum(found_b)], axis=0).astype(BF16)
            sends[part - 1][...] = dot(table, data[...], TN).astype(BF16)


def expert_kernel(
    padded, steps, recv, order, back_order, saved_pre, up, down,
    out, rows, total_f, total_b, inner, results,
):
    expert, step = pl.program_id(0), pl.program_id(1)
    held = pl.num_programs(0)
    width = rows.shape[1]

    @pl.when((expert == 0) & (step == 0))
    def _():
        rows[...] = dot(order[...], recv[...]).astype(BF16)
        results[:, width:] = jnp.zeros((results.shape[0], results.shape[1] - width), BF16)

    own_f = pl.ds(pl.multiple_of(expert * padded, ROWS), padded)
    own_b = pl.ds(pl.multiple_of((held + expert) * padded, ROWS), padded)
    pre_act = dot(rows[own_f, :], up[0])
    hidden_grad = dot(rows[own_b, :], down[0], NT)
    hidden = (pre_act / (1.0 + jnp.exp(-pre_act))).astype(BF16)
    pre = saved_pre[0].astype(F32)
    gate = 1.0 / (1.0 + jnp.exp(-pre))
    inner_part = jnp.sum(hidden_grad * (pre * gate).astype(BF16).astype(F32), axis=1, keepdims=True)
    pre_grad = (hidden_grad * gate * (1.0 + pre * (1.0 - gate))).astype(BF16)
    part_f = dot(hidden, down[0])
    part_b = dot(pre_grad, up[0], NT)

    @pl.when(step == 0)
    def _():
        total_f[...] = part_f
        total_b[...] = part_b
        inner[...] = jnp.broadcast_to(inner_part, inner.shape)

    @pl.when(step > 0)
    def _():
        total_f[...] += part_f
        total_b[...] += part_b
        inner[...] += jnp.broadcast_to(inner_part, inner.shape)

    @pl.when(step == steps - 1)
    def _():
        results[own_f, :width] = total_f[...].astype(BF16)
        results[own_b, :width] = total_b[...].astype(BF16)
        results[own_b, width:] = inner[...].astype(BF16)

    @pl.when((expert == held - 1) & (step == steps - 1))
    def _():
        out[...] = dot(back_order[...], results[...]).astype(BF16)


def combine_kernel(
    experts, tokens, saved, upstream, gain, router, routes, mixing_f, mixing_b, tables, shares, *refs
):
    *backs, output, gradient = refs
    width = tokens.shape[1]
    parts = range(len(backs))
    widened = saved[...].astype(F32)
    inv_rms = lax.rsqrt(jnp.mean(widened * widened, axis=-1, keepdims=True) + EPS)
    hits = expert_hits(routes[...], experts)
    top = len(hits)
    share = [shares[k][:, :1] for k in range(top)]
    inner = [sum(dot(tables[p, k], backs[p][:, width:]) for p in parts)[:, :1] for k in range(top)]
    mean = sum(share[k] * inner[k] for k in range(top))
    logit_grad = sum(share[k] * (inner[k] - mean) * hits[k] for k in range(top))
    high = logit_grad.astype(BF16)
    rest = logit_grad - high.astype(F32)
    middle = rest.astype(BF16)
    low = (rest - middle.astype(F32)).astype(BF16)
    output[0] = (
        tokens[...].astype(F32) + sum(dot(mixing_f[p], backs[p][:, :width]) for p in parts)
    ).astype(BF16)
    normed_grad = sum(dot(mixing_b[p], backs[p][:, :width]) for p in parts)
    for piece in (high, middle, low):
        normed_grad += dot(piece, router[...])
    gained = normed_grad * gain[...].astype(F32)
    projected = jnp.mean(widened * gained, axis=-1, keepdims=True)
    grad = inv_rms * gained - widened * (inv_rms * inv_rms * inv_rms * projected)
    gradient[0] = (upstream[...].astype(F32) + grad).astype(BF16)


def exchange_order(parts, sources, local, capacity, padded):
    held = local // parts
    slots = sources * local * capacity
    keys = np.zeros((parts, 2 * sources * held * capacity), np.int32)
    table = np.zeros((2 * held * padded, keys.shape[1]), np.float32)
    for source in range(sources):
        for batch in range(2):
            for expert in range(held):
                for slot in range(capacity):
                    row = ((source * 2 + batch) * held + expert) * capacity + slot
                    for part in range(parts):
                        full = (source * local + part * held + expert) * capacity + slot
                        keys[part, row] = batch * slots + full
                    table[(batch * held + expert) * padded + source * capacity + slot, row] = 1.0
    return keys, table


def on_device(
    forward_sent,
    embedded,
    forward_routes,
    backward_sent,
    loss_gradient,
    saved_inputs,
    backward_routes,
    pre_activation,
    norm_gain,
    router,
    up_weight,
    down_weight,
):
    section = lax.axis_index("section")
    last = lax.axis_size("section") - 1
    sources = lax.axis_size("expert")
    experts = router.shape[2]
    capacity = pre_activation.shape[3]
    local, width, hidden = up_weight.shape
    count = embedded.shape[0]
    top = forward_routes.shape[2]
    slots = experts * capacity
    rows = sources * capacity
    padded = -(-rows // ROWS) * ROWS
    steps = 2
    chunk = hidden // steps
    shape = jax.ShapeDtypeStruct
    parts = 2 if local % 2 == 0 else 1
    held = local // parts
    moved = 2 * slots // parts
    row_keys, order = exchange_order(parts, sources, local, capacity, padded)
    order, back_order = jnp.asarray(order, BF16), jnp.asarray(order.T, BF16)

    router_t = router[0].T
    arrived_f = from_behind(forward_sent[0], "section", 1)
    arrived_b = from_behind(backward_sent[0], "section", -1)
    tokens, upstream, data, send = call(
        functools.partial(first_send_kernel, capacity, experts),
        (
            shape((count, width), BF16),
            shape((count, width), BF16),
            shape((2 * count, width), BF16),
            shape((moved, width), BF16),
        ),
        (4 * moved * count * width, 2 * (8 * count + moved) * width),
        in_specs=[SMEM] + [VMEM] * 8,
    )(
        jnp.stack([section, jnp.full_like(section, last)]).astype(jnp.int32),
        arrived_f, arrived_b, embedded, loss_gradient, norm_gain,
        forward_routes[0], backward_routes[0], row_keys,
    )
    mixing_f, mixing_b, tables_b, shares_b, *sends = call(
        functools.partial(mixing_kernel, capacity, experts),
        (
            shape((parts, count, moved), BF16),
            shape((parts, count, moved), BF16),
            shape((parts, top, count, moved), BF16),
            shape((top, count, LANES), F32),
        )
        + (shape((moved, width), BF16),) * (parts - 1),
        (4 * moved * count * width, 2 * (4 * count + moved) * width),
    )(
        data, saved_inputs[0], norm_gain, router_t, forward_routes[0], backward_routes[0], row_keys
    )
    saved_pre = jnp.transpose(pre_activation[0], (1, 0, 2, 3)).reshape(local, rows, hidden)
    saved_pre = jnp.pad(saved_pre, ((0, 0), (0, padded - rows), (0, 0)))

    received = [exchange(data) for data in (send, *sends)]
    backs = []
    for part, got in enumerate(received):
        result = call(
            functools.partial(expert_kernel, padded, steps),
            shape((moved, width + LANES), BF16),
            (8 * held * padded * width * hidden, 4 * held * width * hidden),
            grid=(held, steps),
            in_specs=[
                full_spec((moved, width)),
                full_spec(order.shape),
                full_spec(back_order.shape),
                pl.BlockSpec((1, padded, chunk), lambda e, f, p=part: (p * held + e, 0, f)),
                pl.BlockSpec((1, width, chunk), lambda e, f, p=part: (p * held + e, 0, f)),
                pl.BlockSpec((1, chunk, width), lambda e, f, p=part: (p * held + e, f, 0)),
            ],
            out_specs=full_spec((moved, width + LANES)),
            scratch_shapes=[
                pltpu.VMEM((2 * held * padded, width), BF16),
                pltpu.VMEM((padded, width), F32),
                pltpu.VMEM((padded, width), F32),
                pltpu.VMEM((padded, LANES), F32),
                pltpu.VMEM((2 * held * padded, width + LANES), BF16),
            ],
        )(got, order, back_order, saved_pre, up_weight, down_weight)
        backs.append(exchange(result))
    return tuple(
        call(
            functools.partial(combine_kernel, experts),
            (shape((1, count, width), BF16),) * 2,
            (8 * moved * count * width, 2 * (5 * count + 2 * moved) * width),
        )(
            tokens, saved_inputs[0], upstream, norm_gain, router_t, backward_routes[0],
            mixing_f, mixing_b, tables_b, shares_b, *backs,
        )
    )


def solution(mesh):
    return jax.shard_map(
        on_device,
        mesh=mesh,
        in_specs=(
            P("section", "expert", None),
            P("expert", None),
            P("section", "expert", None),
            P("section", "expert", None),
            P("expert", None),
            P("section", "expert", None),
            P("section", "expert", None),
            P("section", None, "expert", None, None),
            P("section", None),
            P("section", None, None),
            P("expert", None, None),
            P("expert", None, None),
        ),
        out_specs=(P("section", "expert", None), P("section", "expert", None)),
        check_vma=False,
    )
```

```python
import functools

import jax
import jax.numpy as jnp
import numpy as np
from jax import lax
from jax.experimental import pallas as pl
from jax.experimental.pallas import tpu as pltpu
from jax.sharding import PartitionSpec as P

EPS = 1e-06
BF16 = jnp.bfloat16
F32 = jnp.float32
LANES = 128
ROWS = 16
VMEM_LIMIT = 60 * 1024 * 1024
NT = (((1,), (1,)), ((), ()))
TN = (((0,), (0,)), ((), ()))


def dot(a, b, dims=(((1,), (0,)), ((), ()))):
    return lax.dot_general(a, b, dims, preferred_element_type=F32)


def call(kernel, out_shape, cost, **kwargs):
    flops, moved = cost
    return pl.pallas_call(
        kernel,
        out_shape=out_shape,
        compiler_params=pltpu.CompilerParams(vmem_limit_bytes=VMEM_LIMIT),
        cost_estimate=pl.CostEstimate(flops=flops, bytes_accessed=moved, transcendentals=0),
        **kwargs,
    )


def full_spec(shape):
    return pl.BlockSpec(shape, lambda *_: (0,) * len(shape))


SMEM = pl.BlockSpec(memory_space=pltpu.SMEM)
VMEM = pl.BlockSpec(memory_space=pltpu.VMEM)


def from_behind(block, axis, distance):
    devices = range(lax.axis_size(axis))
    route = [(i - distance, i) for i in devices if i - distance in devices]
    return lax.ppermute(block, axis, route)


def exchange(blocks, direction):
    size = lax.axis_size("expert")
    if len(blocks) == 1:
        return [lax.all_to_all(blocks[0], "expert", split_axis=0, concat_axis=0, tiled=True)]
    got = list(blocks)
    for d in sorted(range(1, size), key=lambda d: abs(2 * d - size)):
        route = [(i, (i + direction * d) % size) for i in range(size)]
        got[d] = lax.ppermute(blocks[d], "expert", route)
    return got


def joined(refs):
    if len(refs) == 1:
        return refs[0][...]
    return jnp.concatenate([ref[...].astype(F32) for ref in refs], axis=0).astype(BF16)


def parted(value, refs):
    share = value.shape[0] // len(refs)
    for d, ref in enumerate(refs):
        ref[...] = value[d * share : (d + 1) * share].astype(BF16)


def partners(me, distance, sources, direction, turned):
    if not turned:
        return distance
    device = me + direction * distance
    return jnp.where(device < 0, device + sources, jnp.where(device >= sources, device - sources, device))


def expert_hits(routes, experts):
    top, count = routes.shape
    lane = lax.broadcasted_iota(jnp.int32, (experts, count), 0)
    return [(routes[k : k + 1, :] == lane).astype(F32) for k in range(top)]


def slot_targets(routes, experts, capacity):
    top, count = routes.shape
    hits = expert_hits(routes, experts)
    earlier = lax.broadcasted_iota(jnp.int32, (count, count), 0) < lax.broadcasted_iota(
        jnp.int32, (count, count), 1
    )
    before = dot(sum(hits).astype(BF16), earlier.astype(F32).astype(BF16))
    targets = []
    for k in range(top):
        ranked = jnp.sum((before + sum(hits[:k], jnp.zeros_like(before))) * hits[k], 0, keepdims=True)
        targets.append(routes[k : k + 1, :] * capacity + ranked.astype(jnp.int32))
    return targets, hits


def tables_of(targets, row_keys):
    return [(row_keys == target).astype(F32) for target in targets]


def normalise(tokens, gain):
    widened = tokens.astype(F32)
    inv_rms = lax.rsqrt(jnp.mean(widened * widened, axis=-1, keepdims=True) + EPS)
    return widened, inv_rms, (widened * inv_rms * gain.astype(F32)).astype(BF16)


def route_shares(normed, router, hits):
    logits = dot(router, normed, NT)
    exponents = [jnp.exp(jnp.sum(logits * hit, axis=0, keepdims=True)) for hit in hits]
    total = sum(exponents)
    return [exponent / total for exponent in exponents]


def keys_of_part(sizes, me, columns, part):
    device = partners(me, columns[:, 0:1], sizes["sources"], 1, sizes["turned"])
    return columns[:, 2 + part : 3 + part] + device * sizes["share"]


def first_send_kernel(
    sizes, place, arrived_f, arrived_b, embedded, loss, gain, routes_f, routes_b,
    columns, tokens, upstream, data, *send,
):
    experts, capacity = sizes["experts"], sizes["capacity"]
    count = embedded.shape[0]
    chosen = jnp.where(place[0] == 0, embedded[...], arrived_f[...])
    tokens[...] = chosen
    data[:count, :] = normalise(chosen, gain[...])[2]
    chosen = jnp.where(place[0] == place[1], loss[...], arrived_b[...])
    upstream[...] = chosen
    data[count:, :] = chosen
    targets_f, _ = slot_targets(routes_f[...], experts, capacity)
    targets_b, _ = slot_targets(routes_b[...], experts, capacity)
    keys = keys_of_part(sizes, place[2], columns, 0)
    table_f = sum(tables_of(targets_f, keys))
    table_b = sum(tables_of([t + experts * capacity for t in targets_b], keys))
    table = jnp.concatenate([table_f, table_b], axis=1).astype(BF16)
    parted(dot(table, data[...]), send)


def mixing_kernel(
    sizes, place, data, saved, gain, router, routes_f, routes_b, columns,
    mixing_f, mixing_b, tables_b, shares_b, *sends,
):
    experts, capacity = sizes["experts"], sizes["capacity"]
    count = saved.shape[0]
    targets_f, hits = slot_targets(routes_f[...], experts, capacity)
    shares_f = route_shares(data[:count, :], router[...], hits)
    targets_b, hits = slot_targets(routes_b[...], experts, capacity)
    targets_b = [t + experts * capacity for t in targets_b]
    _, _, rows = normalise(saved[...], gain[...])
    own_shares = route_shares(rows, router[...], hits)
    for k, share in enumerate(own_shares):
        shares_b[k] = jnp.broadcast_to(share, shares_b.shape[1:])
    parts = mixing_f.shape[0]
    for part in range(parts):
        keys = keys_of_part(sizes, place[2], columns, part)
        found_f, found_b = tables_of(targets_f, keys), tables_of(targets_b, keys)
        mixing_f[part] = sum(t * s.astype(BF16).astype(F32) for t, s in zip(found_f, shares_f))
        mixing_b[part] = sum(t * s.astype(BF16).astype(F32) for t, s in zip(found_b, own_shares))
        for k, table in enumerate(found_b):
            tables_b[part, k] = table
        if part > 0:
            blocks = len(sends) // (parts - 1)
            table = jnp.concatenate([sum(found_f), sum(found_b)], axis=1).astype(BF16)
            parted(dot(table, data[...]), sends[(part - 1) * blocks : part * blocks])


def expert_kernel(sizes, steps, blocks, place, columns, lanes, wanted, wanted_lanes, *refs):
    got, (saved_pre, up, down) = refs[:blocks], refs[blocks : blocks + 3]
    out = refs[blocks + 3 : 2 * blocks + 3]
    rows, total_f, total_b, inner, results = refs[2 * blocks + 3 :]
    expert, step = pl.program_id(0), pl.program_id(1)
    held = pl.num_programs(0)
    width = rows.shape[1]
    padded, block_rows = sizes["padded"], sizes["block_rows"]
    source = (sizes["sources"], -1, sizes["turned"])

    @pl.when((expert == 0) & (step == 0))
    def _():
        have = partners(place[2], lanes[0:1, :], *source) * block_rows + lanes[1:2, :]
        order = (wanted[...] == have).astype(F32).astype(BF16)
        rows[...] = dot(order, joined(got)).astype(BF16)
        results[:, width:] = jnp.zeros((results.shape[0], results.shape[1] - width), BF16)

    own_f = pl.ds(pl.multiple_of(expert * padded, ROWS), padded)
    own_b = pl.ds(pl.multiple_of((held + expert) * padded, ROWS), padded)
    pre_act = dot(rows[own_f, :], up[0])
    hidden_grad = dot(rows[own_b, :], down[0], NT)
    hidden = (pre_act / (1.0 + jnp.exp(-pre_act))).astype(BF16)
    pre = saved_pre[0].astype(F32)
    gate = 1.0 / (1.0 + jnp.exp(-pre))
    inner_part = jnp.sum(hidden_grad * (pre * gate).astype(BF16).astype(F32), axis=1, keepdims=True)
    pre_grad = (hidden_grad * gate * (1.0 + pre * (1.0 - gate))).astype(BF16)
    part_f = dot(hidden, down[0])
    part_b = dot(pre_grad, up[0], NT)

    @pl.when(step == 0)
    def _():
        total_f[...] = part_f
        total_b[...] = part_b
        inner[...] = jnp.broadcast_to(inner_part, inner.shape)

    @pl.when(step > 0)
    def _():
        total_f[...] += part_f
        total_b[...] += part_b
        inner[...] += jnp.broadcast_to(inner_part, inner.shape)

    @pl.when(step == steps - 1)
    def _():
        results[own_f, :width] = total_f[...].astype(BF16)
        results[own_b, :width] = total_b[...].astype(BF16)
        results[own_b, width:] = inner[...].astype(BF16)

    @pl.when((expert == held - 1) & (step == steps - 1))
    def _():
        have = partners(place[2], columns[:, 0:1], *source) * block_rows + columns[:, 1:2]
        order = (have == wanted_lanes[...]).astype(F32).astype(BF16)
        parted(dot(order, results[...]), out)


def combine_kernel(
    experts, tokens, saved, upstream, gain, router, routes, mixing_f, mixing_b, tables, shares, *refs
):
    *backs, output, gradient = refs
    width = tokens.shape[1]
    parts = range(mixing_f.shape[0])
    blocks = len(backs) // len(parts)
    back = [joined(backs[p * blocks : (p + 1) * blocks]) for p in parts]
    widened = saved[...].astype(F32)
    inv_rms = lax.rsqrt(jnp.mean(widened * widened, axis=-1, keepdims=True) + EPS)
    hits = expert_hits(routes[...], experts)
    top = len(hits)
    share = [shares[k][:1, :] for k in range(top)]
    sums = [back[p][:, width:].astype(F32)[:, :1] for p in parts]
    inner = [
        sum(jnp.sum(tables[p, k] * sums[p], axis=0, keepdims=True) for p in parts)
        for k in range(top)
    ]
    mean = sum(share[k] * inner[k] for k in range(top))
    logit_grad = sum(share[k] * (inner[k] - mean) * hits[k] for k in range(top))
    high = logit_grad.astype(BF16)
    rest = logit_grad - high.astype(F32)
    middle = rest.astype(BF16)
    low = (rest - middle.astype(F32)).astype(BF16)
    output[0] = (
        tokens[...].astype(F32)
        + sum(dot(mixing_f[p].astype(BF16), back[p][:, :width], TN) for p in parts)
    ).astype(BF16)
    normed_grad = sum(dot(mixing_b[p].astype(BF16), back[p][:, :width], TN) for p in parts)
    for piece in (high, middle, low):
        normed_grad += dot(piece, router[...], TN)
    gained = normed_grad * gain[...].astype(F32)
    projected = jnp.mean(widened * gained, axis=-1, keepdims=True)
    grad = inv_rms * gained - widened * (inv_rms * inv_rms * inv_rms * projected)
    gradient[0] = (upstream[...].astype(F32) + grad).astype(BF16)


def exchange_order(parts, sources, local, capacity, padded):
    held = local // parts
    slots = sources * local * capacity
    block_rows = 2 * held * capacity
    columns = np.zeros((sources * block_rows, 2 + parts), np.int32)
    wanted = np.full((2 * held * padded, 1), -1, np.int32)
    for source in range(sources):
        for batch in range(2):
            for expert in range(held):
                for slot in range(capacity):
                    within = (batch * held + expert) * capacity + slot
                    row = source * block_rows + within
                    columns[row, :2] = source, within
                    for part in range(parts):
                        own = (part * held + expert) * capacity + slot
                        columns[row, 2 + part] = batch * slots + own
                    wanted[(batch * held + expert) * padded + source * capacity + slot] = row
    return columns, wanted


def on_device(
    forward_sent,
    embedded,
    forward_routes,
    backward_sent,
    loss_gradient,
    saved_inputs,
    backward_routes,
    pre_activation,
    norm_gain,
    router,
    up_weight,
    down_weight,
):
    section = lax.axis_index("section")
    last = lax.axis_size("section") - 1
    sources = lax.axis_size("expert")
    experts = router.shape[2]
    capacity = pre_activation.shape[3]
    local, width, hidden = up_weight.shape
    count = embedded.shape[0]
    top = forward_routes.shape[2]
    slots = experts * capacity
    rows = sources * capacity
    padded = -(-rows // ROWS) * ROWS
    steps = 2
    chunk = hidden // steps
    shape = jax.ShapeDtypeStruct
    parts = 2 if local % 2 == 0 else 1
    held = local // parts
    moved = 2 * slots // parts
    turned = sources <= 8
    blocks = sources if turned else 1
    columns, wanted = exchange_order(parts, sources, local, capacity, padded)
    lanes, wanted_lanes = np.ascontiguousarray(columns.T), np.ascontiguousarray(wanted.T)
    sizes = {
        "experts": experts,
        "capacity": capacity,
        "sources": sources,
        "share": local * capacity,
        "turned": turned,
        "padded": padded,
        "block_rows": moved // sources,
    }
    place = jnp.stack([section, jnp.full_like(section, last), lax.axis_index("expert")])
    place = place.astype(jnp.int32)
    sent = (shape((moved // blocks, width), BF16),) * blocks
    result = (shape((moved // blocks, width + LANES), BF16),) * blocks

    router_t = router[0].T
    routes_f, routes_b = forward_routes[0].T, backward_routes[0].T
    arrived_f = from_behind(forward_sent[0], "section", 1)
    arrived_b = from_behind(backward_sent[0], "section", -1)
    tokens, upstream, data, *send = call(
        functools.partial(first_send_kernel, sizes),
        (
            shape((count, width), BF16),
            shape((count, width), BF16),
            shape((2 * count, width), BF16),
            *sent,
        ),
        (4 * moved * count * width, 2 * (8 * count + moved) * width),
        in_specs=[SMEM] + [VMEM] * 8,
    )(
        place, arrived_f, arrived_b, embedded, loss_gradient, norm_gain, routes_f, routes_b, columns
    )
    mixing_f, mixing_b, tables_b, shares_b, *sends = call(
        functools.partial(mixing_kernel, sizes),
        (
            shape((parts, moved, count), F32),
            shape((parts, moved, count), F32),
            shape((parts, top, moved, count), F32),
            shape((top, 8, count), F32),
            *(sent * (parts - 1)),
        ),
        (4 * moved * count * width, 2 * (4 * count + moved) * width),
        in_specs=[SMEM] + [VMEM] * 7,
    )(place, data, saved_inputs[0], norm_gain, router_t, routes_f, routes_b, columns)
    saved_pre = jnp.transpose(pre_activation[0], (1, 0, 2, 3)).reshape(local, rows, hidden)
    saved_pre = jnp.pad(saved_pre, ((0, 0), (0, padded - rows), (0, 0)))
    sends, saved_pre = lax.optimization_barrier((sends, saved_pre))

    sends = [send] + [sends[p * blocks : (p + 1) * blocks] for p in range(parts - 1)]
    received = [exchange(blocks_out, 1) for blocks_out in sends]
    backs = []
    for part, got in enumerate(received):
        done = call(
            functools.partial(expert_kernel, sizes, steps, blocks),
            result,
            (8 * held * padded * width * hidden, 4 * held * width * hidden),
            grid=(held, steps),
            in_specs=[
                SMEM,
                full_spec(columns.shape),
                full_spec(lanes.shape),
                full_spec(wanted.shape),
                full_spec(wanted_lanes.shape),
                *[full_spec(block.shape) for block in got],
                pl.BlockSpec((1, padded, chunk), lambda e, f, p=part: (p * held + e, 0, f)),
                pl.BlockSpec((1, width, chunk), lambda e, f, p=part: (p * held + e, 0, f)),
                pl.BlockSpec((1, chunk, width), lambda e, f, p=part: (p * held + e, f, 0)),
            ],
            out_specs=tuple(full_spec(block.shape) for block in result),
            scratch_shapes=[
                pltpu.VMEM((2 * held * padded, width), BF16),
                pltpu.VMEM((padded, width), F32),
                pltpu.VMEM((padded, width), F32),
                pltpu.VMEM((padded, LANES), F32),
                pltpu.VMEM((2 * held * padded, width + LANES), BF16),
            ],
        )(place, columns, lanes, wanted, wanted_lanes, *got, saved_pre, up_weight, down_weight)
        backs += exchange(list(done), -1)
    return tuple(
        call(
            functools.partial(combine_kernel, experts),
            (shape((1, count, width), BF16),) * 2,
            (8 * moved * count * width, 2 * (5 * count + 2 * moved) * width),
        )(
            tokens, saved_inputs[0], upstream, norm_gain, router_t, routes_b,
            mixing_f, mixing_b, tables_b, shares_b, *backs,
        )
    )


def solution(mesh):
    return jax.shard_map(
        on_device,
        mesh=mesh,
        in_specs=(
            P("section", "expert", None),
            P("expert", None),
            P("section", "expert", None),
            P("section", "expert", None),
            P("expert", None),
            P("section", "expert", None),
            P("section", "expert", None),
            P("section", None, "expert", None, None),
            P("section", None),
            P("section", None, None),
            P("expert", None, None),
            P("expert", None, None),
        ),
        out_specs=(P("section", "expert", None), P("section", "expert", None)),
        check_vma=False,
    )
```

```python
import functools

import jax
import jax.numpy as jnp
import numpy as np
from jax import lax
from jax.experimental import pallas as pl
from jax.experimental.pallas import tpu as pltpu
from jax.sharding import PartitionSpec as P

EPS = 1e-06
BF16 = jnp.bfloat16
F32 = jnp.float32
LANES = 128
ROWS = 16
VMEM_LIMIT = 60 * 1024 * 1024
NT = (((1,), (1,)), ((), ()))
TN = (((0,), (0,)), ((), ()))


def dot(a, b, dims=(((1,), (0,)), ((), ()))):
    return lax.dot_general(a, b, dims, preferred_element_type=F32)


def call(kernel, out_shape, cost, **kwargs):
    flops, moved = cost
    return pl.pallas_call(
        kernel,
        out_shape=out_shape,
        compiler_params=pltpu.CompilerParams(vmem_limit_bytes=VMEM_LIMIT),
        cost_estimate=pl.CostEstimate(flops=flops, bytes_accessed=moved, transcendentals=0),
        **kwargs,
    )


def full_spec(shape):
    return pl.BlockSpec(shape, lambda *_: (0,) * len(shape))


SMEM = pl.BlockSpec(memory_space=pltpu.SMEM)
VMEM = pl.BlockSpec(memory_space=pltpu.VMEM)


def from_behind(block, axis, distance):
    devices = range(lax.axis_size(axis))
    route = [(i - distance, i) for i in devices if i - distance in devices]
    return lax.ppermute(block, axis, route)


def exchange(blocks, direction):
    size = lax.axis_size("expert")
    if len(blocks) == 1:
        return [lax.all_to_all(blocks[0], "expert", split_axis=0, concat_axis=0, tiled=True)]
    got = list(blocks)
    for d in sorted(range(1, size), key=lambda d: abs(2 * d - size)):
        route = [(i, (i + direction * d) % size) for i in range(size)]
        got[d] = lax.ppermute(blocks[d], "expert", route)
    return got


def joined(refs):
    if len(refs) == 1:
        return refs[0][...]
    return jnp.concatenate([ref[...].astype(F32) for ref in refs], axis=0).astype(BF16)


def parted(value, refs):
    share = value.shape[0] // len(refs)
    for d, ref in enumerate(refs):
        ref[...] = value[d * share : (d + 1) * share].astype(BF16)


def partners(me, distance, sources, direction, turned):
    if not turned:
        return distance
    device = me + direction * distance
    return jnp.where(device < 0, device + sources, jnp.where(device >= sources, device - sources, device))


def expert_hits(routes, experts):
    top, count = routes.shape
    lane = lax.broadcasted_iota(jnp.int32, (experts, count), 0)
    return [(routes[k : k + 1, :] == lane).astype(F32) for k in range(top)]


def slot_targets(routes, experts, capacity):
    top, count = routes.shape
    hits = expert_hits(routes, experts)
    earlier = lax.broadcasted_iota(jnp.int32, (count, count), 0) < lax.broadcasted_iota(
        jnp.int32, (count, count), 1
    )
    before = dot(sum(hits).astype(BF16), earlier.astype(F32).astype(BF16))
    targets = []
    for k in range(top):
        ranked = jnp.sum((before + sum(hits[:k], jnp.zeros_like(before))) * hits[k], 0, keepdims=True)
        targets.append(routes[k : k + 1, :] * capacity + ranked.astype(jnp.int32))
    return targets, hits


def tables_of(targets, row_keys):
    return [(row_keys == target).astype(F32) for target in targets]


def normalise(tokens, gain):
    widened = tokens.astype(F32)
    inv_rms = lax.rsqrt(jnp.mean(widened * widened, axis=-1, keepdims=True) + EPS)
    return widened, inv_rms, (widened * inv_rms * gain.astype(F32)).astype(BF16)


def route_shares(normed, router, hits):
    logits = dot(router, normed, NT)
    exponents = [jnp.exp(jnp.sum(logits * hit, axis=0, keepdims=True)) for hit in hits]
    total = sum(exponents)
    return [exponent / total for exponent in exponents]


def keys_of_part(sizes, me, columns, part, turned):
    device = partners(me, columns[:, 0:1], sizes["sources"], 1, turned)
    return columns[:, 2 + part : 3 + part] + device * sizes["share"]


def first_send_kernel(
    sizes, place, arrived_f, arrived_b, embedded, loss, gain, routes_f, routes_b,
    columns, tokens, upstream, data, *send,
):
    experts, capacity = sizes["experts"], sizes["capacity"]
    count = embedded.shape[0]
    chosen = jnp.where(place[0] == 0, embedded[...], arrived_f[...])
    tokens[...] = chosen
    data[:count, :] = normalise(chosen, gain[...])[2]
    chosen = jnp.where(place[0] == place[1], loss[...], arrived_b[...])
    upstream[...] = chosen
    data[count:, :] = chosen
    targets_f, _ = slot_targets(routes_f[...], experts, capacity)
    targets_b, _ = slot_targets(routes_b[...], experts, capacity)
    keys = keys_of_part(sizes, place[2], columns, 0, sizes["there"][0])
    table_f = sum(tables_of(targets_f, keys))
    table_b = sum(tables_of([t + experts * capacity for t in targets_b], keys))
    table = jnp.concatenate([table_f, table_b], axis=1).astype(BF16)
    parted(dot(table, data[...]), send)


def mixing_kernel(
    sizes, place, data, saved, gain, router, routes_f, routes_b, columns,
    mixing_f, mixing_b, tables_b, shares_b, *sends,
):
    experts, capacity = sizes["experts"], sizes["capacity"]
    count = saved.shape[0]
    targets_f, hits = slot_targets(routes_f[...], experts, capacity)
    shares_f = route_shares(data[:count, :], router[...], hits)
    targets_b, hits = slot_targets(routes_b[...], experts, capacity)
    targets_b = [t + experts * capacity for t in targets_b]
    _, _, rows = normalise(saved[...], gain[...])
    own_shares = route_shares(rows, router[...], hits)
    for k, share in enumerate(own_shares):
        shares_b[k] = jnp.broadcast_to(share, shares_b.shape[1:])
    sends = list(sends)
    for part in range(mixing_f.shape[0]):
        there, back = sizes["there"][part], sizes["back"][part]
        keys = keys_of_part(sizes, place[2], columns, part, back)
        found_f, found_b = tables_of(targets_f, keys), tables_of(targets_b, keys)
        mixing_f[part] = sum(t * s.astype(BF16).astype(F32) for t, s in zip(found_f, shares_f))
        mixing_b[part] = sum(t * s.astype(BF16).astype(F32) for t, s in zip(found_b, own_shares))
        for k, table in enumerate(found_b):
            tables_b[part, k] = table
        if part > 0:
            if there != back:
                keys = keys_of_part(sizes, place[2], columns, part, there)
                found_f, found_b = tables_of(targets_f, keys), tables_of(targets_b, keys)
            blocks = sizes["sources"] if there else 1
            table = jnp.concatenate([sum(found_f), sum(found_b)], axis=1).astype(BF16)
            parted(dot(table, data[...]), sends[:blocks])
            sends = sends[blocks:]


def expert_kernel(sizes, steps, part, place, columns, lanes, wanted, wanted_lanes, *refs):
    there, back = sizes["there"][part], sizes["back"][part]
    blocks = sizes["sources"] if there else 1
    got, (saved_pre, up, down) = refs[:blocks], refs[blocks : blocks + 3]
    out, (rows, total_f, total_b, inner, results) = refs[blocks + 3 : -5], refs[-5:]
    expert, step = pl.program_id(0), pl.program_id(1)
    held = pl.num_programs(0)
    width = rows.shape[1]
    padded, block_rows = sizes["padded"], sizes["block_rows"]
    source = (sizes["sources"], -1)

    @pl.when((expert == 0) & (step == 0))
    def _():
        have = partners(place[2], lanes[0:1, :], *source, there) * block_rows + lanes[1:2, :]
        order = (wanted[...] == have).astype(F32).astype(BF16)
        rows[...] = dot(order, joined(got)).astype(BF16)
        results[:, width:] = jnp.zeros((results.shape[0], results.shape[1] - width), BF16)

    own_f = pl.ds(pl.multiple_of(expert * padded, ROWS), padded)
    own_b = pl.ds(pl.multiple_of((held + expert) * padded, ROWS), padded)
    pre_act = dot(rows[own_f, :], up[0])
    hidden_grad = dot(rows[own_b, :], down[0], NT)
    hidden = (pre_act / (1.0 + jnp.exp(-pre_act))).astype(BF16)
    pre = saved_pre[0].astype(F32)
    gate = 1.0 / (1.0 + jnp.exp(-pre))
    inner_part = jnp.sum(hidden_grad * (pre * gate).astype(BF16).astype(F32), axis=1, keepdims=True)
    pre_grad = (hidden_grad * gate * (1.0 + pre * (1.0 - gate))).astype(BF16)
    part_f = dot(hidden, down[0])
    part_b = dot(pre_grad, up[0], NT)

    @pl.when(step == 0)
    def _():
        total_f[...] = part_f
        total_b[...] = part_b
        inner[...] = jnp.broadcast_to(inner_part, inner.shape)

    @pl.when(step > 0)
    def _():
        total_f[...] += part_f
        total_b[...] += part_b
        inner[...] += jnp.broadcast_to(inner_part, inner.shape)

    @pl.when(step == steps - 1)
    def _():
        results[own_f, :width] = total_f[...].astype(BF16)
        results[own_b, :width] = total_b[...].astype(BF16)
        results[own_b, width:] = inner[...].astype(BF16)

    @pl.when((expert == held - 1) & (step == steps - 1))
    def _():
        have = partners(place[2], columns[:, 0:1], *source, back) * block_rows + columns[:, 1:2]
        order = (have == wanted_lanes[...]).astype(F32).astype(BF16)
        parted(dot(order, results[...]), out)


def add_up(part, blocks, mixing_f, mixing_b, tables):
    back = joined(blocks)
    width = back.shape[1] - LANES
    sums = back[:, width:].astype(F32)[:, :1]
    return (
        dot(mixing_f[part].astype(BF16), back[:, :width], TN),
        dot(mixing_b[part].astype(BF16), back[:, :width], TN),
        [jnp.sum(tables[part, k] * sums, axis=0, keepdims=True) for k in range(tables.shape[1])],
    )


def early_kernel(sizes, tokens, mixing_f, mixing_b, tables, *refs):
    *backs, output, gradient, inner = refs
    sum_f, sum_b, sums = tokens[...].astype(F32), None, None
    for part, turned in enumerate(sizes["back"][:-1]):
        blocks = sizes["sources"] if turned else 1
        more_f, more_b, more = add_up(part, backs[:blocks], mixing_f, mixing_b, tables)
        backs = backs[blocks:]
        sum_f += more_f
        sum_b = more_b if sum_b is None else sum_b + more_b
        sums = more if sums is None else [a + b for a, b in zip(sums, more)]
    output[...] = sum_f
    if sums is None:
        gradient[...] = jnp.zeros(gradient.shape, F32)
        inner[...] = jnp.zeros(inner.shape, F32)
    else:
        gradient[...] = sum_b
        for k, row in enumerate(sums):
            inner[k] = jnp.broadcast_to(row, inner.shape[1:])


def late_kernel(
    experts, early_f, early_b, early_inner, saved, upstream, gain, router, routes,
    mixing_f, mixing_b, tables, shares, *refs,
):
    *backs, output, gradient = refs
    more_f, more_b, more = add_up(mixing_f.shape[0] - 1, backs, mixing_f, mixing_b, tables)
    widened = saved[...].astype(F32)
    inv_rms = lax.rsqrt(jnp.mean(widened * widened, axis=-1, keepdims=True) + EPS)
    hits = expert_hits(routes[...], experts)
    top = len(hits)
    share = [shares[k][:1, :] for k in range(top)]
    inner = [early_inner[k][:1, :] + more[k] for k in range(top)]
    mean = sum(share[k] * inner[k] for k in range(top))
    logit_grad = sum(share[k] * (inner[k] - mean) * hits[k] for k in range(top))
    high = logit_grad.astype(BF16)
    rest = logit_grad - high.astype(F32)
    middle = rest.astype(BF16)
    low = (rest - middle.astype(F32)).astype(BF16)
    output[0] = (early_f[...] + more_f).astype(BF16)
    normed_grad = early_b[...] + more_b
    for piece in (high, middle, low):
        normed_grad += dot(piece, router[...], TN)
    gained = normed_grad * gain[...].astype(F32)
    projected = jnp.mean(widened * gained, axis=-1, keepdims=True)
    grad = inv_rms * gained - widened * (inv_rms * inv_rms * inv_rms * projected)
    gradient[0] = (upstream[...].astype(F32) + grad).astype(BF16)


def exchange_order(parts, sources, local, capacity, padded):
    held = local // parts
    slots = sources * local * capacity
    block_rows = 2 * held * capacity
    columns = np.zeros((sources * block_rows, 2 + parts), np.int32)
    wanted = np.full((2 * held * padded, 1), -1, np.int32)
    for source in range(sources):
        for batch in range(2):
            for expert in range(held):
                for slot in range(capacity):
                    within = (batch * held + expert) * capacity + slot
                    row = source * block_rows + within
                    columns[row, :2] = source, within
                    for part in range(parts):
                        own = (part * held + expert) * capacity + slot
                        columns[row, 2 + part] = batch * slots + own
                    wanted[(batch * held + expert) * padded + source * capacity + slot] = row
    return columns, wanted


def on_device(
    forward_sent,
    embedded,
    forward_routes,
    backward_sent,
    loss_gradient,
    saved_inputs,
    backward_routes,
    pre_activation,
    norm_gain,
    router,
    up_weight,
    down_weight,
):
    section = lax.axis_index("section")
    last = lax.axis_size("section") - 1
    sources = lax.axis_size("expert")
    experts = router.shape[2]
    capacity = pre_activation.shape[3]
    local, width, hidden = up_weight.shape
    count = embedded.shape[0]
    top = forward_routes.shape[2]
    slots = experts * capacity
    rows = sources * capacity
    padded = -(-rows // ROWS) * ROWS
    steps = 2
    chunk = hidden // steps
    shape = jax.ShapeDtypeStruct
    parts = 2 if local % 2 == 0 else 1
    held = local // parts
    moved = 2 * slots // parts
    few = sources <= 8
    there = [few and part == 0 for part in range(parts)]
    back = [few and part == parts - 1 for part in range(parts)]
    columns, wanted = exchange_order(parts, sources, local, capacity, padded)
    lanes, wanted_lanes = np.ascontiguousarray(columns.T), np.ascontiguousarray(wanted.T)
    sizes = {
        "experts": experts,
        "capacity": capacity,
        "sources": sources,
        "share": local * capacity,
        "there": there,
        "back": back,
        "padded": padded,
        "block_rows": moved // sources,
    }
    place = jnp.stack([section, jnp.full_like(section, last), lax.axis_index("expert")])
    place = place.astype(jnp.int32)

    def blocks_of(turned, columns):
        blocks = sources if turned else 1
        return [shape((moved // blocks, columns), BF16)] * blocks

    later = [block for turned in there[1:] for block in blocks_of(turned, width)]

    router_t = router[0].T
    routes_f, routes_b = forward_routes[0].T, backward_routes[0].T
    arrived_f = from_behind(forward_sent[0], "section", 1)
    arrived_b = from_behind(backward_sent[0], "section", -1)
    tokens, upstream, data, *send = call(
        functools.partial(first_send_kernel, sizes),
        (
            shape((count, width), BF16),
            shape((count, width), BF16),
            shape((2 * count, width), BF16),
            *blocks_of(there[0], width),
        ),
        (4 * moved * count * width, 2 * (8 * count + moved) * width),
        in_specs=[SMEM] + [VMEM] * 8,
    )(
        place, arrived_f, arrived_b, embedded, loss_gradient, norm_gain, routes_f, routes_b, columns
    )
    mixing_f, mixing_b, tables_b, shares_b, *sends = call(
        functools.partial(mixing_kernel, sizes),
        (
            shape((parts, moved, count), F32),
            shape((parts, moved, count), F32),
            shape((parts, top, moved, count), F32),
            shape((top, 8, count), F32),
            *later,
        ),
        (4 * moved * count * width, 2 * (4 * count + moved) * width),
        in_specs=[SMEM] + [VMEM] * 7,
    )(place, data, saved_inputs[0], norm_gain, router_t, routes_f, routes_b, columns)
    saved_pre = jnp.transpose(pre_activation[0], (1, 0, 2, 3)).reshape(local, rows, hidden)
    saved_pre = jnp.pad(saved_pre, ((0, 0), (0, padded - rows), (0, 0)))
    backs = []
    got = exchange(send, 1)
    for part in range(parts):
        if part + 1 < parts:
            sends, saved_pre, got = lax.optimization_barrier((sends, saved_pre, got))
            blocks = len(blocks_of(there[part + 1], width))
            coming = exchange(sends[:blocks], 1)
            sends = sends[blocks:]
        result = blocks_of(back[part], width + LANES)
        done = call(
            functools.partial(expert_kernel, sizes, steps, part),
            tuple(result),
            (8 * held * padded * width * hidden, 4 * held * width * hidden),
            grid=(held, steps),
            in_specs=[
                SMEM,
                full_spec(columns.shape),
                full_spec(lanes.shape),
                full_spec(wanted.shape),
                full_spec(wanted_lanes.shape),
                *[full_spec(block.shape) for block in got],
                pl.BlockSpec((1, padded, chunk), lambda e, f, p=part: (p * held + e, 0, f)),
                pl.BlockSpec((1, width, chunk), lambda e, f, p=part: (p * held + e, 0, f)),
                pl.BlockSpec((1, chunk, width), lambda e, f, p=part: (p * held + e, f, 0)),
            ],
            out_specs=tuple(full_spec(block.shape) for block in result),
            scratch_shapes=[
                pltpu.VMEM((2 * held * padded, width), BF16),
                pltpu.VMEM((padded, width), F32),
                pltpu.VMEM((padded, width), F32),
                pltpu.VMEM((padded, LANES), F32),
                pltpu.VMEM((2 * held * padded, width + LANES), BF16),
            ],
        )(place, columns, lanes, wanted, wanted_lanes, *got, saved_pre, up_weight, down_weight)
        backs.append(exchange(list(done), -1))
        got = coming if part + 1 < parts else None
    early = call(
        functools.partial(early_kernel, sizes),
        (
            shape((count, width), F32),
            shape((count, width), F32),
            shape((top, 8, count), F32),
        ),
        (4 * moved * count * width, 2 * (5 * count + moved) * width),
    )(tokens, mixing_f, mixing_b, tables_b, *[block for got in backs[:-1] for block in got])
    return tuple(
        call(
            functools.partial(late_kernel, experts),
            (shape((1, count, width), BF16),) * 2,
            (4 * moved * count * width, 2 * (8 * count + moved) * width),
        )(
            *early, saved_inputs[0], upstream, norm_gain, router_t, routes_b,
            mixing_f, mixing_b, tables_b, shares_b, *backs[-1],
        )
    )


def solution(mesh):
    return jax.shard_map(
        on_device,
        mesh=mesh,
        in_specs=(
            P("section", "expert", None),
            P("expert", None),
            P("section", "expert", None),
            P("section", "expert", None),
            P("expert", None),
            P("section", "expert", None),
            P("section", "expert", None),
            P("section", None, "expert", None, None),
            P("section", None),
            P("section", None, None),
            P("expert", None, None),
            P("expert", None, None),
        ),
        out_specs=(P("section", "expert", None), P("section", "expert", None)),
        check_vma=False,
    )
```

```python
import functools

import jax
import jax.numpy as jnp
import numpy as np
from jax import lax
from jax.experimental import pallas as pl
from jax.experimental.pallas import tpu as pltpu
from jax.sharding import PartitionSpec as P

EPS = 1e-06
BF16 = jnp.bfloat16
F32 = jnp.float32
LANES = 128
ROWS = 16
VMEM_LIMIT = 60 * 1024 * 1024
NT = (((1,), (1,)), ((), ()))
TN = (((0,), (0,)), ((), ()))


def dot(a, b, dims=(((1,), (0,)), ((), ()))):
    return lax.dot_general(a, b, dims, preferred_element_type=F32)


def call(kernel, out_shape, cost, **kwargs):
    flops, moved = cost
    return pl.pallas_call(
        kernel,
        out_shape=out_shape,
        compiler_params=pltpu.CompilerParams(vmem_limit_bytes=VMEM_LIMIT),
        cost_estimate=pl.CostEstimate(flops=flops, bytes_accessed=moved, transcendentals=0),
        **kwargs,
    )


def full_spec(shape):
    return pl.BlockSpec(shape, lambda *_: (0,) * len(shape))


SMEM = pl.BlockSpec(memory_space=pltpu.SMEM)
VMEM = pl.BlockSpec(memory_space=pltpu.VMEM)


def from_behind(block, axis, distance):
    devices = range(lax.axis_size(axis))
    route = [(i - distance, i) for i in devices if i - distance in devices]
    return lax.ppermute(block, axis, route)


def rotate(block, axis, distance):
    size = lax.axis_size(axis)
    return lax.ppermute(block, axis, [(i, (i + distance) % size) for i in range(size)])


def exchange(blocks, direction):
    size = lax.axis_size("expert")
    if len(blocks) == 1:
        return [lax.all_to_all(blocks[0], "expert", split_axis=0, concat_axis=0, tiled=True)]
    got = list(blocks)
    for d in sorted(range(1, size), key=lambda d: abs(2 * d - size)):
        route = [(i, (i + direction * d) % size) for i in range(size)]
        got[d] = lax.ppermute(blocks[d], "expert", route)
    return got


def joined(refs):
    if len(refs) == 1:
        return refs[0][...]
    return jnp.concatenate([ref[...].astype(F32) for ref in refs], axis=0).astype(BF16)


def parted(value, refs):
    share = value.shape[0] // len(refs)
    for d, ref in enumerate(refs):
        ref[...] = value[d * share : (d + 1) * share].astype(BF16)


def partners(me, distance, sources, direction, turned):
    if not turned:
        return distance
    device = me + direction * distance
    return jnp.where(device < 0, device + sources, jnp.where(device >= sources, device - sources, device))


def expert_hits(routes, experts):
    top, count = routes.shape
    lane = lax.broadcasted_iota(jnp.int32, (experts, count), 0)
    return [(routes[k : k + 1, :] == lane).astype(F32) for k in range(top)]


def slot_targets(routes, experts, capacity):
    top, count = routes.shape
    hits = expert_hits(routes, experts)
    earlier = lax.broadcasted_iota(jnp.int32, (count, count), 0) < lax.broadcasted_iota(
        jnp.int32, (count, count), 1
    )
    before = dot(sum(hits).astype(BF16), earlier.astype(F32).astype(BF16))
    targets = []
    for k in range(top):
        ranked = jnp.sum((before + sum(hits[:k], jnp.zeros_like(before))) * hits[k], 0, keepdims=True)
        targets.append(routes[k : k + 1, :] * capacity + ranked.astype(jnp.int32))
    return targets, hits


def tables_of(targets, row_keys):
    return [(row_keys == target).astype(F32) for target in targets]


def normalise(tokens, gain):
    widened = tokens.astype(F32)
    inv_rms = lax.rsqrt(jnp.mean(widened * widened, axis=-1, keepdims=True) + EPS)
    return widened, inv_rms, (widened * inv_rms * gain.astype(F32)).astype(BF16)


def route_shares(normed, router, hits):
    logits = dot(router, normed, NT)
    exponents = [jnp.exp(jnp.sum(logits * hit, axis=0, keepdims=True)) for hit in hits]
    total = sum(exponents)
    return [exponent / total for exponent in exponents]


def keys_of_part(sizes, me, columns, part, turned):
    device = partners(me, columns[:, 0:1], sizes["sources"], 1, turned)
    return columns[:, 2 + part : 3 + part] + device * sizes["share"]


def forward_rows_kernel(
    sizes, place, sent, embedded, gain, routes, columns, tokens, normed, rows
):
    chosen = jnp.where(place[0] == place[1], embedded[...], sent[...])
    tokens[...] = chosen
    data = normalise(chosen, gain[...])[2]
    normed[...] = data
    targets, _ = slot_targets(routes[...], sizes["experts"], sizes["capacity"])
    keys = keys_of_part(sizes, place[2], columns, 0, sizes["there"][0])
    rows[...] = dot(sum(tables_of(targets, keys)).astype(BF16), data).astype(BF16)


def first_send_kernel(sizes, place, arrived, loss, routes, columns, rows, upstream, *send):
    experts, capacity = sizes["experts"], sizes["capacity"]
    chosen = jnp.where(place[0] == place[1], loss[...], arrived[...])
    upstream[...] = chosen
    targets, _ = slot_targets(routes[...], experts, capacity)
    keys = keys_of_part(sizes, place[2], columns, 0, sizes["there"][0])
    table = sum(tables_of([t + experts * capacity for t in targets], keys)).astype(BF16)
    parted(rows[...].astype(F32) + dot(table, chosen), send)


def later_send_kernel(sizes, place, normed, upstream, routes_f, routes_b, columns, *sends):
    experts, capacity = sizes["experts"], sizes["capacity"]
    targets_f, _ = slot_targets(routes_f[...], experts, capacity)
    targets_b, _ = slot_targets(routes_b[...], experts, capacity)
    targets_b = [t + experts * capacity for t in targets_b]
    data = jnp.concatenate([normed[...], upstream[...]], axis=0)
    for part, there in enumerate(sizes["there"]):
        if part > 0:
            keys = keys_of_part(sizes, place[2], columns, part, there)
            found = [sum(tables_of(targets, keys)) for targets in (targets_f, targets_b)]
            blocks = sizes["sources"] if there else 1
            parted(dot(jnp.concatenate(found, axis=1).astype(BF16), data), sends[:blocks])
            sends = sends[blocks:]


def mixing_kernel(
    sizes, place, normed, saved, router_f, routes_f, gain, router_b, routes_b, columns,
    shares_b, *refs,
):
    experts, capacity = sizes["experts"], sizes["capacity"]
    targets_f, hits = slot_targets(routes_f[...], experts, capacity)
    shares_f = route_shares(normed[...], router_f[...], hits)
    targets_b, hits = slot_targets(routes_b[...], experts, capacity)
    targets_b = [t + experts * capacity for t in targets_b]
    own_shares = route_shares(normalise(saved[...], gain[...])[2], router_b[...], hits)
    for k, share in enumerate(own_shares):
        shares_b[k] = jnp.broadcast_to(share, shares_b.shape[1:])
    for part, back in enumerate(sizes["back"]):
        mixing_f, mixing_b, tables_b = refs[3 * part : 3 * part + 3]
        keys = keys_of_part(sizes, place[2], columns, part, back)
        found_f, found_b = tables_of(targets_f, keys), tables_of(targets_b, keys)
        for mixing, found, shares in (
            (mixing_f, found_f, shares_f), (mixing_b, found_b, own_shares)
        ):
            mixed = sum(t * s.astype(BF16).astype(F32) for t, s in zip(found, shares))
            mixing[...] = jnp.transpose(mixed).astype(BF16)
        for k, table in enumerate(found_b):
            tables_b[k] = table


def expert_kernel(sizes, steps, part, place, columns, lanes, wanted, wanted_lanes, *refs):
    there, back = sizes["there"][part], sizes["back"][part]
    blocks = sizes["sources"] if there else 1
    got, (saved_pre, up, down) = refs[:blocks], refs[blocks : blocks + 3]
    out, (rows, total_f, total_b, inner, results) = refs[blocks + 3 : -5], refs[-5:]
    expert, step = pl.program_id(0), pl.program_id(1)
    held = pl.num_programs(0)
    width = rows.shape[1]
    padded, block_rows = sizes["padded"], sizes["block_rows"]
    source = (sizes["sources"], -1)

    @pl.when((expert == 0) & (step == 0))
    def _():
        have = partners(place[2], lanes[0:1, :], *source, there) * block_rows + lanes[1:2, :]
        order = (wanted[...] == have).astype(F32).astype(BF16)
        rows[...] = dot(order, joined(got)).astype(BF16)
        results[:, width:] = jnp.zeros((results.shape[0], results.shape[1] - width), BF16)

    own_f = pl.ds(pl.multiple_of(expert * padded, ROWS), padded)
    own_b = pl.ds(pl.multiple_of((held + expert) * padded, ROWS), padded)
    pre_act = dot(rows[own_f, :], up[0])
    hidden_grad = dot(rows[own_b, :], down[0], NT)
    hidden = (pre_act / (1.0 + jnp.exp(-pre_act))).astype(BF16)
    pre = saved_pre[0].astype(F32)
    gate = 1.0 / (1.0 + jnp.exp(-pre))
    inner_part = jnp.sum(hidden_grad * (pre * gate).astype(BF16).astype(F32), axis=1, keepdims=True)
    pre_grad = (hidden_grad * gate * (1.0 + pre * (1.0 - gate))).astype(BF16)
    part_f = dot(hidden, down[0])
    part_b = dot(pre_grad, up[0], NT)

    @pl.when(step == 0)
    def _():
        total_f[...] = part_f
        total_b[...] = part_b
        inner[...] = jnp.broadcast_to(inner_part, inner.shape)

    @pl.when(step > 0)
    def _():
        total_f[...] += part_f
        total_b[...] += part_b
        inner[...] += jnp.broadcast_to(inner_part, inner.shape)

    @pl.when(step == steps - 1)
    def _():
        results[own_f, :width] = total_f[...].astype(BF16)
        results[own_b, :width] = total_b[...].astype(BF16)
        results[own_b, width:] = inner[...].astype(BF16)

    @pl.when((expert == held - 1) & (step == steps - 1))
    def _():
        have = partners(place[2], columns[:, 0:1], *source, back) * block_rows + columns[:, 1:2]
        order = (have == wanted_lanes[...]).astype(F32).astype(BF16)
        parted(dot(order, results[...]), out)


def inner_of(back, tables):
    width = back.shape[1] - LANES
    sums = back[:, width:].astype(F32)[:, :1]
    return [jnp.sum(tables[k] * sums, axis=0, keepdims=True) for k in range(tables.shape[0])]


def early_kernel(sizes, tokens, *refs):
    *refs, output, gradient, inner = refs
    width = tokens.shape[1]
    sum_f, sum_b = tokens[...].astype(F32), jnp.zeros(tokens.shape, F32)
    sums = [jnp.zeros((1, inner.shape[2]), F32)] * inner.shape[0]
    for turned in sizes["back"][:-1]:
        blocks = sizes["sources"] if turned else 1
        back = joined(refs[3 : 3 + blocks])
        mixing_f, mixing_b, tables = refs[:3]
        refs = refs[3 + blocks :]
        sum_f += dot(mixing_f[...], back[:, :width])
        sum_b += dot(mixing_b[...], back[:, :width])
        sums = [a + b for a, b in zip(sums, inner_of(back, tables))]
    output[...] = sum_f
    gradient[...] = sum_b
    for k, row in enumerate(sums):
        inner[k] = jnp.broadcast_to(row, inner.shape[1:])


def late_forward_kernel(early, mixing, *refs):
    *blocks, output = refs
    output[...] = (
        early[...] + dot(mixing[...], joined(blocks)[:, : early.shape[1]])
    ).astype(BF16)


def late_backward_kernel(
    experts, early, early_inner, mixing, tables, saved, upstream, gain, router, routes, shares, *refs
):
    *blocks, gradient = refs
    back = joined(blocks)
    widened = saved[...].astype(F32)
    inv_rms = lax.rsqrt(jnp.mean(widened * widened, axis=-1, keepdims=True) + EPS)
    hits = expert_hits(routes[...], experts)
    top = len(hits)
    share = [shares[k][:1, :] for k in range(top)]
    inner = [early_inner[k][:1, :] + row for k, row in enumerate(inner_of(back, tables))]
    mean = sum(share[k] * inner[k] for k in range(top))
    logit_grad = sum(share[k] * (inner[k] - mean) * hits[k] for k in range(top))
    high = logit_grad.astype(BF16)
    rest = logit_grad - high.astype(F32)
    middle = rest.astype(BF16)
    low = (rest - middle.astype(F32)).astype(BF16)
    normed_grad = early[...] + dot(mixing[...], back[:, : early.shape[1]])
    for piece in (high, middle, low):
        normed_grad += dot(piece, router[...], TN)
    gained = normed_grad * gain[...].astype(F32)
    projected = jnp.mean(widened * gained, axis=-1, keepdims=True)
    grad = inv_rms * gained - widened * (inv_rms * inv_rms * inv_rms * projected)
    gradient[0] = (upstream[...].astype(F32) + grad).astype(BF16)


def exchange_order(parts, sources, local, capacity, padded):
    held = local // parts
    slots = sources * local * capacity
    block_rows = 2 * held * capacity
    columns = np.zeros((sources * block_rows, 2 + parts), np.int32)
    wanted = np.full((2 * held * padded, 1), -1, np.int32)
    for source in range(sources):
        for batch in range(2):
            for expert in range(held):
                for slot in range(capacity):
                    within = (batch * held + expert) * capacity + slot
                    row = source * block_rows + within
                    columns[row, :2] = source, within
                    for part in range(parts):
                        own = (part * held + expert) * capacity + slot
                        columns[row, 2 + part] = batch * slots + own
                    wanted[(batch * held + expert) * padded + source * capacity + slot] = row
    return columns, wanted


def on_device(
    forward_sent,
    embedded,
    forward_routes,
    backward_sent,
    loss_gradient,
    saved_inputs,
    backward_routes,
    pre_activation,
    norm_gain,
    router,
    up_weight,
    down_weight,
):
    section = lax.axis_index("section")
    last = lax.axis_size("section") - 1
    sources = lax.axis_size("expert")
    experts = router.shape[2]
    capacity = pre_activation.shape[3]
    local, width, hidden = up_weight.shape
    count = embedded.shape[0]
    top = forward_routes.shape[2]
    slots = experts * capacity
    rows = sources * capacity
    padded = -(-rows // ROWS) * ROWS
    steps = 2
    chunk = hidden // steps
    shape = jax.ShapeDtypeStruct
    parts = 2 if local % 2 == 0 else 1
    held = local // parts
    moved = 2 * slots // parts
    few = sources <= 8
    there = [few and part == 0 for part in range(parts)]
    back = [few and part == parts - 1 for part in range(parts)]
    columns, wanted = exchange_order(parts, sources, local, capacity, padded)
    lanes, wanted_lanes = np.ascontiguousarray(columns.T), np.ascontiguousarray(wanted.T)
    sizes = {
        "experts": experts,
        "capacity": capacity,
        "sources": sources,
        "share": local * capacity,
        "there": there,
        "back": back,
        "padded": padded,
        "block_rows": moved // sources,
    }
    place = jnp.stack([section, jnp.full_like(section, last), lax.axis_index("expert")])
    place = place.astype(jnp.int32)

    def blocks_of(turned, columns):
        blocks = sources if turned else 1
        return [shape((moved // blocks, columns), BF16)] * blocks

    later = [block for turned in there[1:] for block in blocks_of(turned, width)]

    router_t = router[0].T
    routes_b = backward_routes[0].T
    arrived = from_behind(backward_sent[0], "section", -1)
    routes_f = rotate(forward_routes[0].T, "section", -1)
    gain_f = rotate(norm_gain, "section", -1)
    tokens, normed, first_rows = call(
        functools.partial(forward_rows_kernel, sizes),
        (
            shape((count, width), BF16),
            shape((count, width), BF16),
            shape((moved, width), BF16),
        ),
        (2 * moved * count * width, 2 * (4 * count + moved) * width),
        in_specs=[SMEM] + [VMEM] * 5,
    )(place, forward_sent[0], embedded, gain_f, routes_f, columns)
    arrived, first_rows = lax.optimization_barrier((arrived, first_rows))
    upstream, *send = call(
        functools.partial(first_send_kernel, sizes),
        (shape((count, width), BF16), *blocks_of(there[0], width)),
        (2 * moved * count * width, 2 * (3 * count + 2 * moved) * width),
        in_specs=[SMEM] + [VMEM] * 5,
    )(place, arrived, loss_gradient, routes_b, columns, first_rows)
    sends = []
    if parts > 1:
        sends = call(
            functools.partial(later_send_kernel, sizes),
            tuple(later),
            (4 * moved * count * width, 2 * (2 * count + moved) * width),
            in_specs=[SMEM] + [VMEM] * 5,
        )(place, normed, upstream, routes_f, routes_b, columns)
    router_late, _ = lax.optimization_barrier((router_t, send[0]))
    router_f = rotate(router_late, "section", -1)
    shares_b, *mixing = call(
        functools.partial(mixing_kernel, sizes),
        (
            shape((top, 8, count), F32),
            *[
                shape((count, moved), BF16),
                shape((count, moved), BF16),
                shape((top, moved, count), F32),
            ]
            * parts,
        ),
        (4 * count * width * experts, 2 * (2 * count + 2 * experts) * width),
        in_specs=[SMEM] + [VMEM] * 8,
    )(
        place, normed, saved_inputs[0], router_f, routes_f, norm_gain, router_t, routes_b, columns
    )
    mixing = [mixing[3 * part : 3 * part + 3] for part in range(parts)]
    saved_pre = jnp.transpose(pre_activation[0], (1, 0, 2, 3)).reshape(local, rows, hidden)
    saved_pre = jnp.pad(saved_pre, ((0, 0), (0, padded - rows), (0, 0)))
    backs = []
    got = exchange(send, 1)
    for part in range(parts):
        if part + 1 < parts:
            sends, saved_pre, got, mixing = lax.optimization_barrier(
                (sends, saved_pre, got, mixing)
            )
            blocks = len(blocks_of(there[part + 1], width))
            coming = exchange(sends[:blocks], 1)
            sends = sends[blocks:]
        result = blocks_of(back[part], width + LANES)
        done = call(
            functools.partial(expert_kernel, sizes, steps, part),
            tuple(result),
            (8 * held * padded * width * hidden, 4 * held * width * hidden),
            grid=(held, steps),
            in_specs=[
                SMEM,
                full_spec(columns.shape),
                full_spec(lanes.shape),
                full_spec(wanted.shape),
                full_spec(wanted_lanes.shape),
                *[full_spec(block.shape) for block in got],
                pl.BlockSpec((1, padded, chunk), lambda e, f, p=part: (p * held + e, 0, f)),
                pl.BlockSpec((1, width, chunk), lambda e, f, p=part: (p * held + e, 0, f)),
                pl.BlockSpec((1, chunk, width), lambda e, f, p=part: (p * held + e, f, 0)),
            ],
            out_specs=tuple(full_spec(block.shape) for block in result),
            scratch_shapes=[
                pltpu.VMEM((2 * held * padded, width), BF16),
                pltpu.VMEM((padded, width), F32),
                pltpu.VMEM((padded, width), F32),
                pltpu.VMEM((padded, LANES), F32),
                pltpu.VMEM((2 * held * padded, width + LANES), BF16),
            ],
        )(place, columns, lanes, wanted, wanted_lanes, *got, saved_pre, up_weight, down_weight)
        backs.append(exchange(list(done), -1))
        got = coming if part + 1 < parts else None
    early_f, early_b, early_inner = call(
        functools.partial(early_kernel, sizes),
        (
            shape((count, width), F32),
            shape((count, width), F32),
            shape((top, 8, count), F32),
        ),
        (4 * moved * count * width, 2 * (5 * count + moved) * width),
    )(tokens, *[ref for part in range(parts - 1) for ref in (*mixing[part], *backs[part])])
    mixing_f, mixing_b, tables_b = mixing[-1]
    output = call(
        late_forward_kernel,
        shape((count, width), BF16),
        (2 * moved * count * width, 2 * (3 * count + moved) * width),
    )(early_f, mixing_f, *backs[-1])
    output = rotate(output, "section", 1)
    gradient = call(
        functools.partial(late_backward_kernel, experts),
        shape((1, count, width), BF16),
        (2 * moved * count * width, 2 * (7 * count + moved) * width),
    )(
        early_b, early_inner, mixing_b, tables_b, saved_inputs[0], upstream, norm_gain, router_t,
        routes_b, shares_b, *backs[-1],
    )
    return (output[None], gradient)


def solution(mesh):
    return jax.shard_map(
        on_device,
        mesh=mesh,
        in_specs=(
            P("section", "expert", None),
            P("expert", None),
            P("section", "expert", None),
            P("section", "expert", None),
            P("expert", None),
            P("section", "expert", None),
            P("section", "expert", None),
            P("section", None, "expert", None, None),
            P("section", None),
            P("section", None, None),
            P("expert", None, None),
            P("expert", None, None),
        ),
        out_specs=(P("section", "expert", None), P("section", "expert", None)),
        check_vma=False,
    )
```

```python
import functools

import jax
import jax.numpy as jnp
import numpy as np
from jax import lax
from jax.experimental import pallas as pl
from jax.experimental.pallas import tpu as pltpu
from jax.sharding import PartitionSpec as P

EPS = 1e-06
BF16 = jnp.bfloat16
F32 = jnp.float32
LANES = 128
ROWS = 16
VMEM_LIMIT = 60 * 1024 * 1024
NT = (((1,), (1,)), ((), ()))
TN = (((0,), (0,)), ((), ()))


def dot(a, b, dims=(((1,), (0,)), ((), ()))):
    return lax.dot_general(a, b, dims, preferred_element_type=F32)


def call(kernel, out_shape, cost, **kwargs):
    flops, moved = cost
    return pl.pallas_call(
        kernel,
        out_shape=out_shape,
        compiler_params=pltpu.CompilerParams(vmem_limit_bytes=VMEM_LIMIT),
        cost_estimate=pl.CostEstimate(flops=flops, bytes_accessed=moved, transcendentals=0),
        **kwargs,
    )


SMEM = pl.BlockSpec(memory_space=pltpu.SMEM)
VMEM = pl.BlockSpec(memory_space=pltpu.VMEM)
HBM = pl.BlockSpec(memory_space=pl.ANY)


def from_behind(block, axis, distance):
    devices = range(lax.axis_size(axis))
    route = [(i - distance, i) for i in devices if i - distance in devices]
    return lax.ppermute(block, axis, route)


def exchange(blocks, direction):
    size = lax.axis_size("expert")
    if len(blocks) == 1:
        return [lax.all_to_all(blocks[0], "expert", split_axis=0, concat_axis=0, tiled=True)]
    got = list(blocks)
    for d in sorted(range(1, size), key=lambda d: abs(2 * d - size)):
        route = [(i, (i + direction * d) % size) for i in range(size)]
        got[d] = lax.ppermute(blocks[d], "expert", route)
    return got


def joined(refs):
    if len(refs) == 1:
        return refs[0][...]
    return jnp.concatenate([ref[...].astype(F32) for ref in refs], axis=0).astype(BF16)


def parted(value, refs):
    share = value.shape[0] // len(refs)
    for d, ref in enumerate(refs):
        ref[...] = value[d * share : (d + 1) * share].astype(BF16)


def partners(me, distance, sources, direction, turned):
    if not turned:
        return distance
    device = me + direction * distance
    return jnp.where(device < 0, device + sources, jnp.where(device >= sources, device - sources, device))


def expert_hits(routes, experts):
    top, count = routes.shape
    lane = lax.broadcasted_iota(jnp.int32, (experts, count), 0)
    return [(routes[k : k + 1, :] == lane).astype(F32) for k in range(top)]


def slot_targets(routes, experts, capacity):
    top, count = routes.shape
    hits = expert_hits(routes, experts)
    earlier = lax.broadcasted_iota(jnp.int32, (count, count), 0) < lax.broadcasted_iota(
        jnp.int32, (count, count), 1
    )
    before = dot(sum(hits).astype(BF16), earlier.astype(F32).astype(BF16))
    targets = []
    for k in range(top):
        ranked = jnp.sum((before + sum(hits[:k], jnp.zeros_like(before))) * hits[k], 0, keepdims=True)
        targets.append(routes[k : k + 1, :] * capacity + ranked.astype(jnp.int32))
    return targets, hits


def tables_of(targets, row_keys):
    return [(row_keys == target).astype(F32) for target in targets]


def normalise(tokens, gain):
    widened = tokens.astype(F32)
    inv_rms = lax.rsqrt(jnp.mean(widened * widened, axis=-1, keepdims=True) + EPS)
    return widened, inv_rms, (widened * inv_rms * gain.astype(F32)).astype(BF16)


def route_shares(normed, router, hits):
    logits = dot(router, normed, NT)
    exponents = [jnp.exp(jnp.sum(logits * hit, axis=0, keepdims=True)) for hit in hits]
    total = sum(exponents)
    return [exponent / total for exponent in exponents]


def keys_of_part(sizes, me, columns, part, turned):
    device = partners(me, columns[:, 0:1], sizes["sources"], 1, turned)
    return columns[:, 2 + part : 3 + part] + device * sizes["share"]


def rows_to_send(place, arrived_f, arrived_b, embedded, loss, gain):
    tokens = jnp.where(place[0] == 0, embedded[...], arrived_f[...])
    upstream = jnp.where(place[0] == place[1], loss[...], arrived_b[...])
    return tokens, normalise(tokens, gain[...])[2], upstream


def first_send_kernel(
    sizes, place, arrived_f, arrived_b, embedded, loss, gain, routes_f, routes_b, columns, *send
):
    experts, capacity = sizes["experts"], sizes["capacity"]
    _, normed, upstream = rows_to_send(place, arrived_f, arrived_b, embedded, loss, gain)
    targets_f, _ = slot_targets(routes_f[...], experts, capacity)
    targets_b, _ = slot_targets(routes_b[...], experts, capacity)
    keys = keys_of_part(sizes, place[2], columns, 0, sizes["there"][0])
    table_f = sum(tables_of(targets_f, keys))
    table_b = sum(tables_of([t + experts * capacity for t in targets_b], keys))
    table = jnp.concatenate([table_f, table_b], axis=1).astype(BF16)
    parted(dot(table, jnp.concatenate([normed, upstream], axis=0)), send)


def mixing_kernel(
    sizes, place, arrived_f, arrived_b, embedded, loss, gain, routes_f, routes_b, columns,
    saved, router, tokens, upstream, shares_b, *refs,
):
    experts, capacity = sizes["experts"], sizes["capacity"]
    parts = len(sizes["back"])
    mixing, sends = refs[: 3 * parts], refs[3 * parts :]
    tokens[...], normed, upstream[...] = rows_to_send(
        place, arrived_f, arrived_b, embedded, loss, gain
    )
    data = jnp.concatenate([normed, upstream[...]], axis=0)
    targets_f, hits = slot_targets(routes_f[...], experts, capacity)
    shares_f = route_shares(normed, router[...], hits)
    targets_b, hits = slot_targets(routes_b[...], experts, capacity)
    targets_b = [t + experts * capacity for t in targets_b]
    own_shares = route_shares(normalise(saved[...], gain[...])[2], router[...], hits)
    for k, share in enumerate(own_shares):
        shares_b[k] = jnp.broadcast_to(share, shares_b.shape[1:])
    for part in range(parts):
        there, back = sizes["there"][part], sizes["back"][part]
        mixing_f, mixing_b, tables_b = mixing[3 * part : 3 * part + 3]
        keys = keys_of_part(sizes, place[2], columns, part, back)
        found_f, found_b = tables_of(targets_f, keys), tables_of(targets_b, keys)
        for out, found, shares in ((mixing_f, found_f, shares_f), (mixing_b, found_b, own_shares)):
            mixed = sum(t * s.astype(BF16).astype(F32) for t, s in zip(found, shares))
            out[...] = jnp.transpose(mixed).astype(BF16)
        for k, table in enumerate(found_b):
            tables_b[k] = table
        if part > 0:
            if there != back:
                keys = keys_of_part(sizes, place[2], columns, part, there)
                found_f, found_b = tables_of(targets_f, keys), tables_of(targets_b, keys)
            blocks = sizes["sources"] if there else 1
            table = jnp.concatenate([sum(found_f), sum(found_b)], axis=1).astype(BF16)
            parted(dot(table, data), sends[:blocks])
            sends = sends[blocks:]


def expert_kernel(
    sizes, part, held, place, columns, lanes, wanted, wanted_lanes, saved_pre, up, down, *refs
):
    there, back = sizes["there"][part], sizes["back"][part]
    blocks = sizes["sources"] if there else 1
    got, out = refs[:blocks], refs[blocks:-5]
    rows, results, up_held, down_held, sems = refs[-5:]
    width = rows.shape[1]
    slots, halves = sems.shape[:2]
    half = up.shape[2] // halves
    padded, block_rows = sizes["padded"], sizes["block_rows"]
    source = (sizes["sources"], -1)

    def copies(expert, piece):
        slot = lax.rem(expert, slots)
        piece_of = pl.ds(piece * half, half)
        return [
            pltpu.make_async_copy(
                up.at[part * held + expert, :, piece_of],
                up_held.at[slot, :, piece_of],
                sems.at[slot, piece, 0],
            ),
            pltpu.make_async_copy(
                down.at[part * held + expert, piece_of, :],
                down_held.at[slot, piece_of, :],
                sems.at[slot, piece, 1],
            ),
        ]

    for expert in range(min(slots, held)):
        for piece in range(halves):
            for copy in copies(jnp.int32(expert), piece):
                copy.start()

    have = partners(place[2], lanes[0:1, :], *source, there) * block_rows + lanes[1:2, :]
    order = (wanted[...] == have).astype(F32).astype(BF16)
    rows[...] = dot(order, joined(got)).astype(BF16)
    results[:, width:] = jnp.zeros((results.shape[0], results.shape[1] - width), BF16)

    def one_expert(expert, carry):
        slot = lax.rem(expert, slots)
        own_f = pl.ds(pl.multiple_of(expert * padded, ROWS), padded)
        own_b = pl.ds(pl.multiple_of((held + expert) * padded, ROWS), padded)
        hidden, pre_grad, inner = [], [], 0.0
        for piece in range(halves):
            for copy in copies(expert, piece):
                copy.wait()
            span = slice(piece * half, (piece + 1) * half)
            pre_act = dot(rows[own_f, :], up_held[slot, :, span])
            hidden_grad = dot(rows[own_b, :], down_held[slot, span, :], NT)
            hidden.append((pre_act / (1.0 + jnp.exp(-pre_act))).astype(BF16))
            pre = saved_pre[part * held + expert, :, span].astype(F32)
            gate = 1.0 / (1.0 + jnp.exp(-pre))
            inner += jnp.sum(
                hidden_grad * (pre * gate).astype(BF16).astype(F32), axis=1, keepdims=True
            )
            pre_grad.append((hidden_grad * gate * (1.0 + pre * (1.0 - gate))).astype(BF16))
        result_f = dot(jnp.concatenate(hidden, axis=1), down_held[slot])
        result_b = dot(jnp.concatenate(pre_grad, axis=1), up_held[slot], NT)
        results[own_f, :width] = result_f.astype(BF16)
        results[own_b, :width] = result_b.astype(BF16)
        results[own_b, width:] = jnp.broadcast_to(inner, (padded, LANES)).astype(BF16)

        @pl.when(expert + slots < held)
        def _():
            for piece in range(halves):
                for copy in copies(expert + slots, piece):
                    copy.start()

        return carry

    lax.fori_loop(0, held, one_expert, 0)
    have = partners(place[2], columns[:, 0:1], *source, back) * block_rows + columns[:, 1:2]
    order = (have == wanted_lanes[...]).astype(F32).astype(BF16)
    parted(dot(order, results[...]), out)


def add_up(blocks, mixing_f, mixing_b, tables):
    back = joined(blocks)
    width = back.shape[1] - LANES
    sums = back[:, width:].astype(F32)[:, :1]
    return (
        dot(mixing_f[...], back[:, :width]),
        dot(mixing_b[...], back[:, :width]),
        [jnp.sum(tables[k] * sums, axis=0, keepdims=True) for k in range(tables.shape[0])],
    )


def early_kernel(sizes, tokens, *refs):
    *refs, output, gradient, inner = refs
    sum_f, sum_b, sums = tokens[...].astype(F32), None, None
    for turned in sizes["back"][:-1]:
        blocks = sizes["sources"] if turned else 1
        more_f, more_b, more = add_up(refs[3 : 3 + blocks], *refs[:3])
        refs = refs[3 + blocks :]
        sum_f += more_f
        sum_b = more_b if sum_b is None else sum_b + more_b
        sums = more if sums is None else [a + b for a, b in zip(sums, more)]
    output[...] = sum_f
    if sums is None:
        gradient[...] = jnp.zeros(gradient.shape, F32)
        inner[...] = jnp.zeros(inner.shape, F32)
    else:
        gradient[...] = sum_b
        for k, row in enumerate(sums):
            inner[k] = jnp.broadcast_to(row, inner.shape[1:])


def late_kernel(
    experts, early_f, early_b, early_inner, saved, upstream, gain, router, routes,
    mixing_f, mixing_b, tables, shares, *refs,
):
    *backs, output, gradient = refs
    more_f, more_b, more = add_up(backs, mixing_f, mixing_b, tables)
    widened = saved[...].astype(F32)
    inv_rms = lax.rsqrt(jnp.mean(widened * widened, axis=-1, keepdims=True) + EPS)
    hits = expert_hits(routes[...], experts)
    top = len(hits)
    share = [shares[k][:1, :] for k in range(top)]
    inner = [early_inner[k][:1, :] + more[k] for k in range(top)]
    mean = sum(share[k] * inner[k] for k in range(top))
    logit_grad = sum(share[k] * (inner[k] - mean) * hits[k] for k in range(top))
    high = logit_grad.astype(BF16)
    rest = logit_grad - high.astype(F32)
    middle = rest.astype(BF16)
    low = (rest - middle.astype(F32)).astype(BF16)
    output[0] = (early_f[...] + more_f).astype(BF16)
    normed_grad = early_b[...] + more_b
    for piece in (high, middle, low):
        normed_grad += dot(piece, router[...], TN)
    gained = normed_grad * gain[...].astype(F32)
    projected = jnp.mean(widened * gained, axis=-1, keepdims=True)
    grad = inv_rms * gained - widened * (inv_rms * inv_rms * inv_rms * projected)
    gradient[0] = (upstream[...].astype(F32) + grad).astype(BF16)


def exchange_order(parts, sources, local, capacity, padded):
    held = local // parts
    slots = sources * local * capacity
    block_rows = 2 * held * capacity
    columns = np.zeros((sources * block_rows, 2 + parts), np.int32)
    wanted = np.full((2 * held * padded, 1), -1, np.int32)
    for source in range(sources):
        for batch in range(2):
            for expert in range(held):
                for slot in range(capacity):
                    within = (batch * held + expert) * capacity + slot
                    row = source * block_rows + within
                    columns[row, :2] = source, within
                    for part in range(parts):
                        own = (part * held + expert) * capacity + slot
                        columns[row, 2 + part] = batch * slots + own
                    wanted[(batch * held + expert) * padded + source * capacity + slot] = row
    return columns, wanted


def on_device(
    forward_sent,
    embedded,
    forward_routes,
    backward_sent,
    loss_gradient,
    saved_inputs,
    backward_routes,
    pre_activation,
    norm_gain,
    router,
    up_weight,
    down_weight,
):
    section = lax.axis_index("section")
    last = lax.axis_size("section") - 1
    sources = lax.axis_size("expert")
    experts = router.shape[2]
    capacity = pre_activation.shape[3]
    local, width, hidden = up_weight.shape
    count = embedded.shape[0]
    top = forward_routes.shape[2]
    slots = experts * capacity
    rows = sources * capacity
    padded = -(-rows // ROWS) * ROWS
    shape = jax.ShapeDtypeStruct
    parts = 2 if local % 2 == 0 else 1
    held = local // parts
    moved = 2 * slots // parts
    few = sources <= 8
    there = [few and part == 0 for part in range(parts)]
    back = [few and part == parts - 1 for part in range(parts)]
    columns, wanted = exchange_order(parts, sources, local, capacity, padded)
    lanes, wanted_lanes = np.ascontiguousarray(columns.T), np.ascontiguousarray(wanted.T)
    sizes = {
        "experts": experts,
        "capacity": capacity,
        "sources": sources,
        "share": local * capacity,
        "there": there,
        "back": back,
        "padded": padded,
        "block_rows": moved // sources,
    }
    place = jnp.stack([section, jnp.full_like(section, last), lax.axis_index("expert")])
    place = place.astype(jnp.int32)

    def blocks_of(turned, columns):
        blocks = sources if turned else 1
        return [shape((moved // blocks, columns), BF16)] * blocks

    later = [block for turned in there[1:] for block in blocks_of(turned, width)]

    router_t = router[0].T
    routes_f, routes_b = forward_routes[0].T, backward_routes[0].T
    arrived_f = from_behind(forward_sent[0], "section", 1)
    arrived_b = from_behind(backward_sent[0], "section", -1)
    inputs = (
        place, arrived_f, arrived_b, embedded, loss_gradient, norm_gain, routes_f, routes_b, columns
    )
    send = call(
        functools.partial(first_send_kernel, sizes),
        tuple(blocks_of(there[0], width)),
        (4 * moved * count * width, 2 * (4 * count + moved) * width),
        in_specs=[SMEM] + [VMEM] * 8,
    )(*inputs)
    tokens, upstream, shares_b, *rest = call(
        functools.partial(mixing_kernel, sizes),
        (
            shape((count, width), BF16),
            shape((count, width), BF16),
            shape((top, 8, count), F32),
            *[
                shape((count, moved), BF16),
                shape((count, moved), BF16),
                shape((top, moved, count), F32),
            ]
            * parts,
            *later,
        ),
        (4 * moved * count * width, 2 * (8 * count + moved) * width),
        in_specs=[SMEM] + [VMEM] * 10,
    )(*inputs, saved_inputs[0], router_t)
    mixing = [rest[3 * part : 3 * part + 3] for part in range(parts)]
    sends = rest[3 * parts :]
    saved_pre = jnp.transpose(pre_activation[0], (1, 0, 2, 3)).reshape(local, rows, hidden)
    saved_pre = jnp.pad(saved_pre, ((0, 0), (0, padded - rows), (0, 0)))
    backs = []
    got = exchange(send, 1)
    for part in range(parts):
        if part + 1 < parts:
            sends, saved_pre, got = lax.optimization_barrier((sends, saved_pre, got))
            blocks = len(blocks_of(there[part + 1], width))
            coming = exchange(sends[:blocks], 1)
            sends = sends[blocks:]
        result = blocks_of(back[part], width + LANES)
        done = call(
            functools.partial(expert_kernel, sizes, part, held),
            tuple(result),
            (8 * held * padded * width * hidden, 4 * held * width * hidden),
            in_specs=[SMEM] + [VMEM] * 5 + [HBM] * 2 + [VMEM] * len(got),
            out_specs=(VMEM,) * len(result),
            scratch_shapes=[
                pltpu.VMEM((2 * held * padded, width), BF16),
                pltpu.VMEM((2 * held * padded, width + LANES), BF16),
                pltpu.VMEM((min(2, held), width, hidden), BF16),
                pltpu.VMEM((min(2, held), hidden, width), BF16),
                pltpu.SemaphoreType.DMA((min(2, held), 2, 2)),
            ],
        )(place, columns, lanes, wanted, wanted_lanes, saved_pre, up_weight, down_weight, *got)
        backs.append(exchange(list(done), -1))
        got = coming if part + 1 < parts else None
    early = call(
        functools.partial(early_kernel, sizes),
        (
            shape((count, width), F32),
            shape((count, width), F32),
            shape((top, 8, count), F32),
        ),
        (4 * moved * count * width, 2 * (5 * count + moved) * width),
    )(tokens, *[ref for part in range(parts - 1) for ref in (*mixing[part], *backs[part])])
    return tuple(
        call(
            functools.partial(late_kernel, experts),
            (shape((1, count, width), BF16),) * 2,
            (4 * moved * count * width, 2 * (8 * count + moved) * width),
        )(
            *early, saved_inputs[0], upstream, norm_gain, router_t, routes_b,
            *mixing[-1], shares_b, *backs[-1],
        )
    )


def solution(mesh):
    return jax.shard_map(
        on_device,
        mesh=mesh,
        in_specs=(
            P("section", "expert", None),
            P("expert", None),
            P("section", "expert", None),
            P("section", "expert", None),
            P("expert", None),
            P("section", "expert", None),
            P("section", "expert", None),
            P("section", None, "expert", None, None),
            P("section", None),
            P("section", None, None),
            P("expert", None, None),
            P("expert", None, None),
        ),
        out_specs=(P("section", "expert", None), P("section", "expert", None)),
        check_vma=False,
    )
```

```python
import functools

import jax
import jax.numpy as jnp
import numpy as np
from jax import lax
from jax.experimental import pallas as pl
from jax.experimental.pallas import tpu as pltpu
from jax.sharding import PartitionSpec as P

EPS = 1e-06
BF16 = jnp.bfloat16
F32 = jnp.float32
LANES = 128
ROWS = 16
SMALL_VMEM = 16 * 1024 * 1024
EXPERT_VMEM = 44 * 1024 * 1024
NT = (((1,), (1,)), ((), ()))
TN = (((0,), (0,)), ((), ()))


def dot(a, b, dims=(((1,), (0,)), ((), ()))):
    return lax.dot_general(a, b, dims, preferred_element_type=F32)


def call(kernel, out_shape, cost, vmem=SMALL_VMEM, **kwargs):
    flops, moved = cost
    return pl.pallas_call(
        kernel,
        out_shape=out_shape,
        compiler_params=pltpu.CompilerParams(vmem_limit_bytes=vmem),
        cost_estimate=pl.CostEstimate(flops=flops, bytes_accessed=moved, transcendentals=0),
        **kwargs,
    )


SMEM = pl.BlockSpec(memory_space=pltpu.SMEM)
VMEM = pl.BlockSpec(memory_space=pltpu.VMEM)
HBM = pl.BlockSpec(memory_space=pl.ANY)


def from_behind(block, axis, distance):
    devices = range(lax.axis_size(axis))
    route = [(i - distance, i) for i in devices if i - distance in devices]
    return lax.ppermute(block, axis, route)


def exchange(blocks, direction):
    size = lax.axis_size("expert")
    if len(blocks) == 1:
        return [lax.all_to_all(blocks[0], "expert", split_axis=0, concat_axis=0, tiled=True)]
    got = list(blocks)
    for d in sorted(range(1, size), key=lambda d: abs(2 * d - size)):
        route = [(i, (i + direction * d) % size) for i in range(size)]
        got[d] = lax.ppermute(blocks[d], "expert", route)
    return got


def joined(refs):
    if len(refs) == 1:
        return refs[0][...]
    return jnp.concatenate([ref[...].astype(F32) for ref in refs], axis=0).astype(BF16)


def parted(value, refs):
    share = value.shape[0] // len(refs)
    for d, ref in enumerate(refs):
        ref[...] = value[d * share : (d + 1) * share].astype(BF16)


def partners(me, distance, sources, direction, turned):
    if not turned:
        return distance
    device = me + direction * distance
    return jnp.where(device < 0, device + sources, jnp.where(device >= sources, device - sources, device))


def expert_hits(routes, experts):
    top, count = routes.shape
    lane = lax.broadcasted_iota(jnp.int32, (experts, count), 0)
    return [(routes[k : k + 1, :] == lane).astype(F32) for k in range(top)]


def slot_targets(routes, experts, capacity):
    top, count = routes.shape
    hits = expert_hits(routes, experts)
    earlier = lax.broadcasted_iota(jnp.int32, (count, count), 0) < lax.broadcasted_iota(
        jnp.int32, (count, count), 1
    )
    before = dot(sum(hits).astype(BF16), earlier.astype(F32).astype(BF16))
    targets = []
    for k in range(top):
        ranked = jnp.sum((before + sum(hits[:k], jnp.zeros_like(before))) * hits[k], 0, keepdims=True)
        targets.append(routes[k : k + 1, :] * capacity + ranked.astype(jnp.int32))
    return targets, hits


def tables_of(targets, row_keys):
    return [(row_keys == target).astype(F32) for target in targets]


def normalise(tokens, gain):
    widened = tokens.astype(F32)
    inv_rms = lax.rsqrt(jnp.mean(widened * widened, axis=-1, keepdims=True) + EPS)
    return widened, inv_rms, (widened * inv_rms * gain.astype(F32)).astype(BF16)


def route_shares(normed, router, hits):
    logits = dot(router, normed, NT)
    exponents = [jnp.exp(jnp.sum(logits * hit, axis=0, keepdims=True)) for hit in hits]
    total = sum(exponents)
    return [exponent / total for exponent in exponents]


def keys_of_part(sizes, me, columns, part, turned):
    device = partners(me, columns[:, 0:1], sizes["sources"], 1, turned)
    return columns[:, 2 + part : 3 + part] + device * sizes["share"]


def rows_to_send(place, arrived_f, arrived_b, embedded, loss, gain):
    tokens = jnp.where(place[0] == 0, embedded[...], arrived_f[...])
    upstream = jnp.where(place[0] == place[1], loss[...], arrived_b[...])
    return tokens, normalise(tokens, gain[...])[2], upstream


def table_kernel(
    sizes, place, embedded, loss, gain, routes_f, routes_b, columns,
    table, embedded_out, loss_out, gain_out,
):
    experts, capacity = sizes["experts"], sizes["capacity"]
    targets_f, _ = slot_targets(routes_f[...], experts, capacity)
    targets_b, _ = slot_targets(routes_b[...], experts, capacity)
    keys = keys_of_part(sizes, place[2], columns, 0, sizes["there"][0])
    table_f = sum(tables_of(targets_f, keys))
    table_b = sum(tables_of([t + experts * capacity for t in targets_b], keys))
    table[...] = jnp.concatenate([table_f, table_b], axis=1).astype(BF16)
    embedded_out[...] = embedded[...]
    loss_out[...] = loss[...]
    gain_out[...] = gain[...]


def first_send_kernel(place, arrived_f, arrived_b, embedded, loss, gain, table, *send):
    _, normed, upstream = rows_to_send(place, arrived_f, arrived_b, embedded, loss, gain)
    parted(dot(table[...], jnp.concatenate([normed, upstream], axis=0)), send)


def mixing_kernel(
    sizes, place, arrived_f, arrived_b, embedded, loss, gain, routes_f, routes_b, columns,
    lanes, wanted, wanted_lanes, saved, router, tokens, upstream, shares_b, *refs,
):
    experts, capacity = sizes["experts"], sizes["capacity"]
    parts = len(sizes["back"])
    mixing, orders, sends = refs[: 3 * parts], refs[3 * parts : 5 * parts], refs[5 * parts :]
    tokens[...], normed, upstream[...] = rows_to_send(
        place, arrived_f, arrived_b, embedded, loss, gain
    )
    data = jnp.concatenate([normed, upstream[...]], axis=0)
    targets_f, hits = slot_targets(routes_f[...], experts, capacity)
    shares_f = route_shares(normed, router[...], hits)
    targets_b, hits = slot_targets(routes_b[...], experts, capacity)
    targets_b = [t + experts * capacity for t in targets_b]
    own_shares = route_shares(normalise(saved[...], gain[...])[2], router[...], hits)
    for k, share in enumerate(own_shares):
        shares_b[k] = jnp.broadcast_to(share, shares_b.shape[1:])
    for part in range(parts):
        there, back = sizes["there"][part], sizes["back"][part]
        mixing_f, mixing_b, tables_b = mixing[3 * part : 3 * part + 3]
        keys = keys_of_part(sizes, place[2], columns, part, back)
        found_f, found_b = tables_of(targets_f, keys), tables_of(targets_b, keys)
        for out, found, shares in ((mixing_f, found_f, shares_f), (mixing_b, found_b, own_shares)):
            mixed = sum(t * s.astype(BF16).astype(F32) for t, s in zip(found, shares))
            out[...] = jnp.transpose(mixed).astype(BF16)
        for k, table in enumerate(found_b):
            tables_b[k] = table
        source = (sizes["sources"], -1)
        have = partners(place[2], lanes[0:1, :], *source, there) * sizes["block_rows"] + lanes[1:2, :]
        orders[2 * part][...] = (wanted[...] == have).astype(F32).astype(BF16)
        have = partners(place[2], columns[:, 0:1], *source, back) * sizes["block_rows"]
        have += columns[:, 1:2]
        orders[2 * part + 1][...] = (have == wanted_lanes[...]).astype(F32).astype(BF16)
        if part > 0:
            if there != back:
                keys = keys_of_part(sizes, place[2], columns, part, there)
                found_f, found_b = tables_of(targets_f, keys), tables_of(targets_b, keys)
            blocks = sizes["sources"] if there else 1
            table = jnp.concatenate([sum(found_f), sum(found_b)], axis=1).astype(BF16)
            parted(dot(table, data), sends[:blocks])
            sends = sends[blocks:]


def expert_kernel(sizes, part, held, order, back_order, saved_pre, up, down, *refs):
    blocks = sizes["sources"] if sizes["there"][part] else 1
    got, out = refs[:blocks], refs[blocks:-5]
    rows, results, up_held, down_held, sems = refs[-5:]
    width = rows.shape[1]
    slots, halves = sems.shape[:2]
    half = up.shape[2] // halves
    padded = sizes["padded"]

    def copies(expert, piece):
        slot = lax.rem(expert, slots)
        piece_of = pl.ds(piece * half, half)
        return [
            pltpu.make_async_copy(
                up.at[part * held + expert, :, piece_of],
                up_held.at[slot, :, piece_of],
                sems.at[slot, piece, 0],
            ),
            pltpu.make_async_copy(
                down.at[part * held + expert, piece_of, :],
                down_held.at[slot, piece_of, :],
                sems.at[slot, piece, 1],
            ),
        ]

    for expert in range(min(slots, held)):
        for piece in range(halves):
            for copy in copies(jnp.int32(expert), piece):
                copy.start()

    rows[...] = dot(order[...], joined(got)).astype(BF16)
    results[:, width:] = jnp.zeros((results.shape[0], results.shape[1] - width), BF16)

    def one_expert(expert, carry):
        slot = lax.rem(expert, slots)
        own_f = pl.ds(pl.multiple_of(expert * padded, ROWS), padded)
        own_b = pl.ds(pl.multiple_of((held + expert) * padded, ROWS), padded)
        hidden, pre_grad, inner = [], [], 0.0
        for piece in range(halves):
            for copy in copies(expert, piece):
                copy.wait()
            span = slice(piece * half, (piece + 1) * half)
            pre_act = dot(rows[own_f, :], up_held[slot, :, span])
            hidden_grad = dot(rows[own_b, :], down_held[slot, span, :], NT)
            hidden.append((pre_act / (1.0 + jnp.exp(-pre_act))).astype(BF16))
            pre = saved_pre[part * held + expert, :, span].astype(F32)
            gate = 1.0 / (1.0 + jnp.exp(-pre))
            inner += jnp.sum(
                hidden_grad * (pre * gate).astype(BF16).astype(F32), axis=1, keepdims=True
            )
            pre_grad.append((hidden_grad * gate * (1.0 + pre * (1.0 - gate))).astype(BF16))
        result_f = dot(jnp.concatenate(hidden, axis=1), down_held[slot])
        result_b = dot(jnp.concatenate(pre_grad, axis=1), up_held[slot], NT)
        results[own_f, :width] = result_f.astype(BF16)
        results[own_b, :width] = result_b.astype(BF16)
        results[own_b, width:] = jnp.broadcast_to(inner, (padded, LANES)).astype(BF16)

        @pl.when(expert + slots < held)
        def _():
            for piece in range(halves):
                for copy in copies(expert + slots, piece):
                    copy.start()

        return carry

    lax.fori_loop(0, held, one_expert, 0)
    parted(dot(back_order[...], results[...]), out)


def add_up(blocks, mixing_f, mixing_b, tables):
    back = joined(blocks)
    width = back.shape[1] - LANES
    sums = back[:, width:].astype(F32)[:, :1]
    return (
        dot(mixing_f[...], back[:, :width]),
        dot(mixing_b[...], back[:, :width]),
        [jnp.sum(tables[k] * sums, axis=0, keepdims=True) for k in range(tables.shape[0])],
    )


def early_kernel(sizes, handed, tokens, *refs):
    output, gradient, inner, *copies = refs[-3 - handed :]
    for given, copied in zip(refs, copies):
        copied[...] = given[...]
    refs = refs[handed : -3 - handed]
    sum_f, sum_b, sums = tokens[...].astype(F32), None, None
    for turned in sizes["back"][:-1]:
        blocks = sizes["sources"] if turned else 1
        more_f, more_b, more = add_up(refs[3 : 3 + blocks], *refs[:3])
        refs = refs[3 + blocks :]
        sum_f += more_f
        sum_b = more_b if sum_b is None else sum_b + more_b
        sums = more if sums is None else [a + b for a, b in zip(sums, more)]
    output[...] = sum_f
    if sums is None:
        gradient[...] = jnp.zeros(gradient.shape, F32)
        inner[...] = jnp.zeros(inner.shape, F32)
    else:
        gradient[...] = sum_b
        for k, row in enumerate(sums):
            inner[k] = jnp.broadcast_to(row, inner.shape[1:])


def late_kernel(
    experts, early_f, early_b, early_inner, saved, upstream, gain, router, routes,
    mixing_f, mixing_b, tables, shares, *refs,
):
    *backs, output, gradient = refs
    more_f, more_b, more = add_up(backs, mixing_f, mixing_b, tables)
    widened = saved[...].astype(F32)
    inv_rms = lax.rsqrt(jnp.mean(widened * widened, axis=-1, keepdims=True) + EPS)
    hits = expert_hits(routes[...], experts)
    top = len(hits)
    share = [shares[k][:1, :] for k in range(top)]
    inner = [early_inner[k][:1, :] + more[k] for k in range(top)]
    mean = sum(share[k] * inner[k] for k in range(top))
    logit_grad = sum(share[k] * (inner[k] - mean) * hits[k] for k in range(top))
    high = logit_grad.astype(BF16)
    rest = logit_grad - high.astype(F32)
    middle = rest.astype(BF16)
    low = (rest - middle.astype(F32)).astype(BF16)
    output[0] = (early_f[...] + more_f).astype(BF16)
    normed_grad = early_b[...] + more_b
    for piece in (high, middle, low):
        normed_grad += dot(piece, router[...], TN)
    gained = normed_grad * gain[...].astype(F32)
    projected = jnp.mean(widened * gained, axis=-1, keepdims=True)
    grad = inv_rms * gained - widened * (inv_rms * inv_rms * inv_rms * projected)
    gradient[0] = (upstream[...].astype(F32) + grad).astype(BF16)


def exchange_order(parts, sources, local, capacity, padded):
    held = local // parts
    slots = sources * local * capacity
    block_rows = 2 * held * capacity
    columns = np.zeros((sources * block_rows, 2 + parts), np.int32)
    wanted = np.full((2 * held * padded, 1), -1, np.int32)
    for source in range(sources):
        for batch in range(2):
            for expert in range(held):
                for slot in range(capacity):
                    within = (batch * held + expert) * capacity + slot
                    row = source * block_rows + within
                    columns[row, :2] = source, within
                    for part in range(parts):
                        own = (part * held + expert) * capacity + slot
                        columns[row, 2 + part] = batch * slots + own
                    wanted[(batch * held + expert) * padded + source * capacity + slot] = row
    return columns, wanted


def on_device(
    forward_sent,
    embedded,
    forward_routes,
    backward_sent,
    loss_gradient,
    saved_inputs,
    backward_routes,
    pre_activation,
    norm_gain,
    router,
    up_weight,
    down_weight,
):
    section = lax.axis_index("section")
    last = lax.axis_size("section") - 1
    sources = lax.axis_size("expert")
    experts = router.shape[2]
    capacity = pre_activation.shape[3]
    local, width, hidden = up_weight.shape
    count = embedded.shape[0]
    top = forward_routes.shape[2]
    slots = experts * capacity
    rows = sources * capacity
    padded = -(-rows // ROWS) * ROWS
    shape = jax.ShapeDtypeStruct
    parts = 2 if local % 2 == 0 else 1
    held = local // parts
    moved = 2 * slots // parts
    few = sources <= 8
    there = [few and part == 0 for part in range(parts)]
    back = [few and part == parts - 1 for part in range(parts)]
    columns, wanted = exchange_order(parts, sources, local, capacity, padded)
    lanes, wanted_lanes = np.ascontiguousarray(columns.T), np.ascontiguousarray(wanted.T)
    sizes = {
        "experts": experts,
        "capacity": capacity,
        "sources": sources,
        "share": local * capacity,
        "there": there,
        "back": back,
        "padded": padded,
        "block_rows": moved // sources,
    }
    place = jnp.stack([section, jnp.full_like(section, last), lax.axis_index("expert")])
    place = place.astype(jnp.int32)

    def blocks_of(turned, columns):
        blocks = sources if turned else 1
        return [shape((moved // blocks, columns), BF16)] * blocks

    later = [block for turned in there[1:] for block in blocks_of(turned, width)]

    router_t = router[0].T
    routes_f, routes_b = forward_routes[0].T, backward_routes[0].T
    arrived_f = from_behind(forward_sent[0], "section", 1)
    arrived_b = from_behind(backward_sent[0], "section", -1)
    row_shape = shape((count, width), BF16)
    table, embedded_held, loss_held, gain_held = call(
        functools.partial(table_kernel, sizes),
        (shape((moved, 2 * count), BF16), row_shape, row_shape, shape((1, width), BF16)),
        (4 * moved * count, 4 * (2 * count + moved) * width),
        in_specs=[SMEM] + [VMEM] * 6,
    )(place, embedded, loss_gradient, norm_gain, routes_f, routes_b, columns)
    given = (place, arrived_f, arrived_b, embedded_held, loss_held, gain_held)
    send = call(
        first_send_kernel,
        tuple(blocks_of(there[0], width)),
        (4 * moved * count * width, 2 * (4 * count + moved) * width),
        in_specs=[SMEM] + [VMEM] * 6,
    )(*given, table)
    mixing_shapes = [
        shape((count, moved), BF16),
        shape((count, moved), BF16),
        shape((top, moved, count), F32),
    ]
    order_shapes = [
        shape((2 * held * padded, moved), BF16),
        shape((moved, 2 * held * padded), BF16),
    ]
    tokens, upstream, shares_b, *rest = call(
        functools.partial(mixing_kernel, sizes),
        (
            row_shape,
            row_shape,
            shape((top, 8, count), F32),
            *mixing_shapes * parts,
            *order_shapes * parts,
            *later,
        ),
        (4 * moved * count * width, 2 * (8 * count + moved) * width),
        in_specs=[SMEM] + [VMEM] * 13,
    )(
        *given, routes_f, routes_b, columns, lanes, wanted, wanted_lanes, saved_inputs[0], router_t
    )
    mixing = [rest[3 * part : 3 * part + 3] for part in range(parts)]
    orders = [rest[3 * parts + 2 * part : 3 * parts + 2 * part + 2] for part in range(parts)]
    sends = rest[5 * parts :]
    saved_pre = jnp.transpose(pre_activation[0], (1, 0, 2, 3)).reshape(local, rows, hidden)
    saved_pre = jnp.pad(saved_pre, ((0, 0), (0, padded - rows), (0, 0)))
    backs = []
    got = exchange(send, 1)
    for part in range(parts):
        if part + 1 < parts:
            sends, saved_pre, got = lax.optimization_barrier((sends, saved_pre, got))
            blocks = len(blocks_of(there[part + 1], width))
            coming = exchange(sends[:blocks], 1)
            sends = sends[blocks:]
        result = blocks_of(back[part], width + LANES)
        done = call(
            functools.partial(expert_kernel, sizes, part, held),
            tuple(result),
            (8 * held * padded * width * hidden, 4 * held * width * hidden),
            vmem=EXPERT_VMEM,
            in_specs=[VMEM] * 3 + [HBM] * 2 + [VMEM] * len(got),
            out_specs=(VMEM,) * len(result),
            scratch_shapes=[
                pltpu.VMEM((2 * held * padded, width), BF16),
                pltpu.VMEM((2 * held * padded, width + LANES), BF16),
                pltpu.VMEM((min(2, held), width, hidden), BF16),
                pltpu.VMEM((min(2, held), hidden, width), BF16),
                pltpu.SemaphoreType.DMA((min(2, held), 2, 2)),
            ],
        )(*orders[part], saved_pre, up_weight, down_weight, *got)
        backs.append(exchange(list(done), -1))
        got = coming if part + 1 < parts else None
    handed = (
        saved_inputs[0], upstream, norm_gain, router_t, routes_b, *mixing[-1], shares_b,
    )
    early = call(
        functools.partial(early_kernel, sizes, len(handed)),
        (
            shape((count, width), F32),
            shape((count, width), F32),
            shape((top, 8, count), F32),
            *[shape(array.shape, array.dtype) for array in handed],
        ),
        (4 * moved * count * width, 2 * (10 * count + moved) * width),
    )(tokens, *handed, *[ref for part in range(parts - 1) for ref in (*mixing[part], *backs[part])])
    return tuple(
        call(
            functools.partial(late_kernel, experts),
            (shape((1, count, width), BF16),) * 2,
            (4 * moved * count * width, 2 * (8 * count + moved) * width),
        )(*early, *backs[-1])
    )


def solution(mesh):
    return jax.shard_map(
        on_device,
        mesh=mesh,
        in_specs=(
            P("section", "expert", None),
            P("expert", None),
            P("section", "expert", None),
            P("section", "expert", None),
            P("expert", None),
            P("section", "expert", None),
            P("section", "expert", None),
            P("section", None, "expert", None, None),
            P("section", None),
            P("section", None, None),
            P("expert", None, None),
            P("expert", None, None),
        ),
        out_specs=(P("section", "expert", None), P("section", "expert", None)),
        check_vma=False,
    )
```

```python
import functools

import jax
import jax.numpy as jnp
import numpy as np
from jax import lax
from jax.experimental import pallas as pl
from jax.experimental.pallas import tpu as pltpu
from jax.sharding import PartitionSpec as P

EPS = 1e-06
BF16 = jnp.bfloat16
F32 = jnp.float32
LANES = 128
ROWS = 16
SMALL_VMEM = 16 * 1024 * 1024
EXPERT_VMEM = 24 * 1024 * 1024
NT = (((1,), (1,)), ((), ()))
TN = (((0,), (0,)), ((), ()))


def dot(a, b, dims=(((1,), (0,)), ((), ()))):
    return lax.dot_general(a, b, dims, preferred_element_type=F32)


def call(kernel, out_shape, cost, vmem=SMALL_VMEM, **kwargs):
    flops, moved = cost
    return pl.pallas_call(
        kernel,
        out_shape=out_shape,
        compiler_params=pltpu.CompilerParams(vmem_limit_bytes=vmem),
        cost_estimate=pl.CostEstimate(flops=flops, bytes_accessed=moved, transcendentals=0),
        **kwargs,
    )


SMEM = pl.BlockSpec(memory_space=pltpu.SMEM)
VMEM = pl.BlockSpec(memory_space=pltpu.VMEM)
HBM = pl.BlockSpec(memory_space=pl.ANY)


def from_behind(block, axis, distance):
    devices = range(lax.axis_size(axis))
    route = [(i - distance, i) for i in devices if i - distance in devices]
    return lax.ppermute(block, axis, route)


def exchange(blocks, direction):
    size = lax.axis_size("expert")
    if len(blocks) == 1:
        return [lax.all_to_all(blocks[0], "expert", split_axis=0, concat_axis=0, tiled=True)]
    got = list(blocks)
    for d in sorted(range(1, size), key=lambda d: abs(2 * d - size)):
        route = [(i, (i + direction * d) % size) for i in range(size)]
        got[d] = lax.ppermute(blocks[d], "expert", route)
    return got


def joined(refs):
    if len(refs) == 1:
        return refs[0][...]
    return jnp.concatenate([ref[...].astype(F32) for ref in refs], axis=0).astype(BF16)


def parted(value, refs):
    share = value.shape[0] // len(refs)
    for d, ref in enumerate(refs):
        ref[...] = value[d * share : (d + 1) * share].astype(BF16)


def partners(me, distance, sources, direction, turned):
    if not turned:
        return distance
    device = me + direction * distance
    return jnp.where(device < 0, device + sources, jnp.where(device >= sources, device - sources, device))


def expert_hits(routes, experts):
    top, count = routes.shape
    lane = lax.broadcasted_iota(jnp.int32, (experts, count), 0)
    return [(routes[k : k + 1, :] == lane).astype(F32) for k in range(top)]


def slot_targets(routes, experts, capacity):
    top, count = routes.shape
    hits = expert_hits(routes, experts)
    earlier = lax.broadcasted_iota(jnp.int32, (count, count), 0) < lax.broadcasted_iota(
        jnp.int32, (count, count), 1
    )
    before = dot(sum(hits).astype(BF16), earlier.astype(F32).astype(BF16))
    targets = []
    for k in range(top):
        ranked = jnp.sum((before + sum(hits[:k], jnp.zeros_like(before))) * hits[k], 0, keepdims=True)
        targets.append(routes[k : k + 1, :] * capacity + ranked.astype(jnp.int32))
    return targets, hits


def tables_of(targets, row_keys):
    return [(row_keys == target).astype(F32) for target in targets]


def normalise(tokens, gain):
    widened = tokens.astype(F32)
    inv_rms = lax.rsqrt(jnp.mean(widened * widened, axis=-1, keepdims=True) + EPS)
    return widened, inv_rms, (widened * inv_rms * gain.astype(F32)).astype(BF16)


def route_shares(normed, router, hits):
    logits = dot(router, normed, NT)
    exponents = [jnp.exp(jnp.sum(logits * hit, axis=0, keepdims=True)) for hit in hits]
    total = sum(exponents)
    return [exponent / total for exponent in exponents]


def keys_of_part(sizes, me, columns, part, turned):
    device = partners(me, columns[:, 0:1], sizes["sources"], 1, turned)
    return columns[:, 2 + part : 3 + part] + device * sizes["share"]


def rows_to_send(place, arrived_f, arrived_b, embedded, loss, gain):
    tokens = jnp.where(place[0] == 0, embedded[...], arrived_f[...])
    upstream = jnp.where(place[0] == place[1], loss[...], arrived_b[...])
    return tokens, normalise(tokens, gain[...])[2], upstream


def table_kernel(
    sizes, place, embedded, loss, gain, routes_f, routes_b, columns,
    table, embedded_out, loss_out, gain_out,
):
    experts, capacity = sizes["experts"], sizes["capacity"]
    targets_f, _ = slot_targets(routes_f[...], experts, capacity)
    targets_b, _ = slot_targets(routes_b[...], experts, capacity)
    keys = keys_of_part(sizes, place[2], columns, 0, sizes["there"][0])
    table_f = sum(tables_of(targets_f, keys))
    table_b = sum(tables_of([t + experts * capacity for t in targets_b], keys))
    table[...] = jnp.concatenate([table_f, table_b], axis=1).astype(BF16)
    embedded_out[...] = embedded[...]
    loss_out[...] = loss[...]
    gain_out[...] = gain[...]


def first_send_kernel(place, arrived_f, arrived_b, embedded, loss, gain, table, *send):
    _, normed, upstream = rows_to_send(place, arrived_f, arrived_b, embedded, loss, gain)
    parted(dot(table[...], jnp.concatenate([normed, upstream], axis=0)), send)


def mixing_kernel(
    sizes, place, arrived_f, arrived_b, embedded, loss, gain, routes_f, routes_b, columns,
    lanes, wanted, wanted_lanes, saved, router, tokens, upstream, shares_b, *refs,
):
    experts, capacity = sizes["experts"], sizes["capacity"]
    parts = len(sizes["back"])
    mixing, orders, sends = refs[: 3 * parts], refs[3 * parts : 5 * parts], refs[5 * parts :]
    tokens[...], normed, upstream[...] = rows_to_send(
        place, arrived_f, arrived_b, embedded, loss, gain
    )
    data = jnp.concatenate([normed, upstream[...]], axis=0)
    targets_f, hits = slot_targets(routes_f[...], experts, capacity)
    shares_f = route_shares(normed, router[...], hits)
    targets_b, hits = slot_targets(routes_b[...], experts, capacity)
    targets_b = [t + experts * capacity for t in targets_b]
    own_shares = route_shares(normalise(saved[...], gain[...])[2], router[...], hits)
    for k, share in enumerate(own_shares):
        shares_b[k] = jnp.broadcast_to(share, shares_b.shape[1:])
    for part in range(parts):
        there, back = sizes["there"][part], sizes["back"][part]
        mixing_f, mixing_b, tables_b = mixing[3 * part : 3 * part + 3]
        keys = keys_of_part(sizes, place[2], columns, part, back)
        found_f, found_b = tables_of(targets_f, keys), tables_of(targets_b, keys)
        for out, found, shares in ((mixing_f, found_f, shares_f), (mixing_b, found_b, own_shares)):
            mixed = sum(t * s.astype(BF16).astype(F32) for t, s in zip(found, shares))
            out[...] = jnp.transpose(mixed).astype(BF16)
        for k, table in enumerate(found_b):
            tables_b[k] = table
        source = (sizes["sources"], -1)
        have = partners(place[2], lanes[0:1, :], *source, there) * sizes["block_rows"] + lanes[1:2, :]
        orders[2 * part][...] = (wanted[...] == have).astype(F32).astype(BF16)
        have = partners(place[2], columns[:, 0:1], *source, back) * sizes["block_rows"]
        have += columns[:, 1:2]
        orders[2 * part + 1][...] = (have == wanted_lanes[...]).astype(F32).astype(BF16)
        if part > 0:
            if there != back:
                keys = keys_of_part(sizes, place[2], columns, part, there)
                found_f, found_b = tables_of(targets_f, keys), tables_of(targets_b, keys)
            blocks = sizes["sources"] if there else 1
            table = jnp.concatenate([sum(found_f), sum(found_b)], axis=1).astype(BF16)
            parted(dot(table, data), sends[:blocks])
            sends = sends[blocks:]


def expert_kernel(sizes, part, held, order, back_order, saved_pre, up, down, *refs):
    blocks = sizes["sources"] if sizes["there"][part] else 1
    got, out = refs[:blocks], refs[blocks:-5]
    rows, results, up_held, down_held, sems = refs[-5:]
    width = rows.shape[1]
    slots, halves = sems.shape[:2]
    half = up.shape[2] // halves
    padded = sizes["padded"]

    def copies(expert, piece):
        slot = lax.rem(expert, slots)
        piece_of = pl.ds(piece * half, half)
        return [
            pltpu.make_async_copy(
                up.at[part * held + expert, :, piece_of],
                up_held.at[slot, :, piece_of],
                sems.at[slot, piece, 0],
            ),
            pltpu.make_async_copy(
                down.at[part * held + expert, piece_of, :],
                down_held.at[slot, piece_of, :],
                sems.at[slot, piece, 1],
            ),
        ]

    for expert in range(min(slots, held)):
        for piece in range(halves):
            for copy in copies(jnp.int32(expert), piece):
                copy.start()

    rows[...] = dot(order[...], joined(got)).astype(BF16)
    results[:, width:] = jnp.zeros((results.shape[0], results.shape[1] - width), BF16)

    def one_expert(expert, carry):
        slot = lax.rem(expert, slots)
        own_f = pl.ds(pl.multiple_of(expert * padded, ROWS), padded)
        own_b = pl.ds(pl.multiple_of((held + expert) * padded, ROWS), padded)
        hidden, pre_grad, inner = [], [], 0.0
        for piece in range(halves):
            for copy in copies(expert, piece):
                copy.wait()
            span = slice(piece * half, (piece + 1) * half)
            pre_act = dot(rows[own_f, :], up_held[slot, :, span])
            hidden_grad = dot(rows[own_b, :], down_held[slot, span, :], NT)
            hidden.append((pre_act / (1.0 + jnp.exp(-pre_act))).astype(BF16))
            pre = saved_pre[part * held + expert, :, span].astype(F32)
            gate = 1.0 / (1.0 + jnp.exp(-pre))
            inner += jnp.sum(
                hidden_grad * (pre * gate).astype(BF16).astype(F32), axis=1, keepdims=True
            )
            pre_grad.append((hidden_grad * gate * (1.0 + pre * (1.0 - gate))).astype(BF16))
        result_f = dot(jnp.concatenate(hidden, axis=1), down_held[slot])
        result_b = dot(jnp.concatenate(pre_grad, axis=1), up_held[slot], NT)
        results[own_f, :width] = result_f.astype(BF16)
        results[own_b, :width] = result_b.astype(BF16)
        results[own_b, width:] = jnp.broadcast_to(inner, (padded, LANES)).astype(BF16)

        @pl.when(expert + slots < held)
        def _():
            for piece in range(halves):
                for copy in copies(expert + slots, piece):
                    copy.start()

        return carry

    lax.fori_loop(0, held, one_expert, 0)
    parted(dot(back_order[...], results[...]), out)


def add_up(blocks, mixing_f, mixing_b, tables):
    back = joined(blocks)
    width = back.shape[1] - LANES
    sums = back[:, width:].astype(F32)[:, :1]
    return (
        dot(mixing_f[...], back[:, :width]),
        dot(mixing_b[...], back[:, :width]),
        [jnp.sum(tables[k] * sums, axis=0, keepdims=True) for k in range(tables.shape[0])],
    )


def early_kernel(sizes, handed, tokens, *refs):
    output, gradient, inner, *copies = refs[-3 - handed :]
    for given, copied in zip(refs, copies):
        copied[...] = given[...]
    refs = refs[handed : -3 - handed]
    sum_f, sum_b, sums = tokens[...].astype(F32), None, None
    for turned in sizes["back"][:-1]:
        blocks = sizes["sources"] if turned else 1
        more_f, more_b, more = add_up(refs[3 : 3 + blocks], *refs[:3])
        refs = refs[3 + blocks :]
        sum_f += more_f
        sum_b = more_b if sum_b is None else sum_b + more_b
        sums = more if sums is None else [a + b for a, b in zip(sums, more)]
    output[...] = sum_f
    if sums is None:
        gradient[...] = jnp.zeros(gradient.shape, F32)
        inner[...] = jnp.zeros(inner.shape, F32)
    else:
        gradient[...] = sum_b
        for k, row in enumerate(sums):
            inner[k] = jnp.broadcast_to(row, inner.shape[1:])


def late_kernel(
    experts, early_f, early_b, early_inner, saved, upstream, gain, router, routes,
    mixing_f, mixing_b, tables, shares, *refs,
):
    *backs, output, gradient = refs
    more_f, more_b, more = add_up(backs, mixing_f, mixing_b, tables)
    widened = saved[...].astype(F32)
    inv_rms = lax.rsqrt(jnp.mean(widened * widened, axis=-1, keepdims=True) + EPS)
    hits = expert_hits(routes[...], experts)
    top = len(hits)
    share = [shares[k][:1, :] for k in range(top)]
    inner = [early_inner[k][:1, :] + more[k] for k in range(top)]
    mean = sum(share[k] * inner[k] for k in range(top))
    logit_grad = sum(share[k] * (inner[k] - mean) * hits[k] for k in range(top))
    high = logit_grad.astype(BF16)
    rest = logit_grad - high.astype(F32)
    middle = rest.astype(BF16)
    low = (rest - middle.astype(F32)).astype(BF16)
    output[0] = (early_f[...] + more_f).astype(BF16)
    normed_grad = early_b[...] + more_b
    for piece in (high, middle, low):
        normed_grad += dot(piece, router[...], TN)
    gained = normed_grad * gain[...].astype(F32)
    projected = jnp.mean(widened * gained, axis=-1, keepdims=True)
    grad = inv_rms * gained - widened * (inv_rms * inv_rms * inv_rms * projected)
    gradient[0] = (upstream[...].astype(F32) + grad).astype(BF16)


def exchange_order(parts, sources, local, capacity, padded):
    held = local // parts
    slots = sources * local * capacity
    block_rows = 2 * held * capacity
    columns = np.zeros((sources * block_rows, 2 + parts), np.int32)
    wanted = np.full((2 * held * padded, 1), -1, np.int32)
    for source in range(sources):
        for batch in range(2):
            for expert in range(held):
                for slot in range(capacity):
                    within = (batch * held + expert) * capacity + slot
                    row = source * block_rows + within
                    columns[row, :2] = source, within
                    for part in range(parts):
                        own = (part * held + expert) * capacity + slot
                        columns[row, 2 + part] = batch * slots + own
                    wanted[(batch * held + expert) * padded + source * capacity + slot] = row
    return columns, wanted


def on_device(
    forward_sent,
    embedded,
    forward_routes,
    backward_sent,
    loss_gradient,
    saved_inputs,
    backward_routes,
    pre_activation,
    norm_gain,
    router,
    up_weight,
    down_weight,
):
    section = lax.axis_index("section")
    last = lax.axis_size("section") - 1
    sources = lax.axis_size("expert")
    experts = router.shape[2]
    capacity = pre_activation.shape[3]
    local, width, hidden = up_weight.shape
    count = embedded.shape[0]
    top = forward_routes.shape[2]
    slots = experts * capacity
    rows = sources * capacity
    padded = -(-rows // ROWS) * ROWS
    shape = jax.ShapeDtypeStruct
    parts = 2 if local % 2 == 0 else 1
    held = local // parts
    moved = 2 * slots // parts
    few = sources <= 8
    there = [few and part == 0 for part in range(parts)]
    back = [few and part == parts - 1 for part in range(parts)]
    columns, wanted = exchange_order(parts, sources, local, capacity, padded)
    lanes, wanted_lanes = np.ascontiguousarray(columns.T), np.ascontiguousarray(wanted.T)
    sizes = {
        "experts": experts,
        "capacity": capacity,
        "sources": sources,
        "share": local * capacity,
        "there": there,
        "back": back,
        "padded": padded,
        "block_rows": moved // sources,
    }
    place = jnp.stack([section, jnp.full_like(section, last), lax.axis_index("expert")])
    place = place.astype(jnp.int32)

    def blocks_of(turned, columns):
        blocks = sources if turned else 1
        return [shape((moved // blocks, columns), BF16)] * blocks

    later = [block for turned in there[1:] for block in blocks_of(turned, width)]

    router_t = router[0].T
    routes_f, routes_b = forward_routes[0].T, backward_routes[0].T
    arrived_f = from_behind(forward_sent[0], "section", 1)
    arrived_b = from_behind(backward_sent[0], "section", -1)
    row_shape = shape((count, width), BF16)
    table, embedded_held, loss_held, gain_held = call(
        functools.partial(table_kernel, sizes),
        (shape((moved, 2 * count), BF16), row_shape, row_shape, shape((1, width), BF16)),
        (4 * moved * count, 4 * (2 * count + moved) * width),
        in_specs=[SMEM] + [VMEM] * 6,
    )(place, embedded, loss_gradient, norm_gain, routes_f, routes_b, columns)
    given = (place, arrived_f, arrived_b, embedded_held, loss_held, gain_held)
    send = call(
        first_send_kernel,
        tuple(blocks_of(there[0], width)),
        (4 * moved * count * width, 2 * (4 * count + moved) * width),
        in_specs=[SMEM] + [VMEM] * 6,
    )(*given, table)
    mixing_shapes = [
        shape((count, moved), BF16),
        shape((count, moved), BF16),
        shape((top, moved, count), F32),
    ]
    order_shapes = [
        shape((2 * held * padded, moved), BF16),
        shape((moved, 2 * held * padded), BF16),
    ]
    tokens, upstream, shares_b, *rest = call(
        functools.partial(mixing_kernel, sizes),
        (
            row_shape,
            row_shape,
            shape((top, 8, count), F32),
            *mixing_shapes * parts,
            *order_shapes * parts,
            *later,
        ),
        (4 * moved * count * width, 2 * (8 * count + moved) * width),
        in_specs=[SMEM] + [VMEM] * 13,
    )(
        *given, routes_f, routes_b, columns, lanes, wanted, wanted_lanes, saved_inputs[0], router_t
    )
    mixing = [rest[3 * part : 3 * part + 3] for part in range(parts)]
    orders = [rest[3 * parts + 2 * part : 3 * parts + 2 * part + 2] for part in range(parts)]
    sends = rest[5 * parts :]
    saved_pre = jnp.transpose(pre_activation[0], (1, 0, 2, 3)).reshape(local, rows, hidden)
    saved_pre = jnp.pad(saved_pre, ((0, 0), (0, padded - rows), (0, 0)))
    backs = []
    got = exchange(send, 1)
    for part in range(parts):
        if part + 1 < parts:
            sends, saved_pre, got = lax.optimization_barrier((sends, saved_pre, got))
            blocks = len(blocks_of(there[part + 1], width))
            coming = exchange(sends[:blocks], 1)
            sends = sends[blocks:]
        result = blocks_of(back[part], width + LANES)
        done = call(
            functools.partial(expert_kernel, sizes, part, held),
            tuple(result),
            (8 * held * padded * width * hidden, 4 * held * width * hidden),
            vmem=EXPERT_VMEM,
            in_specs=[VMEM] * 3 + [HBM] * 2 + [VMEM] * len(got),
            out_specs=(VMEM,) * len(result),
            scratch_shapes=[
                pltpu.VMEM((2 * held * padded, width), BF16),
                pltpu.VMEM((2 * held * padded, width + LANES), BF16),
                pltpu.VMEM((min(2, held), width, hidden), BF16),
                pltpu.VMEM((min(2, held), hidden, width), BF16),
                pltpu.SemaphoreType.DMA((min(2, held), 2, 2)),
            ],
        )(*orders[part], saved_pre, up_weight, down_weight, *got)
        backs.append(exchange(list(done), -1))
        got = coming if part + 1 < parts else None
    handed = (
        saved_inputs[0], upstream, norm_gain, router_t, routes_b, *mixing[-1], shares_b,
    )
    early = call(
        functools.partial(early_kernel, sizes, len(handed)),
        (
            shape((count, width), F32),
            shape((count, width), F32),
            shape((top, 8, count), F32),
            *[shape(array.shape, array.dtype) for array in handed],
        ),
        (4 * moved * count * width, 2 * (10 * count + moved) * width),
    )(tokens, *handed, *[ref for part in range(parts - 1) for ref in (*mixing[part], *backs[part])])
    return tuple(
        call(
            functools.partial(late_kernel, experts),
            (shape((1, count, width), BF16),) * 2,
            (4 * moved * count * width, 2 * (8 * count + moved) * width),
        )(*early, *backs[-1])
    )


def solution(mesh):
    return jax.shard_map(
        on_device,
        mesh=mesh,
        in_specs=(
            P("section", "expert", None),
            P("expert", None),
            P("section", "expert", None),
            P("section", "expert", None),
            P("expert", None),
            P("section", "expert", None),
            P("section", "expert", None),
            P("section", None, "expert", None, None),
            P("section", None),
            P("section", None, None),
            P("expert", None, None),
            P("expert", None, None),
        ),
        out_specs=(P("section", "expert", None), P("section", "expert", None)),
        check_vma=False,
    )
```

```python
import functools

import jax
import jax.numpy as jnp
import numpy as np
from jax import lax
from jax.experimental import pallas as pl
from jax.experimental.pallas import tpu as pltpu
from jax.sharding import PartitionSpec as P

EPS = 1e-06
BF16 = jnp.bfloat16
F32 = jnp.float32
LANES = 128
ROWS = 16
SMALL_VMEM = 16 * 1024 * 1024
EXPERT_VMEM = 28 * 1024 * 1024
LARGE_VMEM = 60 * 1024 * 1024
NT = (((1,), (1,)), ((), ()))
TN = (((0,), (0,)), ((), ()))


def dot(a, b, dims=(((1,), (0,)), ((), ()))):
    return lax.dot_general(a, b, dims, preferred_element_type=F32)


def call(kernel, out_shape, cost, vmem=SMALL_VMEM, **kwargs):
    flops, moved = cost
    return pl.pallas_call(
        kernel,
        out_shape=out_shape,
        compiler_params=pltpu.CompilerParams(vmem_limit_bytes=vmem),
        cost_estimate=pl.CostEstimate(flops=flops, bytes_accessed=moved, transcendentals=0),
        **kwargs,
    )


SMEM = pl.BlockSpec(memory_space=pltpu.SMEM)
VMEM = pl.BlockSpec(memory_space=pltpu.VMEM)
HBM = pl.BlockSpec(memory_space=pl.ANY)


def from_behind(block, axis, distance):
    devices = range(lax.axis_size(axis))
    route = [(i - distance, i) for i in devices if i - distance in devices]
    return lax.ppermute(block, axis, route)


def exchange(blocks, direction):
    size = lax.axis_size("expert")
    if len(blocks) == 1:
        return [lax.all_to_all(blocks[0], "expert", split_axis=0, concat_axis=0, tiled=True)]
    got = list(blocks)
    for d in sorted(range(1, size), key=lambda d: abs(2 * d - size)):
        route = [(i, (i + direction * d) % size) for i in range(size)]
        got[d] = lax.ppermute(blocks[d], "expert", route)
    return got


def joined(refs):
    if len(refs) == 1:
        return refs[0][...]
    blocks = [ref[...].astype(F32) if ref is not None else None for ref in refs]
    empty = jnp.zeros_like(next(block for block in blocks if block is not None))
    return jnp.concatenate([empty if b is None else b for b in blocks], axis=0).astype(BF16)


def parted(value, refs):
    share = value.shape[0] // len(refs)
    for d, ref in enumerate(refs):
        ref[...] = value[d * share : (d + 1) * share].astype(BF16)


def partners(me, distance, sources, direction, turned):
    if not turned:
        return distance
    device = me + direction * distance
    return jnp.where(device < 0, device + sources, jnp.where(device >= sources, device - sources, device))


def expert_hits(routes, experts):
    top, count = routes.shape
    lane = lax.broadcasted_iota(jnp.int32, (experts, count), 0)
    return [(routes[k : k + 1, :] == lane).astype(F32) for k in range(top)]


def slot_targets(routes, experts, capacity):
    top, count = routes.shape
    hits = expert_hits(routes, experts)
    earlier = lax.broadcasted_iota(jnp.int32, (count, count), 0) < lax.broadcasted_iota(
        jnp.int32, (count, count), 1
    )
    before = dot(sum(hits).astype(BF16), earlier.astype(F32).astype(BF16))
    targets = []
    for k in range(top):
        ranked = jnp.sum((before + sum(hits[:k], jnp.zeros_like(before))) * hits[k], 0, keepdims=True)
        targets.append(routes[k : k + 1, :] * capacity + ranked.astype(jnp.int32))
    return targets, hits


def tables_of(targets, row_keys):
    return [(row_keys == target).astype(F32) for target in targets]


def normalise(tokens, gain):
    widened = tokens.astype(F32)
    inv_rms = lax.rsqrt(jnp.mean(widened * widened, axis=-1, keepdims=True) + EPS)
    return widened, inv_rms, (widened * inv_rms * gain.astype(F32)).astype(BF16)


def route_shares(normed, router, hits):
    logits = dot(router, normed, NT)
    exponents = [jnp.exp(jnp.sum(logits * hit, axis=0, keepdims=True)) for hit in hits]
    total = sum(exponents)
    return [exponent / total for exponent in exponents]


def keys_of_part(sizes, me, columns, part, turned):
    device = partners(me, columns[:, 0:1], sizes["sources"], 1, turned)
    return columns[:, 2 + part : 3 + part] + device * sizes["share"]


def rows_to_send(place, arrived_f, arrived_b, embedded, loss, gain):
    tokens = jnp.where(place[0] == 0, embedded[...], arrived_f[...])
    upstream = jnp.where(place[0] == place[1], loss[...], arrived_b[...])
    return tokens, normalise(tokens, gain[...])[2], upstream


def table_kernel(
    sizes, place, embedded, loss, gain, routes_f, routes_b, columns,
    table, embedded_out, loss_out, gain_out,
):
    experts, capacity = sizes["experts"], sizes["capacity"]
    targets_f, _ = slot_targets(routes_f[...], experts, capacity)
    targets_b, _ = slot_targets(routes_b[...], experts, capacity)
    keys = keys_of_part(sizes, place[2], columns, 0, sizes["there"][0])
    table_f = sum(tables_of(targets_f, keys))
    table_b = sum(tables_of([t + experts * capacity for t in targets_b], keys))
    table[...] = jnp.concatenate([table_f, table_b], axis=1).astype(BF16)
    embedded_out[...] = embedded[...]
    loss_out[...] = loss[...]
    gain_out[...] = gain[...]


def first_send_kernel(place, arrived_f, arrived_b, embedded, loss, gain, table, *send):
    _, normed, upstream = rows_to_send(place, arrived_f, arrived_b, embedded, loss, gain)
    parted(dot(table[...], jnp.concatenate([normed, upstream], axis=0)), send)


def mixing_kernel(
    sizes, place, arrived_f, arrived_b, embedded, loss, gain, routes_f, routes_b, columns,
    saved, router, tokens, upstream, shares_b, *refs,
):
    experts, capacity = sizes["experts"], sizes["capacity"]
    parts = len(sizes["back"])
    mixing, sends = refs[: 3 * parts], refs[3 * parts :]
    tokens[...], normed, upstream[...] = rows_to_send(
        place, arrived_f, arrived_b, embedded, loss, gain
    )
    data = jnp.concatenate([normed, upstream[...]], axis=0)
    targets_f, hits = slot_targets(routes_f[...], experts, capacity)
    shares_f = route_shares(normed, router[...], hits)
    targets_b, hits = slot_targets(routes_b[...], experts, capacity)
    targets_b = [t + experts * capacity for t in targets_b]
    own_shares = route_shares(normalise(saved[...], gain[...])[2], router[...], hits)
    for k, share in enumerate(own_shares):
        shares_b[k] = jnp.broadcast_to(share, shares_b.shape[1:])
    for part in range(parts):
        there, back = sizes["there"][part], sizes["back"][part]
        mixing_f, mixing_b, tables_b = mixing[3 * part : 3 * part + 3]
        keys = keys_of_part(sizes, place[2], columns, part, back)
        found_f, found_b = tables_of(targets_f, keys), tables_of(targets_b, keys)
        for out, found, shares in ((mixing_f, found_f, shares_f), (mixing_b, found_b, own_shares)):
            mixed = sum(t * s.astype(BF16).astype(F32) for t, s in zip(found, shares))
            out[...] = jnp.transpose(mixed).astype(BF16)
        for k, table in enumerate(found_b):
            tables_b[k] = table
        if part > 0:
            if there != back:
                keys = keys_of_part(sizes, place[2], columns, part, there)
                found_f, found_b = tables_of(targets_f, keys), tables_of(targets_b, keys)
            blocks = sizes["sources"] if there else 1
            table = jnp.concatenate([sum(found_f), sum(found_b)], axis=1).astype(BF16)
            parted(dot(table, data), sends[:blocks])
            sends = sends[blocks:]


def row_order(sizes, me, turned, shape, axis):
    line = tuple(size if i == axis else 1 for i, size in enumerate(shape))
    row = lax.broadcasted_iota(jnp.int32, line, axis)
    block = sum(
        (row >= k * sizes["block_rows"]).astype(jnp.int32) for k in range(1, sizes["sources"])
    )
    within = row - block * sizes["block_rows"]
    group = sum(
        (within >= k * sizes["capacity"]).astype(jnp.int32)
        for k in range(1, sizes["block_rows"] // sizes["capacity"])
    )
    source = partners(me, block, sizes["sources"], -1, turned)
    place = group * (sizes["padded"] - sizes["capacity"]) + source * sizes["capacity"] + within
    return (place == lax.broadcasted_iota(jnp.int32, shape, 1 - axis)).astype(F32).astype(BF16)


def expert_kernel(sizes, part, held, place, saved_all, up, down, *refs):
    there, back = sizes["there"][part], sizes["back"][part]
    blocks = sizes["sources"] if there else 1
    got, out = refs[:blocks], refs[blocks:-7]
    rows, results, saved_pre, up_held, down_held, saved_sem, sems = refs[-7:]
    moved = blocks * got[0].shape[0]
    width = rows.shape[1]
    slots, halves = sems.shape[:2]
    half = up.shape[2] // halves
    padded = sizes["padded"]

    def copies(expert, piece):
        slot = lax.rem(expert, slots)
        piece_of = pl.ds(piece * half, half)
        return [
            pltpu.make_async_copy(
                up.at[part * held + expert, :, piece_of],
                up_held.at[slot, :, piece_of],
                sems.at[slot, piece, 0],
            ),
            pltpu.make_async_copy(
                down.at[part * held + expert, piece_of, :],
                down_held.at[slot, piece_of, :],
                sems.at[slot, piece, 1],
            ),
        ]

    for expert in range(min(slots, held)):
        for piece in range(halves):
            for copy in copies(jnp.int32(expert), piece):
                copy.start()

        if expert == 0:
            saved_copy = pltpu.make_async_copy(
                saved_all.at[pl.ds(part * held, held)], saved_pre, saved_sem
            )
            saved_copy.start()

    order = row_order(sizes, place[2], there, (rows.shape[0], moved), 1)
    rows[...] = dot(order, joined(got)).astype(BF16)
    results[:, width:] = jnp.zeros((results.shape[0], results.shape[1] - width), BF16)

    saved_copy.wait()

    def one_expert(expert, carry):
        slot = lax.rem(expert, slots)
        own_f = pl.ds(pl.multiple_of(expert * padded, ROWS), padded)
        own_b = pl.ds(pl.multiple_of((held + expert) * padded, ROWS), padded)
        hidden, pre_grad, inner = [], [], 0.0
        for piece in range(halves):
            for copy in copies(expert, piece):
                copy.wait()
            span = slice(piece * half, (piece + 1) * half)
            pre_act = dot(rows[own_f, :], up_held[slot, :, span])
            hidden_grad = dot(rows[own_b, :], down_held[slot, span, :], NT)
            hidden.append((pre_act / (1.0 + jnp.exp(-pre_act))).astype(BF16))
            pre = saved_pre[expert, :, span].astype(F32)
            gate = 1.0 / (1.0 + jnp.exp(-pre))
            inner += jnp.sum(
                hidden_grad * (pre * gate).astype(BF16).astype(F32), axis=1, keepdims=True
            )
            pre_grad.append((hidden_grad * gate * (1.0 + pre * (1.0 - gate))).astype(BF16))
        result_f = dot(jnp.concatenate(hidden, axis=1), down_held[slot])
        result_b = dot(jnp.concatenate(pre_grad, axis=1), up_held[slot], NT)
        results[own_f, :width] = result_f.astype(BF16)
        results[own_b, :width] = result_b.astype(BF16)
        results[own_b, width:] = jnp.broadcast_to(inner, (padded, LANES)).astype(BF16)

        @pl.when(expert + slots < held)
        def _():
            for piece in range(halves):
                for copy in copies(expert + slots, piece):
                    copy.start()

        return carry

    lax.fori_loop(0, held, one_expert, 0)
    order = row_order(sizes, place[2], back, (moved, rows.shape[0]), 0)
    parted(dot(order, results[...]), out)


def add_up(blocks, mixing_f, mixing_b, tables):
    back = joined(blocks)
    width = back.shape[1] - LANES
    sums = back[:, width:].astype(F32)[:, :1]
    return (
        dot(mixing_f[...], back[:, :width]),
        dot(mixing_b[...], back[:, :width]),
        [jnp.sum(tables[k] * sums, axis=0, keepdims=True) for k in range(tables.shape[0])],
    )


def early_kernel(sizes, handed, tokens, *refs):
    output, gradient, inner, *copies = refs[-3 - handed :]
    for given, copied in zip(refs, copies):
        copied[...] = given[...]
    refs = refs[handed : -3 - handed]
    own = None
    if sizes["back"][-1]:
        refs, own = refs[:-4], refs[-4:]
    sum_f, sum_b, sums = tokens[...].astype(F32), None, None
    for turned in sizes["back"][:-1]:
        blocks = sizes["sources"] if turned else 1
        more_f, more_b, more = add_up(refs[3 : 3 + blocks], *refs[:3])
        refs = refs[3 + blocks :]
        sum_f += more_f
        sum_b = more_b if sum_b is None else sum_b + more_b
        sums = more if sums is None else [a + b for a, b in zip(sums, more)]
    if own is not None:
        blocks = [own[3]] + [None] * (sizes["sources"] - 1)
        more_f, more_b, more = add_up(blocks, *own[:3])
        sum_f += more_f
        sum_b = more_b if sum_b is None else sum_b + more_b
        sums = more if sums is None else [a + b for a, b in zip(sums, more)]
    output[...] = sum_f
    if sums is None:
        gradient[...] = jnp.zeros(gradient.shape, F32)
        inner[...] = jnp.zeros(inner.shape, F32)
    else:
        gradient[...] = sum_b
        for k, row in enumerate(sums):
            inner[k] = jnp.broadcast_to(row, inner.shape[1:])


def late_kernel(
    sizes, early_f, early_b, early_inner, saved, upstream, gain, router, routes,
    mixing_f, mixing_b, tables, shares, *refs,
):
    *backs, output, gradient = refs
    if sizes["back"][-1]:
        backs = [None] + backs
    more_f, more_b, more = add_up(backs, mixing_f, mixing_b, tables)
    widened = saved[...].astype(F32)
    inv_rms = lax.rsqrt(jnp.mean(widened * widened, axis=-1, keepdims=True) + EPS)
    hits = expert_hits(routes[...], sizes["experts"])
    top = len(hits)
    share = [shares[k][:1, :] for k in range(top)]
    inner = [early_inner[k][:1, :] + more[k] for k in range(top)]
    mean = sum(share[k] * inner[k] for k in range(top))
    logit_grad = sum(share[k] * (inner[k] - mean) * hits[k] for k in range(top))
    high = logit_grad.astype(BF16)
    rest = logit_grad - high.astype(F32)
    middle = rest.astype(BF16)
    low = (rest - middle.astype(F32)).astype(BF16)
    output[0] = (early_f[...] + more_f).astype(BF16)
    normed_grad = early_b[...] + more_b
    for piece in (high, middle, low):
        normed_grad += dot(piece, router[...], TN)
    gained = normed_grad * gain[...].astype(F32)
    projected = jnp.mean(widened * gained, axis=-1, keepdims=True)
    grad = inv_rms * gained - widened * (inv_rms * inv_rms * inv_rms * projected)
    gradient[0] = (upstream[...].astype(F32) + grad).astype(BF16)


def exchange_columns(parts, sources, local, capacity):
    held = local // parts
    slots = sources * local * capacity
    block_rows = 2 * held * capacity
    columns = np.zeros((sources * block_rows, 2 + parts), np.int32)
    for source in range(sources):
        for batch in range(2):
            for expert in range(held):
                for slot in range(capacity):
                    within = (batch * held + expert) * capacity + slot
                    row = source * block_rows + within
                    columns[row, :2] = source, within
                    for part in range(parts):
                        own = (part * held + expert) * capacity + slot
                        columns[row, 2 + part] = batch * slots + own
    return columns


def on_device(
    forward_sent,
    embedded,
    forward_routes,
    backward_sent,
    loss_gradient,
    saved_inputs,
    backward_routes,
    pre_activation,
    norm_gain,
    router,
    up_weight,
    down_weight,
):
    section = lax.axis_index("section")
    last = lax.axis_size("section") - 1
    sources = lax.axis_size("expert")
    experts = router.shape[2]
    capacity = pre_activation.shape[3]
    local, width, hidden = up_weight.shape
    count = embedded.shape[0]
    top = forward_routes.shape[2]
    slots = experts * capacity
    rows = sources * capacity
    padded = -(-rows // ROWS) * ROWS
    shape = jax.ShapeDtypeStruct
    parts = 2 if local % 2 == 0 else 1
    held = local // parts
    moved = 2 * slots // parts
    few = sources <= 8
    there = [few and part == 0 for part in range(parts)]
    back = [few and part == parts - 1 for part in range(parts)]
    columns = exchange_columns(parts, sources, local, capacity)
    sizes = {
        "experts": experts,
        "capacity": capacity,
        "sources": sources,
        "share": local * capacity,
        "there": there,
        "back": back,
        "padded": padded,
        "block_rows": moved // sources,
    }
    place = jnp.stack([section, jnp.full_like(section, last), lax.axis_index("expert")])
    place = place.astype(jnp.int32)

    def blocks_of(turned, columns):
        blocks = sources if turned else 1
        return [shape((moved // blocks, columns), BF16)] * blocks

    later = [block for turned in there[1:] for block in blocks_of(turned, width)]

    router_t = router[0].T
    routes_f, routes_b = forward_routes[0].T, backward_routes[0].T
    arrived_f = from_behind(forward_sent[0], "section", 1)
    arrived_b = from_behind(backward_sent[0], "section", -1)
    row_shape = shape((count, width), BF16)
    table, embedded_held, loss_held, gain_held = call(
        functools.partial(table_kernel, sizes),
        (shape((moved, 2 * count), BF16), row_shape, row_shape, shape((1, width), BF16)),
        (4 * moved * count, 4 * (2 * count + moved) * width),
        in_specs=[SMEM] + [VMEM] * 6,
    )(place, embedded, loss_gradient, norm_gain, routes_f, routes_b, columns)
    given = (place, arrived_f, arrived_b, embedded_held, loss_held, gain_held)
    send = call(
        first_send_kernel,
        tuple(blocks_of(there[0], width)),
        (4 * moved * count * width, 2 * (4 * count + moved) * width),
        in_specs=[SMEM] + [VMEM] * 6,
    )(*given, table)
    mixing_shapes = [
        shape((count, moved), BF16),
        shape((count, moved), BF16),
        shape((top, moved, count), F32),
    ]
    tokens, upstream, shares_b, *rest = call(
        functools.partial(mixing_kernel, sizes),
        (
            row_shape,
            row_shape,
            shape((top, 8, count), F32),
            *mixing_shapes * parts,
            *later,
        ),
        (4 * moved * count * width, 2 * (8 * count + moved) * width),
        vmem=LARGE_VMEM,
        in_specs=[SMEM] + [VMEM] * 10,
    )(
        place, arrived_f, arrived_b, embedded, loss_gradient, norm_gain, routes_f, routes_b, columns,
        saved_inputs[0], router_t,
    )
    mixing = [rest[3 * part : 3 * part + 3] for part in range(parts)]
    sends = rest[3 * parts :]
    saved_pre = jnp.transpose(pre_activation[0], (1, 0, 2, 3)).reshape(local, rows, hidden)
    saved_pre = jnp.pad(saved_pre, ((0, 0), (0, padded - rows), (0, 0)))
    backs = []
    got = exchange(send, 1)
    for part in range(parts):
        if part + 1 < parts:
            sends, saved_pre, got = lax.optimization_barrier((sends, saved_pre, got))
            blocks = len(blocks_of(there[part + 1], width))
            coming = exchange(sends[:blocks], 1)
            sends = sends[blocks:]
        result = blocks_of(back[part], width + LANES)
        done = call(
            functools.partial(expert_kernel, sizes, part, held),
            tuple(result),
            (8 * held * padded * width * hidden, 4 * held * width * hidden),
            vmem=EXPERT_VMEM,
            in_specs=[SMEM] + [HBM] * 3 + [VMEM] * len(got),
            out_specs=(VMEM,) * len(result),
            scratch_shapes=[
                pltpu.VMEM((2 * held * padded, width), BF16),
                pltpu.VMEM((2 * held * padded, width + LANES), BF16),
                pltpu.VMEM((held, padded, hidden), BF16),
                pltpu.VMEM((min(2, held), width, hidden), BF16),
                pltpu.VMEM((min(2, held), hidden, width), BF16),
                pltpu.SemaphoreType.DMA,
                pltpu.SemaphoreType.DMA((min(2, held), 2, 2)),
            ],
        )(place, saved_pre, up_weight, down_weight, *got)
        backs.append(exchange(list(done), -1))
        got = coming if part + 1 < parts else None
    handed = (
        saved_inputs[0], upstream, norm_gain, router_t, routes_b, *mixing[-1], shares_b,
    )
    own = (*mixing[-1], backs[-1][0]) if back[-1] else ()
    early = call(
        functools.partial(early_kernel, sizes, len(handed)),
        (
            shape((count, width), F32),
            shape((count, width), F32),
            shape((top, 8, count), F32),
            *[shape(array.shape, array.dtype) for array in handed],
        ),
        (4 * moved * count * width, 2 * (10 * count + moved) * width),
    )(tokens, *handed, *[ref for part in range(parts - 1) for ref in (*mixing[part], *backs[part])], *own)
    return tuple(
        call(
            functools.partial(late_kernel, sizes),
            (shape((1, count, width), BF16),) * 2,
            (4 * moved * count * width, 2 * (8 * count + moved) * width),
        )(*early, *(backs[-1][1:] if back[-1] else backs[-1]))
    )


def solution(mesh):
    return jax.shard_map(
        on_device,
        mesh=mesh,
        in_specs=(
            P("section", "expert", None),
            P("expert", None),
            P("section", "expert", None),
            P("section", "expert", None),
            P("expert", None),
            P("section", "expert", None),
            P("section", "expert", None),
            P("section", None, "expert", None, None),
            P("section", None),
            P("section", None, None),
            P("expert", None, None),
            P("expert", None, None),
        ),
        out_specs=(P("section", "expert", None), P("section", "expert", None)),
        check_vma=False,
    )
```

```python
import functools

import jax
import jax.numpy as jnp
import numpy as np
from jax import lax
from jax.experimental import pallas as pl
from jax.experimental.pallas import tpu as pltpu
from jax.sharding import PartitionSpec as P

EPS = 1e-06
BF16 = jnp.bfloat16
F32 = jnp.float32
LANES = 128
ROWS = 16
SMALL_VMEM = 16 * 1024 * 1024
EXPERT_VMEM = 28 * 1024 * 1024
LARGE_VMEM = 60 * 1024 * 1024
NT = (((1,), (1,)), ((), ()))
TN = (((0,), (0,)), ((), ()))


def dot(a, b, dims=(((1,), (0,)), ((), ()))):
    return lax.dot_general(a, b, dims, preferred_element_type=F32)


def call(kernel, out_shape, cost, vmem=SMALL_VMEM, **kwargs):
    flops, moved = cost
    return pl.pallas_call(
        kernel,
        out_shape=out_shape,
        compiler_params=pltpu.CompilerParams(vmem_limit_bytes=vmem),
        cost_estimate=pl.CostEstimate(flops=flops, bytes_accessed=moved, transcendentals=0),
        **kwargs,
    )


SMEM = pl.BlockSpec(memory_space=pltpu.SMEM)
VMEM = pl.BlockSpec(memory_space=pltpu.VMEM)
HBM = pl.BlockSpec(memory_space=pl.ANY)


def from_behind(block, axis, distance):
    devices = range(lax.axis_size(axis))
    route = [(i - distance, i) for i in devices if i - distance in devices]
    return lax.ppermute(block, axis, route)


def exchange(blocks, direction):
    size = lax.axis_size("expert")
    if len(blocks) == 1:
        return [lax.all_to_all(blocks[0], "expert", split_axis=0, concat_axis=0, tiled=True)]
    got = list(blocks)
    for d in sorted(range(1, size), key=lambda d: abs(2 * d - size)):
        route = [(i, (i + direction * d) % size) for i in range(size)]
        got[d] = lax.ppermute(blocks[d], "expert", route)
    return got


def joined(refs):
    if len(refs) == 1:
        return refs[0][...]
    blocks = [ref[...].astype(F32) if ref is not None else None for ref in refs]
    empty = jnp.zeros_like(next(block for block in blocks if block is not None))
    return jnp.concatenate([empty if b is None else b for b in blocks], axis=0).astype(BF16)


def parted(value, refs):
    share = value.shape[0] // len(refs)
    for d, ref in enumerate(refs):
        ref[...] = value[d * share : (d + 1) * share].astype(BF16)


def partners(me, distance, sources, direction, turned):
    if not turned:
        return distance
    device = me + direction * distance
    return jnp.where(device < 0, device + sources, jnp.where(device >= sources, device - sources, device))


def expert_hits(routes, experts):
    top, count = routes.shape
    lane = lax.broadcasted_iota(jnp.int32, (experts, count), 0)
    return [(routes[k : k + 1, :] == lane).astype(F32) for k in range(top)]


def slot_targets(routes, experts, capacity):
    top, count = routes.shape
    hits = expert_hits(routes, experts)
    earlier = lax.broadcasted_iota(jnp.int32, (count, count), 0) < lax.broadcasted_iota(
        jnp.int32, (count, count), 1
    )
    before = dot(sum(hits).astype(BF16), earlier.astype(F32).astype(BF16))
    targets = []
    for k in range(top):
        ranked = jnp.sum((before + sum(hits[:k], jnp.zeros_like(before))) * hits[k], 0, keepdims=True)
        targets.append(routes[k : k + 1, :] * capacity + ranked.astype(jnp.int32))
    return targets, hits


def tables_of(targets, row_keys):
    return [(row_keys == target).astype(F32) for target in targets]


def normalise(tokens, gain):
    widened = tokens.astype(F32)
    inv_rms = lax.rsqrt(jnp.mean(widened * widened, axis=-1, keepdims=True) + EPS)
    return widened, inv_rms, (widened * inv_rms * gain.astype(F32)).astype(BF16)


def route_shares(normed, router, hits):
    logits = dot(router, normed, NT)
    exponents = [jnp.exp(jnp.sum(logits * hit, axis=0, keepdims=True)) for hit in hits]
    total = sum(exponents)
    return [exponent / total for exponent in exponents]


def keys_of_part(sizes, me, columns, part, turned):
    device = partners(me, columns[:, 0:1], sizes["sources"], 1, turned)
    return columns[:, 2 + part : 3 + part] + device * sizes["share"]


def rows_to_send(place, arrived_f, arrived_b, embedded, loss, gain):
    tokens = jnp.where(place[0] == 0, embedded[...], arrived_f[...])
    upstream = jnp.where(place[0] == place[1], loss[...], arrived_b[...])
    return tokens, normalise(tokens, gain[...])[2], upstream


def table_kernel(
    sizes, place, embedded, loss, gain, routes_f, routes_b, columns,
    table, embedded_out, loss_out, gain_out,
):
    experts, capacity = sizes["experts"], sizes["capacity"]
    targets_f, _ = slot_targets(routes_f[...], experts, capacity)
    targets_b, _ = slot_targets(routes_b[...], experts, capacity)
    keys = keys_of_part(sizes, place[2], columns, 0, sizes["there"][0])
    table_f = sum(tables_of(targets_f, keys))
    table_b = sum(tables_of([t + experts * capacity for t in targets_b], keys))
    table[...] = jnp.concatenate([table_f, table_b], axis=1).astype(BF16)
    embedded_out[...] = embedded[...]
    loss_out[...] = loss[...]
    gain_out[...] = gain[...]


def first_send_kernel(place, arrived_f, arrived_b, embedded, loss, gain, table, *send):
    _, normed, upstream = rows_to_send(place, arrived_f, arrived_b, embedded, loss, gain)
    parted(dot(table[...], jnp.concatenate([normed, upstream], axis=0)), send)


def mixing_kernel(
    sizes, place, arrived_f, arrived_b, embedded, loss, gain, routes_f, routes_b, columns,
    saved, router, tokens, upstream, shares_b, *refs,
):
    experts, capacity = sizes["experts"], sizes["capacity"]
    parts = len(sizes["back"])
    mixing, sends = refs[: 3 * parts], refs[3 * parts :]
    tokens[...], normed, upstream[...] = rows_to_send(
        place, arrived_f, arrived_b, embedded, loss, gain
    )
    data = jnp.concatenate([normed, upstream[...]], axis=0)
    targets_f, hits = slot_targets(routes_f[...], experts, capacity)
    shares_f = route_shares(normed, router[...], hits)
    targets_b, hits = slot_targets(routes_b[...], experts, capacity)
    targets_b = [t + experts * capacity for t in targets_b]
    own_shares = route_shares(normalise(saved[...], gain[...])[2], router[...], hits)
    for k, share in enumerate(own_shares):
        shares_b[k] = jnp.broadcast_to(share, shares_b.shape[1:])
    for part in range(parts):
        there, back = sizes["there"][part], sizes["back"][part]
        mixing_f, mixing_b, tables_b = mixing[3 * part : 3 * part + 3]
        keys = keys_of_part(sizes, place[2], columns, part, back)
        found_f, found_b = tables_of(targets_f, keys), tables_of(targets_b, keys)
        for out, found, shares in ((mixing_f, found_f, shares_f), (mixing_b, found_b, own_shares)):
            mixed = sum(t * s.astype(BF16).astype(F32) for t, s in zip(found, shares))
            out[...] = jnp.transpose(mixed).astype(BF16)
        for k, table in enumerate(found_b):
            tables_b[k] = table
        if part > 0:
            if there != back:
                keys = keys_of_part(sizes, place[2], columns, part, there)
                found_f, found_b = tables_of(targets_f, keys), tables_of(targets_b, keys)
            blocks = sizes["sources"] if there else 1
            table = jnp.concatenate([sum(found_f), sum(found_b)], axis=1).astype(BF16)
            parted(dot(table, data), sends[:blocks])
            sends = sends[blocks:]


def row_order(sizes, me, turned, shape, axis):
    line = tuple(size if i == axis else 1 for i, size in enumerate(shape))
    row = lax.broadcasted_iota(jnp.int32, line, axis)
    block = sum(
        (row >= k * sizes["block_rows"]).astype(jnp.int32) for k in range(1, sizes["sources"])
    )
    within = row - block * sizes["block_rows"]
    group = sum(
        (within >= k * sizes["capacity"]).astype(jnp.int32)
        for k in range(1, sizes["block_rows"] // sizes["capacity"])
    )
    source = partners(me, block, sizes["sources"], -1, turned)
    place = group * (sizes["padded"] - sizes["capacity"]) + source * sizes["capacity"] + within
    return (place == lax.broadcasted_iota(jnp.int32, shape, 1 - axis)).astype(F32).astype(BF16)


def expert_kernel(sizes, part, held, place, saved_all, up, down, *refs):
    there, back = sizes["there"][part], sizes["back"][part]
    blocks = sizes["sources"] if there else 1
    got, out = refs[:blocks], refs[blocks:-7]
    rows, results, saved_pre, up_held, down_held, saved_sem, sems = refs[-7:]
    moved = blocks * got[0].shape[0]
    width = rows.shape[1]
    slots, halves = sems.shape[:2]
    half = up.shape[2] // halves
    padded = sizes["padded"]

    def copies(expert, piece):
        slot = lax.rem(expert, slots)
        piece_of = pl.ds(piece * half, half)
        return [
            pltpu.make_async_copy(
                up.at[part * held + expert, :, piece_of],
                up_held.at[slot, :, piece_of],
                sems.at[slot, piece, 0],
            ),
            pltpu.make_async_copy(
                down.at[part * held + expert, piece_of, :],
                down_held.at[slot, piece_of, :],
                sems.at[slot, piece, 1],
            ),
        ]

    for expert in range(min(slots, held)):
        for piece in range(halves):
            for copy in copies(jnp.int32(expert), piece):
                copy.start()

        if expert == 0:
            saved_copy = pltpu.make_async_copy(
                saved_all.at[pl.ds(part * held, held)], saved_pre, saved_sem
            )
            saved_copy.start()

    order = row_order(sizes, place[2], there, (rows.shape[0], moved), 1)
    rows[...] = dot(order, joined(got)).astype(BF16)
    results[:, width:] = jnp.zeros((results.shape[0], results.shape[1] - width), BF16)

    saved_copy.wait()

    def one_expert(expert, carry):
        slot = lax.rem(expert, slots)
        own_f = pl.ds(pl.multiple_of(expert * padded, ROWS), padded)
        own_b = pl.ds(pl.multiple_of((held + expert) * padded, ROWS), padded)
        hidden, pre_grad, inner = [], [], 0.0
        for piece in range(halves):
            for copy in copies(expert, piece):
                copy.wait()
            span = slice(piece * half, (piece + 1) * half)
            pre_act = dot(rows[own_f, :], up_held[slot, :, span])
            hidden_grad = dot(rows[own_b, :], down_held[slot, span, :], NT)
            hidden.append((pre_act / (1.0 + jnp.exp(-pre_act))).astype(BF16))
            pre = saved_pre[expert, :, span].astype(F32)
            gate = 1.0 / (1.0 + jnp.exp(-pre))
            inner += jnp.sum(
                hidden_grad * (pre * gate).astype(BF16).astype(F32), axis=1, keepdims=True
            )
            pre_grad.append((hidden_grad * gate * (1.0 + pre * (1.0 - gate))).astype(BF16))
        result_f = dot(jnp.concatenate(hidden, axis=1), down_held[slot])
        result_b = dot(jnp.concatenate(pre_grad, axis=1), up_held[slot], NT)
        results[own_f, :width] = result_f.astype(BF16)
        results[own_b, :width] = result_b.astype(BF16)
        results[own_b, width:] = jnp.broadcast_to(inner, (padded, LANES)).astype(BF16)

        @pl.when(expert + slots < held)
        def _():
            for piece in range(halves):
                for copy in copies(expert + slots, piece):
                    copy.start()

        return carry

    lax.fori_loop(0, held, one_expert, 0)
    order = row_order(sizes, place[2], back, (moved, rows.shape[0]), 0)
    parted(dot(order, results[...]), out)


def add_up(blocks, mixing_f, mixing_b, tables):
    back = joined(blocks)
    width = back.shape[1] - LANES
    sums = back[:, width:].astype(F32)[:, :1]
    return (
        dot(mixing_f[...], back[:, :width]),
        dot(mixing_b[...], back[:, :width]),
        [jnp.sum(tables[k] * sums, axis=0, keepdims=True) for k in range(tables.shape[0])],
    )


def early_kernel(sizes, handed, tokens, *refs):
    output, gradient, inner, *copies = refs[-3 - handed :]
    for given, copied in zip(refs, copies):
        copied[...] = given[...]
    refs = refs[handed : -3 - handed]
    own = None
    if sizes["back"][-1]:
        refs, own = refs[:-4], refs[-4:]
    sum_f, sum_b, sums = tokens[...].astype(F32), None, None
    for turned in sizes["back"][:-1]:
        blocks = sizes["sources"] if turned else 1
        more_f, more_b, more = add_up(refs[3 : 3 + blocks], *refs[:3])
        refs = refs[3 + blocks :]
        sum_f += more_f
        sum_b = more_b if sum_b is None else sum_b + more_b
        sums = more if sums is None else [a + b for a, b in zip(sums, more)]
    if own is not None:
        blocks = [own[3]] + [None] * (sizes["sources"] - 1)
        more_f, more_b, more = add_up(blocks, *own[:3])
        sum_f += more_f
        sum_b = more_b if sum_b is None else sum_b + more_b
        sums = more if sums is None else [a + b for a, b in zip(sums, more)]
    output[...] = sum_f
    if sums is None:
        gradient[...] = jnp.zeros(gradient.shape, F32)
        inner[...] = jnp.zeros(inner.shape, F32)
    else:
        gradient[...] = sum_b
        for k, row in enumerate(sums):
            inner[k] = jnp.broadcast_to(row, inner.shape[1:])


def late_kernel(
    sizes, early_f, early_b, early_inner, saved, upstream, gain, router, routes,
    mixing_f, mixing_b, tables, shares, *refs,
):
    *backs, output, gradient = refs
    if sizes["back"][-1]:
        backs = [None] + backs
    more_f, more_b, more = add_up(backs, mixing_f, mixing_b, tables)
    widened = saved[...].astype(F32)
    inv_rms = lax.rsqrt(jnp.mean(widened * widened, axis=-1, keepdims=True) + EPS)
    hits = expert_hits(routes[...], sizes["experts"])
    top = len(hits)
    share = [shares[k][:1, :] for k in range(top)]
    inner = [early_inner[k][:1, :] + more[k] for k in range(top)]
    mean = sum(share[k] * inner[k] for k in range(top))
    logit_grad = sum(share[k] * (inner[k] - mean) * hits[k] for k in range(top))
    high = logit_grad.astype(BF16)
    rest = logit_grad - high.astype(F32)
    middle = rest.astype(BF16)
    low = (rest - middle.astype(F32)).astype(BF16)
    output[0] = (early_f[...] + more_f).astype(BF16)
    normed_grad = early_b[...] + more_b
    for piece in (high, middle, low):
        normed_grad += dot(piece, router[...], TN)
    gained = normed_grad * gain[...].astype(F32)
    projected = jnp.mean(widened * gained, axis=-1, keepdims=True)
    grad = inv_rms * gained - widened * (inv_rms * inv_rms * inv_rms * projected)
    gradient[0] = (upstream[...].astype(F32) + grad).astype(BF16)


def exchange_columns(parts, sources, local, capacity):
    held = local // parts
    slots = sources * local * capacity
    block_rows = 2 * held * capacity
    columns = np.zeros((sources * block_rows, 2 + parts), np.int32)
    for source in range(sources):
        for batch in range(2):
            for expert in range(held):
                for slot in range(capacity):
                    within = (batch * held + expert) * capacity + slot
                    row = source * block_rows + within
                    columns[row, :2] = source, within
                    for part in range(parts):
                        own = (part * held + expert) * capacity + slot
                        columns[row, 2 + part] = batch * slots + own
    return columns


def on_device(
    forward_sent,
    embedded,
    forward_routes,
    backward_sent,
    loss_gradient,
    saved_inputs,
    backward_routes,
    pre_activation,
    norm_gain,
    router,
    up_weight,
    down_weight,
):
    section = lax.axis_index("section")
    last = lax.axis_size("section") - 1
    sources = lax.axis_size("expert")
    experts = router.shape[2]
    capacity = pre_activation.shape[3]
    local, width, hidden = up_weight.shape
    count = embedded.shape[0]
    top = forward_routes.shape[2]
    slots = experts * capacity
    rows = sources * capacity
    padded = -(-rows // ROWS) * ROWS
    shape = jax.ShapeDtypeStruct
    parts = 2 if local % 2 == 0 else 1
    held = local // parts
    moved = 2 * slots // parts
    few = sources <= 8
    there = [few and part == 0 for part in range(parts)]
    back = [few and part == parts - 1 for part in range(parts)]
    columns = exchange_columns(parts, sources, local, capacity)
    sizes = {
        "experts": experts,
        "capacity": capacity,
        "sources": sources,
        "share": local * capacity,
        "there": there,
        "back": back,
        "padded": padded,
        "block_rows": moved // sources,
    }
    place = jnp.stack([section, jnp.full_like(section, last), lax.axis_index("expert")])
    place = place.astype(jnp.int32)

    def blocks_of(turned, columns):
        blocks = sources if turned else 1
        return [shape((moved // blocks, columns), BF16)] * blocks

    later = [block for turned in there[1:] for block in blocks_of(turned, width)]

    router_t = router[0].T
    routes_f, routes_b = forward_routes[0].T, backward_routes[0].T
    arrived_f = from_behind(forward_sent[0], "section", 1)
    arrived_b = from_behind(backward_sent[0], "section", -1)
    row_shape = shape((count, width), BF16)
    table, embedded_held, loss_held, gain_held = call(
        functools.partial(table_kernel, sizes),
        (shape((moved, 2 * count), BF16), row_shape, row_shape, shape((1, width), BF16)),
        (4 * moved * count, 4 * (2 * count + moved) * width),
        in_specs=[SMEM] + [VMEM] * 6,
    )(place, embedded, loss_gradient, norm_gain, routes_f, routes_b, columns)
    given = (place, arrived_f, arrived_b, embedded_held, loss_held, gain_held)
    send = call(
        first_send_kernel,
        tuple(blocks_of(there[0], width)),
        (4 * moved * count * width, 2 * (4 * count + moved) * width),
        in_specs=[SMEM] + [VMEM] * 6,
    )(*given, table)
    mixing_shapes = [
        shape((count, moved), BF16),
        shape((count, moved), BF16),
        shape((top, moved, count), F32),
    ]
    tokens, upstream, shares_b, *rest = call(
        functools.partial(mixing_kernel, sizes),
        (
            row_shape,
            row_shape,
            shape((top, 8, count), F32),
            *mixing_shapes * parts,
            *later,
        ),
        (4 * moved * count * width, 2 * (8 * count + moved) * width),
        vmem=LARGE_VMEM,
        in_specs=[SMEM] + [VMEM] * 10,
    )(
        place, arrived_f, arrived_b, embedded, loss_gradient, norm_gain, routes_f, routes_b, columns,
        saved_inputs[0], router_t,
    )
    mixing = [rest[3 * part : 3 * part + 3] for part in range(parts)]
    sends = rest[3 * parts :]
    saved_pre = jnp.transpose(pre_activation[0], (1, 0, 2, 3)).reshape(local, rows, hidden)
    saved_pre = jnp.pad(saved_pre, ((0, 0), (0, padded - rows), (0, 0)))
    backs = []
    got = exchange(send, 1)
    for part in range(parts):
        if part + 1 < parts:
            near = got[1 : len(got) // 2] if there[part] else got
            sends, saved_pre, near = lax.optimization_barrier((sends, saved_pre, near))
            if there[part]:
                got[1 : len(got) // 2] = near
            else:
                got = near
            blocks = len(blocks_of(there[part + 1], width))
            coming = exchange(sends[:blocks], 1)
            sends = sends[blocks:]
        result = blocks_of(back[part], width + LANES)
        done = call(
            functools.partial(expert_kernel, sizes, part, held),
            tuple(result),
            (8 * held * padded * width * hidden, 4 * held * width * hidden),
            vmem=EXPERT_VMEM,
            in_specs=[SMEM] + [HBM] * 3 + [VMEM] * len(got),
            out_specs=(VMEM,) * len(result),
            scratch_shapes=[
                pltpu.VMEM((2 * held * padded, width), BF16),
                pltpu.VMEM((2 * held * padded, width + LANES), BF16),
                pltpu.VMEM((held, padded, hidden), BF16),
                pltpu.VMEM((min(2, held), width, hidden), BF16),
                pltpu.VMEM((min(2, held), hidden, width), BF16),
                pltpu.SemaphoreType.DMA,
                pltpu.SemaphoreType.DMA((min(2, held), 2, 2)),
            ],
        )(place, saved_pre, up_weight, down_weight, *got)
        backs.append(exchange(list(done), -1))
        got = coming if part + 1 < parts else None
    handed = (
        saved_inputs[0], upstream, norm_gain, router_t, routes_b, *mixing[-1], shares_b,
    )
    own = (*mixing[-1], backs[-1][0]) if back[-1] else ()
    early = call(
        functools.partial(early_kernel, sizes, len(handed)),
        (
            shape((count, width), F32),
            shape((count, width), F32),
            shape((top, 8, count), F32),
            *[shape(array.shape, array.dtype) for array in handed],
        ),
        (4 * moved * count * width, 2 * (10 * count + moved) * width),
    )(tokens, *handed, *[ref for part in range(parts - 1) for ref in (*mixing[part], *backs[part])], *own)
    return tuple(
        call(
            functools.partial(late_kernel, sizes),
            (shape((1, count, width), BF16),) * 2,
            (4 * moved * count * width, 2 * (8 * count + moved) * width),
        )(*early, *(backs[-1][1:] if back[-1] else backs[-1]))
    )


def solution(mesh):
    return jax.shard_map(
        on_device,
        mesh=mesh,
        in_specs=(
            P("section", "expert", None),
            P("expert", None),
            P("section", "expert", None),
            P("section", "expert", None),
            P("expert", None),
            P("section", "expert", None),
            P("section", "expert", None),
            P("section", None, "expert", None, None),
            P("section", None),
            P("section", None, None),
            P("expert", None, None),
            P("expert", None, None),
        ),
        out_specs=(P("section", "expert", None), P("section", "expert", None)),
        check_vma=False,
    )
```

```python
import functools

import jax
import jax.numpy as jnp
import numpy as np
from jax import lax
from jax.experimental import pallas as pl
from jax.experimental.pallas import tpu as pltpu
from jax.sharding import PartitionSpec as P

EPS = 1e-06
BF16 = jnp.bfloat16
F32 = jnp.float32
LANES = 128
ROWS = 16
SMALL_VMEM = 16 * 1024 * 1024
EXPERT_VMEM = 28 * 1024 * 1024
LARGE_VMEM = 60 * 1024 * 1024
NT = (((1,), (1,)), ((), ()))
TN = (((0,), (0,)), ((), ()))


def dot(a, b, dims=(((1,), (0,)), ((), ()))):
    return lax.dot_general(a, b, dims, preferred_element_type=F32)


def call(kernel, out_shape, cost, vmem=SMALL_VMEM, **kwargs):
    flops, moved = cost
    return pl.pallas_call(
        kernel,
        out_shape=out_shape,
        compiler_params=pltpu.CompilerParams(vmem_limit_bytes=vmem),
        cost_estimate=pl.CostEstimate(flops=flops, bytes_accessed=moved, transcendentals=0),
        **kwargs,
    )


VMEM = pl.BlockSpec(memory_space=pltpu.VMEM)
HBM = pl.BlockSpec(memory_space=pl.ANY)


def from_behind(block, axis, distance):
    devices = range(lax.axis_size(axis))
    route = [(i - distance, i) for i in devices if i - distance in devices]
    return lax.ppermute(block, axis, route)


def exchange(blocks, direction):
    size = lax.axis_size("expert")
    if len(blocks) == 1:
        return [lax.all_to_all(blocks[0], "expert", split_axis=0, concat_axis=0, tiled=True)]
    got = list(blocks)
    for d in sorted(range(1, size), key=lambda d: abs(2 * d - size)):
        route = [(i, (i + direction * d) % size) for i in range(size)]
        got[d] = lax.ppermute(blocks[d], "expert", route)
    return got


def joined(refs):
    if len(refs) == 1:
        return refs[0][...]
    blocks = [ref[...].astype(F32) if ref is not None else None for ref in refs]
    empty = jnp.zeros_like(next(block for block in blocks if block is not None))
    return jnp.concatenate([empty if b is None else b for b in blocks], axis=0).astype(BF16)


def parted(value, refs):
    share = value.shape[0] // len(refs)
    for d, ref in enumerate(refs):
        ref[...] = value[d * share : (d + 1) * share].astype(BF16)


def partners(distance, sources, direction, turned):
    if not turned:
        return distance
    device = lax.axis_index("expert") + direction * distance
    return jnp.where(device < 0, device + sources, jnp.where(device >= sources, device - sources, device))


def expert_hits(routes, experts):
    top, count = routes.shape
    lane = lax.broadcasted_iota(jnp.int32, (experts, count), 0)
    return [(routes[k : k + 1, :] == lane).astype(F32) for k in range(top)]


def slot_targets(routes, experts, capacity):
    top, count = routes.shape
    hits = expert_hits(routes, experts)
    earlier = lax.broadcasted_iota(jnp.int32, (count, count), 0) < lax.broadcasted_iota(
        jnp.int32, (count, count), 1
    )
    before = dot(sum(hits).astype(BF16), earlier.astype(F32).astype(BF16))
    targets = []
    for k in range(top):
        ranked = jnp.sum((before + sum(hits[:k], jnp.zeros_like(before))) * hits[k], 0, keepdims=True)
        targets.append(routes[k : k + 1, :] * capacity + ranked.astype(jnp.int32))
    return targets, hits


def tables_of(targets, row_keys):
    return [(row_keys == target).astype(F32) for target in targets]


def normalise(tokens, gain):
    widened = tokens.astype(F32)
    inv_rms = lax.rsqrt(jnp.mean(widened * widened, axis=-1, keepdims=True) + EPS)
    return widened, inv_rms, (widened * inv_rms * gain.astype(F32)).astype(BF16)


def route_shares(normed, router, hits):
    logits = dot(router, normed, NT)
    exponents = [jnp.exp(jnp.sum(logits * hit, axis=0, keepdims=True)) for hit in hits]
    total = sum(exponents)
    return [exponent / total for exponent in exponents]


def keys_of_part(sizes, columns, part, turned):
    device = partners(columns[:, 0:1], sizes["sources"], 1, turned)
    return columns[:, 2 + part : 3 + part] + device * sizes["share"]


def rows_to_send(arrived_f, arrived_b, embedded, loss, gain):
    section = lax.axis_index("section")
    last = lax.axis_size("section") - 1
    tokens = jnp.where(section == 0, embedded[...], arrived_f[...])
    upstream = jnp.where(section == last, loss[...], arrived_b[...])
    return tokens, normalise(tokens, gain[...])[2], upstream


def table_kernel(
    sizes, embedded, loss, gain, routes_f, routes_b, columns,
    table, embedded_out, loss_out, gain_out,
):
    experts, capacity = sizes["experts"], sizes["capacity"]
    targets_f, _ = slot_targets(routes_f[...], experts, capacity)
    targets_b, _ = slot_targets(routes_b[...], experts, capacity)
    keys = keys_of_part(sizes, columns, 0, sizes["there"][0])
    table_f = sum(tables_of(targets_f, keys))
    table_b = sum(tables_of([t + experts * capacity for t in targets_b], keys))
    table[...] = jnp.concatenate([table_f, table_b], axis=1).astype(BF16)
    embedded_out[...] = embedded[...]
    loss_out[...] = loss[...]
    gain_out[...] = gain[...]


def first_send_kernel(arrived_f, arrived_b, embedded, loss, gain, table, *send):
    _, normed, upstream = rows_to_send(arrived_f, arrived_b, embedded, loss, gain)
    parted(dot(table[...], jnp.concatenate([normed, upstream], axis=0)), send)


def mixing_kernel(
    sizes, arrived_f, arrived_b, embedded, loss, gain, routes_f, routes_b, columns,
    saved, router, tokens, upstream, shares_b, *refs,
):
    experts, capacity = sizes["experts"], sizes["capacity"]
    parts = len(sizes["back"])
    mixing, sends = refs[: 3 * parts], refs[3 * parts :]
    tokens[...], normed, upstream[...] = rows_to_send(
        arrived_f, arrived_b, embedded, loss, gain
    )
    data = jnp.concatenate([normed, upstream[...]], axis=0)
    targets_f, hits = slot_targets(routes_f[...], experts, capacity)
    shares_f = route_shares(normed, router[...], hits)
    targets_b, hits = slot_targets(routes_b[...], experts, capacity)
    targets_b = [t + experts * capacity for t in targets_b]
    own_shares = route_shares(normalise(saved[...], gain[...])[2], router[...], hits)
    for k, share in enumerate(own_shares):
        shares_b[k] = jnp.broadcast_to(share, shares_b.shape[1:])
    for part in range(parts):
        there, back = sizes["there"][part], sizes["back"][part]
        mixing_f, mixing_b, tables_b = mixing[3 * part : 3 * part + 3]
        keys = keys_of_part(sizes, columns, part, back)
        found_f, found_b = tables_of(targets_f, keys), tables_of(targets_b, keys)
        for out, found, shares in ((mixing_f, found_f, shares_f), (mixing_b, found_b, own_shares)):
            mixed = sum(t * s.astype(BF16).astype(F32) for t, s in zip(found, shares))
            out[...] = jnp.transpose(mixed).astype(BF16)
        for k, table in enumerate(found_b):
            tables_b[k] = table.astype(BF16)
        if part > 0:
            if there != back:
                keys = keys_of_part(sizes, columns, part, there)
                found_f, found_b = tables_of(targets_f, keys), tables_of(targets_b, keys)
            blocks = sizes["sources"] if there else 1
            table = jnp.concatenate([sum(found_f), sum(found_b)], axis=1).astype(BF16)
            parted(dot(table, data), sends[:blocks])
            sends = sends[blocks:]


def row_order(sizes, turned, shape, axis):
    line = tuple(size if i == axis else 1 for i, size in enumerate(shape))
    row = lax.broadcasted_iota(jnp.int32, line, axis)
    block = sum(
        (row >= k * sizes["block_rows"]).astype(jnp.int32) for k in range(1, sizes["sources"])
    )
    within = row - block * sizes["block_rows"]
    group = sum(
        (within >= k * sizes["capacity"]).astype(jnp.int32)
        for k in range(1, sizes["block_rows"] // sizes["capacity"])
    )
    source = partners(block, sizes["sources"], -1, turned)
    place = group * (sizes["padded"] - sizes["capacity"]) + source * sizes["capacity"] + within
    return (place == lax.broadcasted_iota(jnp.int32, shape, 1 - axis)).astype(F32).astype(BF16)


def expert_kernel(sizes, part, held, saved_all, up, down, *refs):
    there, back = sizes["there"][part], sizes["back"][part]
    blocks = sizes["sources"] if there else 1
    got, out = refs[:blocks], refs[blocks:-7]
    rows, results, saved_pre, up_held, down_held, saved_sem, sems = refs[-7:]
    moved = blocks * got[0].shape[0]
    width = rows.shape[1]
    slots, halves = sems.shape[:2]
    half = up.shape[2] // halves
    padded = sizes["padded"]

    def copies(expert, piece):
        slot = lax.rem(expert, slots)
        piece_of = pl.ds(piece * half, half)
        return [
            pltpu.make_async_copy(
                up.at[part * held + expert, :, piece_of],
                up_held.at[slot, :, piece_of],
                sems.at[slot, piece, 0],
            ),
            pltpu.make_async_copy(
                down.at[part * held + expert, piece_of, :],
                down_held.at[slot, piece_of, :],
                sems.at[slot, piece, 1],
            ),
        ]

    for expert in range(min(slots, held)):
        for piece in range(halves):
            for copy in copies(jnp.int32(expert), piece):
                copy.start()

        if expert == 0:
            saved_copy = pltpu.make_async_copy(
                saved_all.at[pl.ds(part * held, held)], saved_pre, saved_sem
            )
            saved_copy.start()

    order = row_order(sizes, there, (rows.shape[0], moved), 1)
    rows[...] = dot(order, joined(got)).astype(BF16)
    results[:, width:] = jnp.zeros((results.shape[0], results.shape[1] - width), BF16)

    saved_copy.wait()

    def one_expert(expert, carry):
        slot = lax.rem(expert, slots)
        own_f = pl.ds(pl.multiple_of(expert * padded, ROWS), padded)
        own_b = pl.ds(pl.multiple_of((held + expert) * padded, ROWS), padded)
        hidden, pre_grad, inner = [], [], 0.0
        for piece in range(halves):
            for copy in copies(expert, piece):
                copy.wait()
            span = slice(piece * half, (piece + 1) * half)
            pre_act = dot(rows[own_f, :], up_held[slot, :, span])
            hidden_grad = dot(rows[own_b, :], down_held[slot, span, :], NT)
            hidden.append((pre_act / (1.0 + jnp.exp(-pre_act))).astype(BF16))
            pre = saved_pre[expert, :, span].astype(F32)
            gate = 1.0 / (1.0 + jnp.exp(-pre))
            inner += jnp.sum(
                hidden_grad * (pre * gate).astype(BF16).astype(F32), axis=1, keepdims=True
            )
            pre_grad.append((hidden_grad * gate * (1.0 + pre * (1.0 - gate))).astype(BF16))
        result_f = dot(jnp.concatenate(hidden, axis=1), down_held[slot])
        result_b = dot(jnp.concatenate(pre_grad, axis=1), up_held[slot], NT)
        results[own_f, :width] = result_f.astype(BF16)
        results[own_b, :width] = result_b.astype(BF16)
        results[own_b, width:] = jnp.broadcast_to(inner, (padded, LANES)).astype(BF16)

        @pl.when(expert + slots < held)
        def _():
            for piece in range(halves):
                for copy in copies(expert + slots, piece):
                    copy.start()

        return carry

    lax.fori_loop(0, held, one_expert, 0)
    order = row_order(sizes, back, (moved, rows.shape[0]), 0)
    parted(dot(order, results[...]), out)


def add_up(blocks, mixing_f, mixing_b, tables):
    back = joined(blocks)
    width = back.shape[1] - LANES
    sums = back[:, width:].astype(F32)[:, :1]
    return (
        dot(mixing_f[...], back[:, :width]),
        dot(mixing_b[...], back[:, :width]),
        [jnp.sum(tables[k].astype(F32) * sums, axis=0, keepdims=True) for k in range(tables.shape[0])],
    )


def early_kernel(sizes, handed, tokens, *refs):
    output, gradient, inner, *copies = refs[-3 - handed :]
    for given, copied in zip(refs, copies):
        copied[...] = given[...]
    refs = refs[handed : -3 - handed]
    own = None
    if sizes["back"][-1]:
        refs, own = refs[:-4], refs[-4:]
    sum_f, sum_b, sums = tokens[...].astype(F32), None, None
    for turned in sizes["back"][:-1]:
        blocks = sizes["sources"] if turned else 1
        more_f, more_b, more = add_up(refs[3 : 3 + blocks], *refs[:3])
        refs = refs[3 + blocks :]
        sum_f += more_f
        sum_b = more_b if sum_b is None else sum_b + more_b
        sums = more if sums is None else [a + b for a, b in zip(sums, more)]
    if own is not None:
        blocks = [own[3]] + [None] * (sizes["sources"] - 1)
        more_f, more_b, more = add_up(blocks, *own[:3])
        sum_f += more_f
        sum_b = more_b if sum_b is None else sum_b + more_b
        sums = more if sums is None else [a + b for a, b in zip(sums, more)]
    output[...] = sum_f
    if sums is None:
        gradient[...] = jnp.zeros(gradient.shape, F32)
        inner[...] = jnp.zeros(inner.shape, F32)
    else:
        gradient[...] = sum_b
        for k, row in enumerate(sums):
            inner[k] = jnp.broadcast_to(row, inner.shape[1:])


def late_kernel(
    sizes, early_f, early_b, early_inner, saved, upstream, gain, router, routes,
    mixing_f, mixing_b, tables, shares, *refs,
):
    *backs, output, gradient = refs
    if sizes["back"][-1]:
        backs = [None] + backs
    more_f, more_b, more = add_up(backs, mixing_f, mixing_b, tables)
    widened = saved[...].astype(F32)
    inv_rms = lax.rsqrt(jnp.mean(widened * widened, axis=-1, keepdims=True) + EPS)
    hits = expert_hits(routes[...], sizes["experts"])
    top = len(hits)
    share = [shares[k][:1, :] for k in range(top)]
    inner = [early_inner[k][:1, :] + more[k] for k in range(top)]
    mean = sum(share[k] * inner[k] for k in range(top))
    logit_grad = sum(share[k] * (inner[k] - mean) * hits[k] for k in range(top))
    high = logit_grad.astype(BF16)
    rest = logit_grad - high.astype(F32)
    middle = rest.astype(BF16)
    low = (rest - middle.astype(F32)).astype(BF16)
    output[0] = (early_f[...] + more_f).astype(BF16)
    normed_grad = early_b[...] + more_b
    for piece in (high, middle, low):
        normed_grad += dot(piece, router[...], TN)
    gained = normed_grad * gain[...].astype(F32)
    projected = jnp.mean(widened * gained, axis=-1, keepdims=True)
    grad = inv_rms * gained - widened * (inv_rms * inv_rms * inv_rms * projected)
    gradient[0] = (upstream[...].astype(F32) + grad).astype(BF16)


def exchange_columns(parts, sources, local, capacity):
    held = local // parts
    slots = sources * local * capacity
    block_rows = 2 * held * capacity
    columns = np.zeros((sources * block_rows, 2 + parts), np.int32)
    for source in range(sources):
        for batch in range(2):
            for expert in range(held):
                for slot in range(capacity):
                    within = (batch * held + expert) * capacity + slot
                    row = source * block_rows + within
                    columns[row, :2] = source, within
                    for part in range(parts):
                        own = (part * held + expert) * capacity + slot
                        columns[row, 2 + part] = batch * slots + own
    return columns


def on_device(
    forward_sent,
    embedded,
    forward_routes,
    backward_sent,
    loss_gradient,
    saved_inputs,
    backward_routes,
    pre_activation,
    norm_gain,
    router,
    up_weight,
    down_weight,
):
    sources = lax.axis_size("expert")
    experts = router.shape[2]
    capacity = pre_activation.shape[3]
    local, width, hidden = up_weight.shape
    count = embedded.shape[0]
    top = forward_routes.shape[2]
    slots = experts * capacity
    rows = sources * capacity
    padded = -(-rows // ROWS) * ROWS
    shape = jax.ShapeDtypeStruct
    parts = 2 if local % 2 == 0 else 1
    held = local // parts
    moved = 2 * slots // parts
    few = sources <= 8
    there = [few and part == 0 for part in range(parts)]
    back = [few and part == parts - 1 for part in range(parts)]
    columns = exchange_columns(parts, sources, local, capacity)
    sizes = {
        "experts": experts,
        "capacity": capacity,
        "sources": sources,
        "share": local * capacity,
        "there": there,
        "back": back,
        "padded": padded,
        "block_rows": moved // sources,
    }

    def blocks_of(turned, columns):
        blocks = sources if turned else 1
        return [shape((moved // blocks, columns), BF16)] * blocks

    later = [block for turned in there[1:] for block in blocks_of(turned, width)]

    router_t = router[0].T
    routes_f, routes_b = forward_routes[0].T, backward_routes[0].T
    arrived_f = from_behind(forward_sent[0], "section", 1)
    arrived_b = from_behind(backward_sent[0], "section", -1)
    row_shape = shape((count, width), BF16)
    table, embedded_held, loss_held, gain_held = call(
        functools.partial(table_kernel, sizes),
        (shape((moved, 2 * count), BF16), row_shape, row_shape, shape((1, width), BF16)),
        (4 * moved * count, 4 * (2 * count + moved) * width),
        in_specs=[VMEM] * 6,
    )(embedded, loss_gradient, norm_gain, routes_f, routes_b, columns)
    given = (arrived_f, arrived_b, embedded_held, loss_held, gain_held)
    send = call(
        first_send_kernel,
        tuple(blocks_of(there[0], width)),
        (4 * moved * count * width, 2 * (4 * count + moved) * width),
        in_specs=[VMEM] * 6,
    )(*given, table)
    mixing_shapes = [
        shape((count, moved), BF16),
        shape((count, moved), BF16),
        shape((top, moved, count), BF16),
    ]
    tokens, upstream, shares_b, *rest = call(
        functools.partial(mixing_kernel, sizes),
        (
            row_shape,
            row_shape,
            shape((top, 8, count), F32),
            *mixing_shapes * parts,
            *later,
        ),
        (4 * moved * count * width, 2 * (8 * count + moved) * width),
        vmem=LARGE_VMEM,
        in_specs=[VMEM] * 10,
    )(
        arrived_f, arrived_b, embedded, loss_gradient, norm_gain, routes_f, routes_b, columns,
        saved_inputs[0], router_t,
    )
    mixing = [rest[3 * part : 3 * part + 3] for part in range(parts)]
    sends = rest[3 * parts :]
    saved_pre = jnp.transpose(pre_activation[0], (1, 0, 2, 3)).reshape(local, rows, hidden)
    saved_pre = jnp.pad(saved_pre, ((0, 0), (0, padded - rows), (0, 0)))
    backs = []
    got = exchange(send, 1)
    for part in range(parts):
        if part + 1 < parts:
            sends, saved_pre, got = lax.optimization_barrier((sends, saved_pre, got))
            blocks = len(blocks_of(there[part + 1], width))
            coming = exchange(sends[:blocks], 1)
            sends = sends[blocks:]
        result = blocks_of(back[part], width + LANES)
        done = call(
            functools.partial(expert_kernel, sizes, part, held),
            tuple(result),
            (8 * held * padded * width * hidden, 4 * held * width * hidden),
            vmem=EXPERT_VMEM,
            in_specs=[HBM] * 3 + [VMEM] * len(got),
            out_specs=(VMEM,) * len(result),
            scratch_shapes=[
                pltpu.VMEM((2 * held * padded, width), BF16),
                pltpu.VMEM((2 * held * padded, width + LANES), BF16),
                pltpu.VMEM((held, padded, hidden), BF16),
                pltpu.VMEM((min(2, held), width, hidden), BF16),
                pltpu.VMEM((min(2, held), hidden, width), BF16),
                pltpu.SemaphoreType.DMA,
                pltpu.SemaphoreType.DMA((min(2, held), 2, 2)),
            ],
        )(saved_pre, up_weight, down_weight, *got)
        backs.append(exchange(list(done), -1))
        got = coming if part + 1 < parts else None
    handed = (
        saved_inputs[0], upstream, norm_gain, router_t, routes_b, *mixing[-1], shares_b,
    )
    own = (*mixing[-1], backs[-1][0]) if back[-1] else ()
    early = call(
        functools.partial(early_kernel, sizes, len(handed)),
        (
            shape((count, width), F32),
            shape((count, width), F32),
            shape((top, 8, count), F32),
            *[shape(array.shape, array.dtype) for array in handed],
        ),
        (4 * moved * count * width, 2 * (10 * count + moved) * width),
    )(tokens, *handed, *[ref for part in range(parts - 1) for ref in (*mixing[part], *backs[part])], *own)
    return tuple(
        call(
            functools.partial(late_kernel, sizes),
            (shape((1, count, width), BF16),) * 2,
            (4 * moved * count * width, 2 * (8 * count + moved) * width),
        )(*early, *(backs[-1][1:] if back[-1] else backs[-1]))
    )


def solution(mesh):
    return jax.shard_map(
        on_device,
        mesh=mesh,
        in_specs=(
            P("section", "expert", None),
            P("expert", None),
            P("section", "expert", None),
            P("section", "expert", None),
            P("expert", None),
            P("section", "expert", None),
            P("section", "expert", None),
            P("section", None, "expert", None, None),
            P("section", None),
            P("section", None, None),
            P("expert", None, None),
            P("expert", None, None),
        ),
        out_specs=(P("section", "expert", None), P("section", "expert", None)),
        check_vma=False,
    )
```

```python
import functools

import jax
import jax.numpy as jnp
import numpy as np
from jax import lax
from jax.experimental import pallas as pl
from jax.experimental.pallas import tpu as pltpu
from jax.sharding import PartitionSpec as P

EPS = 1e-06
BF16 = jnp.bfloat16
F32 = jnp.float32
LANES = 128
ROWS = 16
SMALL_VMEM = 16 * 1024 * 1024
EXPERT_VMEM = 28 * 1024 * 1024
LARGE_VMEM = 60 * 1024 * 1024
NT = (((1,), (1,)), ((), ()))
TN = (((0,), (0,)), ((), ()))


def dot(a, b, dims=(((1,), (0,)), ((), ()))):
    return lax.dot_general(a, b, dims, preferred_element_type=F32)


def call(kernel, out_shape, cost, vmem=SMALL_VMEM, **kwargs):
    flops, moved = cost
    return pl.pallas_call(
        kernel,
        out_shape=out_shape,
        compiler_params=pltpu.CompilerParams(vmem_limit_bytes=vmem),
        cost_estimate=pl.CostEstimate(flops=flops, bytes_accessed=moved, transcendentals=0),
        **kwargs,
    )


VMEM = pl.BlockSpec(memory_space=pltpu.VMEM)
HBM = pl.BlockSpec(memory_space=pl.ANY)


def from_behind(block, axis, distance):
    devices = range(lax.axis_size(axis))
    route = [(i - distance, i) for i in devices if i - distance in devices]
    return lax.ppermute(block, axis, route)


def far_first(size):
    return sorted(range(size), key=lambda d: (abs(2 * d - size), d)) if size > 1 else [0]


def by_block(refs):
    ordered = [None] * len(refs)
    for ref, d in zip(refs, far_first(len(refs))):
        ordered[d] = ref
    return ordered


def exchange(blocks, direction):
    size = lax.axis_size("expert")
    if len(blocks) == 1:
        return [lax.all_to_all(blocks[0], "expert", split_axis=0, concat_axis=0, tiled=True)]
    got = list(blocks)
    for d in far_first(size)[:-1]:
        route = [(i, (i + direction * d) % size) for i in range(size)]
        got[d] = lax.ppermute(blocks[d], "expert", route)
    return got


def joined(refs):
    if len(refs) == 1:
        return refs[0][...]
    blocks = [ref[...].astype(F32) if ref is not None else None for ref in refs]
    empty = jnp.zeros_like(next(block for block in blocks if block is not None))
    return jnp.concatenate([empty if b is None else b for b in blocks], axis=0).astype(BF16)


def parted(value, refs):
    share = value.shape[0] // len(refs)
    for d, ref in enumerate(refs):
        ref[...] = value[d * share : (d + 1) * share].astype(BF16)


def partners(distance, sources, direction, turned):
    if not turned:
        return distance
    device = lax.axis_index("expert") + direction * distance
    return jnp.where(device < 0, device + sources, jnp.where(device >= sources, device - sources, device))


def expert_hits(routes, experts):
    top, count = routes.shape
    lane = lax.broadcasted_iota(jnp.int32, (experts, count), 0)
    return [(routes[k : k + 1, :] == lane).astype(F32) for k in range(top)]


def slot_targets(routes, experts, capacity):
    top, count = routes.shape
    hits = expert_hits(routes, experts)
    earlier = lax.broadcasted_iota(jnp.int32, (count, count), 0) < lax.broadcasted_iota(
        jnp.int32, (count, count), 1
    )
    before = dot(sum(hits).astype(BF16), earlier.astype(F32).astype(BF16))
    targets = []
    for k in range(top):
        ranked = jnp.sum((before + sum(hits[:k], jnp.zeros_like(before))) * hits[k], 0, keepdims=True)
        targets.append(routes[k : k + 1, :] * capacity + ranked.astype(jnp.int32))
    return targets, hits


def tables_of(targets, row_keys):
    return [(row_keys == target).astype(F32) for target in targets]


def normalise(tokens, gain):
    widened = tokens.astype(F32)
    inv_rms = lax.rsqrt(jnp.mean(widened * widened, axis=-1, keepdims=True) + EPS)
    return widened, inv_rms, (widened * inv_rms * gain.astype(F32)).astype(BF16)


def route_shares(normed, router, hits):
    logits = dot(router, normed, NT)
    exponents = [jnp.exp(jnp.sum(logits * hit, axis=0, keepdims=True)) for hit in hits]
    total = sum(exponents)
    return [exponent / total for exponent in exponents]


def keys_of_part(sizes, columns, part, turned):
    device = partners(columns[:, 0:1], sizes["sources"], 1, turned)
    return columns[:, 2 + part : 3 + part] + device * sizes["share"]


def rows_to_send(arrived_f, arrived_b, embedded, loss, gain):
    section = lax.axis_index("section")
    last = lax.axis_size("section") - 1
    tokens = jnp.where(section == 0, embedded[...], arrived_f[...])
    upstream = jnp.where(section == last, loss[...], arrived_b[...])
    return tokens, normalise(tokens, gain[...])[2], upstream


def table_kernel(
    sizes, embedded, loss, gain, routes_f, routes_b, columns,
    table, embedded_out, loss_out, gain_out,
):
    experts, capacity = sizes["experts"], sizes["capacity"]
    targets_f, _ = slot_targets(routes_f[...], experts, capacity)
    targets_b, _ = slot_targets(routes_b[...], experts, capacity)
    keys = keys_of_part(sizes, columns, 0, sizes["there"][0])
    table_f = sum(tables_of(targets_f, keys))
    table_b = sum(tables_of([t + experts * capacity for t in targets_b], keys))
    table[...] = jnp.concatenate([table_f, table_b], axis=1).astype(BF16)
    embedded_out[...] = embedded[...]
    loss_out[...] = loss[...]
    gain_out[...] = gain[...]


def first_send_kernel(arrived_f, arrived_b, embedded, loss, gain, table, *send):
    _, normed, upstream = rows_to_send(arrived_f, arrived_b, embedded, loss, gain)
    parted(dot(table[...], jnp.concatenate([normed, upstream], axis=0)), send)


def mixing_kernel(
    sizes, arrived_f, arrived_b, embedded, loss, gain, routes_f, routes_b, columns,
    saved, router, tokens, upstream, shares_b, *refs,
):
    experts, capacity = sizes["experts"], sizes["capacity"]
    parts = len(sizes["back"])
    mixing, sends = refs[: 3 * parts], refs[3 * parts :]
    tokens[...], normed, upstream[...] = rows_to_send(
        arrived_f, arrived_b, embedded, loss, gain
    )
    data = jnp.concatenate([normed, upstream[...]], axis=0)
    targets_f, hits = slot_targets(routes_f[...], experts, capacity)
    shares_f = route_shares(normed, router[...], hits)
    targets_b, hits = slot_targets(routes_b[...], experts, capacity)
    targets_b = [t + experts * capacity for t in targets_b]
    own_shares = route_shares(normalise(saved[...], gain[...])[2], router[...], hits)
    for k, share in enumerate(own_shares):
        shares_b[k] = jnp.broadcast_to(share, shares_b.shape[1:])
    for part in range(parts):
        there, back = sizes["there"][part], sizes["back"][part]
        mixing_f, mixing_b, tables_b = mixing[3 * part : 3 * part + 3]
        keys = keys_of_part(sizes, columns, part, back)
        found_f, found_b = tables_of(targets_f, keys), tables_of(targets_b, keys)
        for out, found, shares in ((mixing_f, found_f, shares_f), (mixing_b, found_b, own_shares)):
            mixed = sum(t * s.astype(BF16).astype(F32) for t, s in zip(found, shares))
            out[...] = jnp.transpose(mixed).astype(BF16)
        for k, table in enumerate(found_b):
            tables_b[k] = table.astype(BF16)
        if part > 0:
            if there != back:
                keys = keys_of_part(sizes, columns, part, there)
                found_f, found_b = tables_of(targets_f, keys), tables_of(targets_b, keys)
            blocks = sizes["sources"] if there else 1
            table = jnp.concatenate([sum(found_f), sum(found_b)], axis=1).astype(BF16)
            parted(dot(table, data), sends[:blocks])
            sends = sends[blocks:]


def row_order(sizes, turned, shape, axis):
    line = tuple(size if i == axis else 1 for i, size in enumerate(shape))
    row = lax.broadcasted_iota(jnp.int32, line, axis)
    block = sum(
        (row >= k * sizes["block_rows"]).astype(jnp.int32) for k in range(1, sizes["sources"])
    )
    within = row - block * sizes["block_rows"]
    group = sum(
        (within >= k * sizes["capacity"]).astype(jnp.int32)
        for k in range(1, sizes["block_rows"] // sizes["capacity"])
    )
    source = partners(block, sizes["sources"], -1, turned)
    place = group * (sizes["padded"] - sizes["capacity"]) + source * sizes["capacity"] + within
    return (place == lax.broadcasted_iota(jnp.int32, shape, 1 - axis)).astype(F32).astype(BF16)


def expert_kernel(sizes, part, held, saved_all, up, down, *refs):
    there, back = sizes["there"][part], sizes["back"][part]
    blocks = sizes["sources"] if there else 1
    got, out = by_block(refs[:blocks]), refs[blocks:-7]
    rows, results, saved_pre, up_held, down_held, saved_sem, sems = refs[-7:]
    moved = blocks * got[0].shape[0]
    width = rows.shape[1]
    slots, halves = sems.shape[:2]
    half = up.shape[2] // halves
    padded = sizes["padded"]

    def copies(expert, piece):
        slot = lax.rem(expert, slots)
        piece_of = pl.ds(piece * half, half)
        return [
            pltpu.make_async_copy(
                up.at[part * held + expert, :, piece_of],
                up_held.at[slot, :, piece_of],
                sems.at[slot, piece, 0],
            ),
            pltpu.make_async_copy(
                down.at[part * held + expert, piece_of, :],
                down_held.at[slot, piece_of, :],
                sems.at[slot, piece, 1],
            ),
        ]

    for expert in range(min(slots, held)):
        for piece in range(halves):
            for copy in copies(jnp.int32(expert), piece):
                copy.start()

        if expert == 0:
            saved_copy = pltpu.make_async_copy(
                saved_all.at[pl.ds(part * held, held)], saved_pre, saved_sem
            )
            saved_copy.start()

    order = row_order(sizes, there, (rows.shape[0], moved), 1)
    rows[...] = dot(order, joined(got)).astype(BF16)
    results[:, width:] = jnp.zeros((results.shape[0], results.shape[1] - width), BF16)

    saved_copy.wait()

    def one_expert(expert, carry):
        slot = lax.rem(expert, slots)
        own_f = pl.ds(pl.multiple_of(expert * padded, ROWS), padded)
        own_b = pl.ds(pl.multiple_of((held + expert) * padded, ROWS), padded)
        hidden, pre_grad, inner = [], [], 0.0
        for piece in range(halves):
            for copy in copies(expert, piece):
                copy.wait()
            span = slice(piece * half, (piece + 1) * half)
            pre_act = dot(rows[own_f, :], up_held[slot, :, span])
            hidden_grad = dot(rows[own_b, :], down_held[slot, span, :], NT)
            hidden.append((pre_act / (1.0 + jnp.exp(-pre_act))).astype(BF16))
            pre = saved_pre[expert, :, span].astype(F32)
            gate = 1.0 / (1.0 + jnp.exp(-pre))
            inner += jnp.sum(
                hidden_grad * (pre * gate).astype(BF16).astype(F32), axis=1, keepdims=True
            )
            pre_grad.append((hidden_grad * gate * (1.0 + pre * (1.0 - gate))).astype(BF16))
        result_f = dot(jnp.concatenate(hidden, axis=1), down_held[slot])
        result_b = dot(jnp.concatenate(pre_grad, axis=1), up_held[slot], NT)
        results[own_f, :width] = result_f.astype(BF16)
        results[own_b, :width] = result_b.astype(BF16)
        results[own_b, width:] = jnp.broadcast_to(inner, (padded, LANES)).astype(BF16)

        @pl.when(expert + slots < held)
        def _():
            for piece in range(halves):
                for copy in copies(expert + slots, piece):
                    copy.start()

        return carry

    lax.fori_loop(0, held, one_expert, 0)
    order = row_order(sizes, back, (moved, rows.shape[0]), 0)
    parted(dot(order, results[...]), out)


def add_up(blocks, mixing_f, mixing_b, tables):
    back = joined(blocks)
    width = back.shape[1] - LANES
    sums = back[:, width:].astype(F32)[:, :1]
    return (
        dot(mixing_f[...], back[:, :width]),
        dot(mixing_b[...], back[:, :width]),
        [jnp.sum(tables[k].astype(F32) * sums, axis=0, keepdims=True) for k in range(tables.shape[0])],
    )


def early_kernel(sizes, handed, tokens, *refs):
    output, gradient, inner, *copies = refs[-3 - handed :]
    for given, copied in zip(refs, copies):
        copied[...] = given[...]
    refs = refs[handed : -3 - handed]
    own = None
    if sizes["back"][-1]:
        refs, own = refs[:-4], refs[-4:]
    sum_f, sum_b, sums = tokens[...].astype(F32), None, None
    for turned in sizes["back"][:-1]:
        blocks = sizes["sources"] if turned else 1
        more_f, more_b, more = add_up(refs[3 : 3 + blocks], *refs[:3])
        refs = refs[3 + blocks :]
        sum_f += more_f
        sum_b = more_b if sum_b is None else sum_b + more_b
        sums = more if sums is None else [a + b for a, b in zip(sums, more)]
    if own is not None:
        blocks = [own[3]] + [None] * (sizes["sources"] - 1)
        more_f, more_b, more = add_up(blocks, *own[:3])
        sum_f += more_f
        sum_b = more_b if sum_b is None else sum_b + more_b
        sums = more if sums is None else [a + b for a, b in zip(sums, more)]
    output[...] = sum_f
    if sums is None:
        gradient[...] = jnp.zeros(gradient.shape, F32)
        inner[...] = jnp.zeros(inner.shape, F32)
    else:
        gradient[...] = sum_b
        for k, row in enumerate(sums):
            inner[k] = jnp.broadcast_to(row, inner.shape[1:])


def late_kernel(
    sizes, early_f, early_b, early_inner, saved, upstream, gain, router, routes, shares,
    mixing_f, mixing_b, tables, *refs,
):
    *backs, output, gradient = refs
    if sizes["back"][-1]:
        backs = by_block(backs + [None])
    more_f, more_b, more = add_up(backs, mixing_f, mixing_b, tables)
    widened = saved[...].astype(F32)
    inv_rms = lax.rsqrt(jnp.mean(widened * widened, axis=-1, keepdims=True) + EPS)
    hits = expert_hits(routes[...], sizes["experts"])
    top = len(hits)
    share = [shares[k][:1, :] for k in range(top)]
    inner = [early_inner[k][:1, :] + more[k] for k in range(top)]
    mean = sum(share[k] * inner[k] for k in range(top))
    logit_grad = sum(share[k] * (inner[k] - mean) * hits[k] for k in range(top))
    high = logit_grad.astype(BF16)
    rest = logit_grad - high.astype(F32)
    middle = rest.astype(BF16)
    low = (rest - middle.astype(F32)).astype(BF16)
    output[0] = (early_f[...] + more_f).astype(BF16)
    normed_grad = early_b[...] + more_b
    for piece in (high, middle, low):
        normed_grad += dot(piece, router[...], TN)
    gained = normed_grad * gain[...].astype(F32)
    projected = jnp.mean(widened * gained, axis=-1, keepdims=True)
    grad = inv_rms * gained - widened * (inv_rms * inv_rms * inv_rms * projected)
    gradient[0] = (upstream[...].astype(F32) + grad).astype(BF16)


def exchange_columns(parts, sources, local, capacity):
    held = local // parts
    slots = sources * local * capacity
    block_rows = 2 * held * capacity
    columns = np.zeros((sources * block_rows, 2 + parts), np.int32)
    for source in range(sources):
        for batch in range(2):
            for expert in range(held):
                for slot in range(capacity):
                    within = (batch * held + expert) * capacity + slot
                    row = source * block_rows + within
                    columns[row, :2] = source, within
                    for part in range(parts):
                        own = (part * held + expert) * capacity + slot
                        columns[row, 2 + part] = batch * slots + own
    return columns


def on_device(
    forward_sent,
    embedded,
    forward_routes,
    backward_sent,
    loss_gradient,
    saved_inputs,
    backward_routes,
    pre_activation,
    norm_gain,
    router,
    up_weight,
    down_weight,
):
    sources = lax.axis_size("expert")
    experts = router.shape[2]
    capacity = pre_activation.shape[3]
    local, width, hidden = up_weight.shape
    count = embedded.shape[0]
    top = forward_routes.shape[2]
    slots = experts * capacity
    rows = sources * capacity
    padded = -(-rows // ROWS) * ROWS
    shape = jax.ShapeDtypeStruct
    parts = 2 if local % 2 == 0 else 1
    held = local // parts
    moved = 2 * slots // parts
    few = sources <= 8
    there = [few and part == 0 for part in range(parts)]
    back = [few and part == parts - 1 for part in range(parts)]
    columns = exchange_columns(parts, sources, local, capacity)
    sizes = {
        "experts": experts,
        "capacity": capacity,
        "sources": sources,
        "share": local * capacity,
        "there": there,
        "back": back,
        "padded": padded,
        "block_rows": moved // sources,
    }

    def blocks_of(turned, columns):
        blocks = sources if turned else 1
        return [shape((moved // blocks, columns), BF16)] * blocks

    later = [block for turned in there[1:] for block in blocks_of(turned, width)]

    router_t = router[0].T
    routes_f, routes_b = forward_routes[0].T, backward_routes[0].T
    arrived_f = from_behind(forward_sent[0], "section", 1)
    arrived_b = from_behind(backward_sent[0], "section", -1)
    row_shape = shape((count, width), BF16)
    table, embedded_held, loss_held, gain_held = call(
        functools.partial(table_kernel, sizes),
        (shape((moved, 2 * count), BF16), row_shape, row_shape, shape((1, width), BF16)),
        (4 * moved * count, 4 * (2 * count + moved) * width),
        in_specs=[VMEM] * 6,
    )(embedded, loss_gradient, norm_gain, routes_f, routes_b, columns)
    given = (arrived_f, arrived_b, embedded_held, loss_held, gain_held)
    send = call(
        first_send_kernel,
        tuple(blocks_of(there[0], width)),
        (4 * moved * count * width, 2 * (4 * count + moved) * width),
        in_specs=[VMEM] * 6,
    )(*given, table)
    mixing_shapes = [
        shape((count, moved), BF16),
        shape((count, moved), BF16),
        shape((top, moved, count), BF16),
    ]
    tokens, upstream, shares_b, *rest = call(
        functools.partial(mixing_kernel, sizes),
        (
            row_shape,
            row_shape,
            shape((top, 8, count), F32),
            *mixing_shapes * parts,
            *later,
        ),
        (4 * moved * count * width, 2 * (8 * count + moved) * width),
        vmem=LARGE_VMEM,
        in_specs=[VMEM] * 10,
    )(
        arrived_f, arrived_b, embedded, loss_gradient, norm_gain, routes_f, routes_b, columns,
        saved_inputs[0], router_t,
    )
    mixing = [rest[3 * part : 3 * part + 3] for part in range(parts)]
    sends = rest[3 * parts :]
    saved_pre = jnp.transpose(pre_activation[0], (1, 0, 2, 3)).reshape(local, rows, hidden)
    saved_pre = jnp.pad(saved_pre, ((0, 0), (0, padded - rows), (0, 0)))
    backs = []
    got = exchange(send, 1)
    for part in range(parts):
        if part + 1 < parts:
            got = [got[d] for d in far_first(len(got))]
            sends, saved_pre, got = lax.optimization_barrier((sends, saved_pre, got))
            got = by_block(got)
            blocks = len(blocks_of(there[part + 1], width))
            coming = exchange(sends[:blocks], 1)
            sends = sends[blocks:]
        result = blocks_of(back[part], width + LANES)
        done = call(
            functools.partial(expert_kernel, sizes, part, held),
            tuple(result),
            (8 * held * padded * width * hidden, 4 * held * width * hidden),
            vmem=EXPERT_VMEM,
            in_specs=[HBM] * 3 + [VMEM] * len(got),
            out_specs=(VMEM,) * len(result),
            scratch_shapes=[
                pltpu.VMEM((2 * held * padded, width), BF16),
                pltpu.VMEM((2 * held * padded, width + LANES), BF16),
                pltpu.VMEM((held, padded, hidden), BF16),
                pltpu.VMEM((min(2, held), width, hidden), BF16),
                pltpu.VMEM((min(2, held), hidden, width), BF16),
                pltpu.SemaphoreType.DMA,
                pltpu.SemaphoreType.DMA((min(2, held), 2, 2)),
            ],
        )(saved_pre, up_weight, down_weight, *[got[d] for d in far_first(len(got))])
        backs.append(exchange(list(done), -1))
        got = coming if part + 1 < parts else None
    handed = (
        saved_inputs[0], upstream, norm_gain, router_t, routes_b, shares_b,
    )
    own = (*mixing[-1], backs[-1][0]) if back[-1] else ()
    early = call(
        functools.partial(early_kernel, sizes, len(handed)),
        (
            shape((count, width), F32),
            shape((count, width), F32),
            shape((top, 8, count), F32),
            *[shape(array.shape, array.dtype) for array in handed],
        ),
        (4 * moved * count * width, 2 * (10 * count + moved) * width),
    )(tokens, *handed, *[ref for part in range(parts - 1) for ref in (*mixing[part], *backs[part])], *own)
    return tuple(
        call(
            functools.partial(late_kernel, sizes),
            (shape((1, count, width), BF16),) * 2,
            (4 * moved * count * width, 2 * (8 * count + moved) * width),
        )(
            *early,
            *mixing[-1],
            *[backs[-1][d] for d in far_first(len(backs[-1])) if d > 0 or not back[-1]],
        )
    )


def solution(mesh):
    return jax.shard_map(
        on_device,
        mesh=mesh,
        in_specs=(
            P("section", "expert", None),
            P("expert", None),
            P("section", "expert", None),
            P("section", "expert", None),
            P("expert", None),
            P("section", "expert", None),
            P("section", "expert", None),
            P("section", None, "expert", None, None),
            P("section", None),
            P("section", None, None),
            P("expert", None, None),
            P("expert", None, None),
        ),
        out_specs=(P("section", "expert", None), P("section", "expert", None)),
        check_vma=False,
    )
```

```python
import functools

import jax
import jax.numpy as jnp
import numpy as np
from jax import lax
from jax.experimental import pallas as pl
from jax.experimental.pallas import tpu as pltpu
from jax.sharding import PartitionSpec as P

EPS = 1e-06
BF16 = jnp.bfloat16
F32 = jnp.float32
LANES = 128
ROWS = 16
SMALL_VMEM = 16 * 1024 * 1024
EXPERT_VMEM = 28 * 1024 * 1024
LARGE_VMEM = 60 * 1024 * 1024
NT = (((1,), (1,)), ((), ()))
TN = (((0,), (0,)), ((), ()))


def dot(a, b, dims=(((1,), (0,)), ((), ()))):
    return lax.dot_general(a, b, dims, preferred_element_type=F32)


def call(kernel, out_shape, cost, vmem=SMALL_VMEM, **kwargs):
    flops, moved = cost
    return pl.pallas_call(
        kernel,
        out_shape=out_shape,
        compiler_params=pltpu.CompilerParams(vmem_limit_bytes=vmem),
        cost_estimate=pl.CostEstimate(flops=flops, bytes_accessed=moved, transcendentals=0),
        **kwargs,
    )


VMEM = pl.BlockSpec(memory_space=pltpu.VMEM)
HBM = pl.BlockSpec(memory_space=pl.ANY)


def from_behind(block, axis, distance):
    devices = range(lax.axis_size(axis))
    route = [(i - distance, i) for i in devices if i - distance in devices]
    return lax.ppermute(block, axis, route)


def far_first(size):
    if size == 1:
        return [0]
    return [1, *range(max(2, size // 2), size), *range(2, size // 2), 0]


def by_block(refs):
    ordered = [None] * len(refs)
    for ref, d in zip(refs, far_first(len(refs))):
        ordered[d] = ref
    return ordered


def exchange(blocks):
    size = lax.axis_size("expert")
    if len(blocks) == 1:
        return [lax.all_to_all(blocks[0], "expert", split_axis=0, concat_axis=0, tiled=True)]
    got = list(blocks)
    for d in far_first(size)[:-1]:
        got[d] = lax.ppermute(blocks[d], "expert", [(i, i ^ d) for i in range(size)])
    return got


def joined(refs):
    if len(refs) == 1:
        return refs[0][...]
    blocks = [ref[...].astype(F32) if ref is not None else None for ref in refs]
    empty = jnp.zeros_like(next(block for block in blocks if block is not None))
    return jnp.concatenate([empty if b is None else b for b in blocks], axis=0).astype(BF16)


def parted(value, refs):
    share = value.shape[0] // len(refs)
    for d, ref in enumerate(refs):
        ref[...] = value[d * share : (d + 1) * share].astype(BF16)


def partners(block, swapped):
    return lax.bitwise_xor(block, jnp.full_like(block, lax.axis_index("expert"))) if swapped else block


def expert_hits(routes, experts):
    top, count = routes.shape
    lane = lax.broadcasted_iota(jnp.int32, (experts, count), 0)
    return [(routes[k : k + 1, :] == lane).astype(F32) for k in range(top)]


def slot_targets(routes, experts, capacity):
    top, count = routes.shape
    hits = expert_hits(routes, experts)
    earlier = lax.broadcasted_iota(jnp.int32, (count, count), 0) < lax.broadcasted_iota(
        jnp.int32, (count, count), 1
    )
    before = dot(sum(hits).astype(BF16), earlier.astype(F32).astype(BF16))
    targets = []
    for k in range(top):
        ranked = jnp.sum((before + sum(hits[:k], jnp.zeros_like(before))) * hits[k], 0, keepdims=True)
        targets.append(routes[k : k + 1, :] * capacity + ranked.astype(jnp.int32))
    return targets, hits


def tables_of(targets, row_keys):
    return [(row_keys == target).astype(F32) for target in targets]


def normalise(tokens, gain):
    widened = tokens.astype(F32)
    inv_rms = lax.rsqrt(jnp.mean(widened * widened, axis=-1, keepdims=True) + EPS)
    return widened, inv_rms, (widened * inv_rms * gain.astype(F32)).astype(BF16)


def route_shares(normed, router, hits):
    logits = dot(router, normed, NT)
    exponents = [jnp.exp(jnp.sum(logits * hit, axis=0, keepdims=True)) for hit in hits]
    total = sum(exponents)
    return [exponent / total for exponent in exponents]


def keys_of_part(sizes, columns, part, swapped):
    device = partners(columns[:, 0:1], swapped)
    return columns[:, 2 + part : 3 + part] + device * sizes["share"]


def rows_to_send(arrived_f, arrived_b, embedded, loss, gain):
    section = lax.axis_index("section")
    last = lax.axis_size("section") - 1
    tokens = jnp.where(section == 0, embedded[...], arrived_f[...])
    upstream = jnp.where(section == last, loss[...], arrived_b[...])
    return tokens, normalise(tokens, gain[...])[2], upstream


def table_kernel(
    sizes, embedded, loss, gain, routes_f, routes_b, columns,
    table, embedded_out, loss_out, gain_out,
):
    experts, capacity = sizes["experts"], sizes["capacity"]
    targets_f, _ = slot_targets(routes_f[...], experts, capacity)
    targets_b, _ = slot_targets(routes_b[...], experts, capacity)
    keys = keys_of_part(sizes, columns, 0, sizes["there"][0])
    table_f = sum(tables_of(targets_f, keys))
    table_b = sum(tables_of([t + experts * capacity for t in targets_b], keys))
    table[...] = jnp.concatenate([table_f, table_b], axis=1).astype(BF16)
    embedded_out[...] = embedded[...]
    loss_out[...] = loss[...]
    gain_out[...] = gain[...]


def first_send_kernel(arrived_f, arrived_b, embedded, loss, gain, table, *send):
    _, normed, upstream = rows_to_send(arrived_f, arrived_b, embedded, loss, gain)
    parted(dot(table[...], jnp.concatenate([normed, upstream], axis=0)), send)


def mixing_kernel(
    sizes, arrived_f, arrived_b, embedded, loss, gain, routes_f, routes_b, columns,
    saved, router, tokens, upstream, shares_b, *refs,
):
    experts, capacity = sizes["experts"], sizes["capacity"]
    parts = len(sizes["back"])
    mixing, sends = refs[: 3 * parts], refs[3 * parts :]
    tokens[...], normed, upstream[...] = rows_to_send(
        arrived_f, arrived_b, embedded, loss, gain
    )
    data = jnp.concatenate([normed, upstream[...]], axis=0)
    targets_f, hits = slot_targets(routes_f[...], experts, capacity)
    shares_f = route_shares(normed, router[...], hits)
    targets_b, hits = slot_targets(routes_b[...], experts, capacity)
    targets_b = [t + experts * capacity for t in targets_b]
    own_shares = route_shares(normalise(saved[...], gain[...])[2], router[...], hits)
    for k, share in enumerate(own_shares):
        shares_b[k] = jnp.broadcast_to(share, shares_b.shape[1:])
    for part in range(parts):
        there, back = sizes["there"][part], sizes["back"][part]
        mixing_f, mixing_b, tables_b = mixing[3 * part : 3 * part + 3]
        keys = keys_of_part(sizes, columns, part, back)
        found_f, found_b = tables_of(targets_f, keys), tables_of(targets_b, keys)
        for out, found, shares in ((mixing_f, found_f, shares_f), (mixing_b, found_b, own_shares)):
            mixed = sum(t * s.astype(BF16).astype(F32) for t, s in zip(found, shares))
            out[...] = jnp.transpose(mixed).astype(BF16)
        for k, table in enumerate(found_b):
            tables_b[k] = table.astype(BF16)
        if part > 0:
            if there != back:
                keys = keys_of_part(sizes, columns, part, there)
                found_f, found_b = tables_of(targets_f, keys), tables_of(targets_b, keys)
            blocks = sizes["sources"] if there else 1
            table = jnp.concatenate([sum(found_f), sum(found_b)], axis=1).astype(BF16)
            parted(dot(table, data), sends[:blocks])
            sends = sends[blocks:]


def row_order(sizes, swapped, shape, axis):
    line = tuple(size if i == axis else 1 for i, size in enumerate(shape))
    row = lax.broadcasted_iota(jnp.int32, line, axis)
    block = sum(
        (row >= k * sizes["block_rows"]).astype(jnp.int32) for k in range(1, sizes["sources"])
    )
    within = row - block * sizes["block_rows"]
    group = sum(
        (within >= k * sizes["capacity"]).astype(jnp.int32)
        for k in range(1, sizes["block_rows"] // sizes["capacity"])
    )
    source = partners(block, swapped)
    place = group * (sizes["padded"] - sizes["capacity"]) + source * sizes["capacity"] + within
    return (place == lax.broadcasted_iota(jnp.int32, shape, 1 - axis)).astype(F32).astype(BF16)


def expert_kernel(sizes, part, held, saved_all, up, down, *refs):
    there, back = sizes["there"][part], sizes["back"][part]
    blocks = sizes["sources"] if there else 1
    got, out = by_block(refs[:blocks]), refs[blocks:-7]
    rows, results, saved_pre, up_held, down_held, saved_sem, sems = refs[-7:]
    moved = blocks * got[0].shape[0]
    width = rows.shape[1]
    slots, halves = sems.shape[:2]
    half = up.shape[2] // halves
    padded = sizes["padded"]

    def copies(expert, piece):
        slot = lax.rem(expert, slots)
        piece_of = pl.ds(piece * half, half)
        return [
            pltpu.make_async_copy(
                up.at[part * held + expert, :, piece_of],
                up_held.at[slot, :, piece_of],
                sems.at[slot, piece, 0],
            ),
            pltpu.make_async_copy(
                down.at[part * held + expert, piece_of, :],
                down_held.at[slot, piece_of, :],
                sems.at[slot, piece, 1],
            ),
        ]

    for expert in range(min(slots, held)):
        for piece in range(halves):
            for copy in copies(jnp.int32(expert), piece):
                copy.start()

        if expert == 0:
            saved_copy = pltpu.make_async_copy(
                saved_all.at[pl.ds(part * held, held)], saved_pre, saved_sem
            )
            saved_copy.start()

    order = row_order(sizes, there, (rows.shape[0], moved), 1)
    rows[...] = dot(order, joined(got)).astype(BF16)
    results[:, width:] = jnp.zeros((results.shape[0], results.shape[1] - width), BF16)

    saved_copy.wait()

    def one_expert(expert, carry):
        slot = lax.rem(expert, slots)
        own_f = pl.ds(pl.multiple_of(expert * padded, ROWS), padded)
        own_b = pl.ds(pl.multiple_of((held + expert) * padded, ROWS), padded)
        hidden, pre_grad, inner = [], [], 0.0
        for piece in range(halves):
            for copy in copies(expert, piece):
                copy.wait()
            span = slice(piece * half, (piece + 1) * half)
            pre_act = dot(rows[own_f, :], up_held[slot, :, span])
            hidden_grad = dot(rows[own_b, :], down_held[slot, span, :], NT)
            hidden.append((pre_act / (1.0 + jnp.exp(-pre_act))).astype(BF16))
            pre = saved_pre[expert, :, span].astype(F32)
            gate = 1.0 / (1.0 + jnp.exp(-pre))
            inner += jnp.sum(
                hidden_grad * (pre * gate).astype(BF16).astype(F32), axis=1, keepdims=True
            )
            pre_grad.append((hidden_grad * gate * (1.0 + pre * (1.0 - gate))).astype(BF16))
        result_f = dot(jnp.concatenate(hidden, axis=1), down_held[slot])
        result_b = dot(jnp.concatenate(pre_grad, axis=1), up_held[slot], NT)
        results[own_f, :width] = result_f.astype(BF16)
        results[own_b, :width] = result_b.astype(BF16)
        results[own_b, width:] = jnp.broadcast_to(inner, (padded, LANES)).astype(BF16)

        @pl.when(expert + slots < held)
        def _():
            for piece in range(halves):
                for copy in copies(expert + slots, piece):
                    copy.start()

        return carry

    lax.fori_loop(0, held, one_expert, 0)
    order = row_order(sizes, back, (moved, rows.shape[0]), 0)
    parted(dot(order, results[...]), out)


def add_up(blocks, mixing_f, mixing_b, tables):
    back = joined(blocks)
    width = back.shape[1] - LANES
    sums = back[:, width:].astype(F32)[:, :1]
    return (
        dot(mixing_f[...], back[:, :width]),
        dot(mixing_b[...], back[:, :width]),
        [jnp.sum(tables[k].astype(F32) * sums, axis=0, keepdims=True) for k in range(tables.shape[0])],
    )


def early_kernel(sizes, handed, tokens, *refs):
    output, gradient, inner, *copies = refs[-3 - handed :]
    for given, copied in zip(refs, copies):
        copied[...] = given[...]
    refs = refs[handed : -3 - handed]
    own = None
    if sizes["back"][-1]:
        refs, own = refs[:-4], refs[-4:]
    sum_f, sum_b, sums = tokens[...].astype(F32), None, None
    for swapped in sizes["back"][:-1]:
        blocks = sizes["sources"] if swapped else 1
        more_f, more_b, more = add_up(refs[3 : 3 + blocks], *refs[:3])
        refs = refs[3 + blocks :]
        sum_f += more_f
        sum_b = more_b if sum_b is None else sum_b + more_b
        sums = more if sums is None else [a + b for a, b in zip(sums, more)]
    if own is not None:
        blocks = [own[3]] + [None] * (sizes["sources"] - 1)
        more_f, more_b, more = add_up(blocks, *own[:3])
        sum_f += more_f
        sum_b = more_b if sum_b is None else sum_b + more_b
        sums = more if sums is None else [a + b for a, b in zip(sums, more)]
    output[...] = sum_f
    if sums is None:
        gradient[...] = jnp.zeros(gradient.shape, F32)
        inner[...] = jnp.zeros(inner.shape, F32)
    else:
        gradient[...] = sum_b
        for k, row in enumerate(sums):
            inner[k] = jnp.broadcast_to(row, inner.shape[1:])


def late_kernel(
    sizes, early_f, early_b, early_inner, saved, upstream, gain, router, routes, shares,
    mixing_f, mixing_b, tables, *refs,
):
    *backs, output, gradient = refs
    if sizes["back"][-1]:
        backs = by_block(backs + [None])
    more_f, more_b, more = add_up(backs, mixing_f, mixing_b, tables)
    widened = saved[...].astype(F32)
    inv_rms = lax.rsqrt(jnp.mean(widened * widened, axis=-1, keepdims=True) + EPS)
    hits = expert_hits(routes[...], sizes["experts"])
    top = len(hits)
    share = [shares[k][:1, :] for k in range(top)]
    inner = [early_inner[k][:1, :] + more[k] for k in range(top)]
    mean = sum(share[k] * inner[k] for k in range(top))
    logit_grad = sum(share[k] * (inner[k] - mean) * hits[k] for k in range(top))
    high = logit_grad.astype(BF16)
    rest = logit_grad - high.astype(F32)
    middle = rest.astype(BF16)
    low = (rest - middle.astype(F32)).astype(BF16)
    output[0] = (early_f[...] + more_f).astype(BF16)
    normed_grad = early_b[...] + more_b
    for piece in (high, middle, low):
        normed_grad += dot(piece, router[...], TN)
    gained = normed_grad * gain[...].astype(F32)
    projected = jnp.mean(widened * gained, axis=-1, keepdims=True)
    grad = inv_rms * gained - widened * (inv_rms * inv_rms * inv_rms * projected)
    gradient[0] = (upstream[...].astype(F32) + grad).astype(BF16)


def exchange_columns(parts, sources, local, capacity):
    held = local // parts
    slots = sources * local * capacity
    block_rows = 2 * held * capacity
    columns = np.zeros((sources * block_rows, 2 + parts), np.int32)
    for source in range(sources):
        for batch in range(2):
            for expert in range(held):
                for slot in range(capacity):
                    within = (batch * held + expert) * capacity + slot
                    row = source * block_rows + within
                    columns[row, :2] = source, within
                    for part in range(parts):
                        own = (part * held + expert) * capacity + slot
                        columns[row, 2 + part] = batch * slots + own
    return columns


def on_device(
    forward_sent,
    embedded,
    forward_routes,
    backward_sent,
    loss_gradient,
    saved_inputs,
    backward_routes,
    pre_activation,
    norm_gain,
    router,
    up_weight,
    down_weight,
):
    sources = lax.axis_size("expert")
    experts = router.shape[2]
    capacity = pre_activation.shape[3]
    local, width, hidden = up_weight.shape
    count = embedded.shape[0]
    top = forward_routes.shape[2]
    slots = experts * capacity
    rows = sources * capacity
    padded = -(-rows // ROWS) * ROWS
    shape = jax.ShapeDtypeStruct
    parts = 2 if local % 2 == 0 else 1
    held = local // parts
    moved = 2 * slots // parts
    few = sources in (2, 4, 8)
    there = [few and part == 0 for part in range(parts)]
    back = [few and part == parts - 1 for part in range(parts)]
    columns = exchange_columns(parts, sources, local, capacity)
    sizes = {
        "experts": experts,
        "capacity": capacity,
        "sources": sources,
        "share": local * capacity,
        "there": there,
        "back": back,
        "padded": padded,
        "block_rows": moved // sources,
    }

    def blocks_of(swapped, columns):
        blocks = sources if swapped else 1
        return [shape((moved // blocks, columns), BF16)] * blocks

    later = [block for swapped in there[1:] for block in blocks_of(swapped, width)]

    router_t = router[0].T
    routes_f, routes_b = forward_routes[0].T, backward_routes[0].T
    arrived_f = from_behind(forward_sent[0], "section", 1)
    arrived_b = from_behind(backward_sent[0], "section", -1)
    row_shape = shape((count, width), BF16)
    table, embedded_held, loss_held, gain_held = call(
        functools.partial(table_kernel, sizes),
        (shape((moved, 2 * count), BF16), row_shape, row_shape, shape((1, width), BF16)),
        (4 * moved * count, 4 * (2 * count + moved) * width),
        in_specs=[VMEM] * 6,
    )(embedded, loss_gradient, norm_gain, routes_f, routes_b, columns)
    given = (arrived_f, arrived_b, embedded_held, loss_held, gain_held)
    send = call(
        first_send_kernel,
        tuple(blocks_of(there[0], width)),
        (4 * moved * count * width, 2 * (4 * count + moved) * width),
        in_specs=[VMEM] * 6,
    )(*given, table)
    mixing_shapes = [
        shape((count, moved), BF16),
        shape((count, moved), BF16),
        shape((top, moved, count), BF16),
    ]
    tokens, upstream, shares_b, *rest = call(
        functools.partial(mixing_kernel, sizes),
        (
            row_shape,
            row_shape,
            shape((top, 8, count), F32),
            *mixing_shapes * parts,
            *later,
        ),
        (4 * moved * count * width, 2 * (8 * count + moved) * width),
        vmem=LARGE_VMEM,
        in_specs=[VMEM] * 10,
    )(
        arrived_f, arrived_b, embedded, loss_gradient, norm_gain, routes_f, routes_b, columns,
        saved_inputs[0], router_t,
    )
    mixing = [rest[3 * part : 3 * part + 3] for part in range(parts)]
    sends = rest[3 * parts :]
    saved_pre = jnp.transpose(pre_activation[0], (1, 0, 2, 3)).reshape(local, rows, hidden)
    saved_pre = jnp.pad(saved_pre, ((0, 0), (0, padded - rows), (0, 0)))
    backs = []
    got = exchange(send)
    for part in range(parts):
        if part + 1 < parts:
            got = [got[d] for d in far_first(len(got))]
            sends, saved_pre, got = lax.optimization_barrier((sends, saved_pre, got))
            got = by_block(got)
            blocks = len(blocks_of(there[part + 1], width))
            coming = exchange(sends[:blocks])
            sends = sends[blocks:]
        result = blocks_of(back[part], width + LANES)
        done = call(
            functools.partial(expert_kernel, sizes, part, held),
            tuple(result),
            (8 * held * padded * width * hidden, 4 * held * width * hidden),
            vmem=EXPERT_VMEM,
            in_specs=[HBM] * 3 + [VMEM] * len(got),
            out_specs=(VMEM,) * len(result),
            scratch_shapes=[
                pltpu.VMEM((2 * held * padded, width), BF16),
                pltpu.VMEM((2 * held * padded, width + LANES), BF16),
                pltpu.VMEM((held, padded, hidden), BF16),
                pltpu.VMEM((min(2, held), width, hidden), BF16),
                pltpu.VMEM((min(2, held), hidden, width), BF16),
                pltpu.SemaphoreType.DMA,
                pltpu.SemaphoreType.DMA((min(2, held), 2, 2)),
            ],
        )(saved_pre, up_weight, down_weight, *[got[d] for d in far_first(len(got))])
        backs.append(exchange(list(done)))
        got = coming if part + 1 < parts else None
    handed = (
        saved_inputs[0], upstream, norm_gain, router_t, routes_b, shares_b,
    )
    own = (*mixing[-1], backs[-1][0]) if back[-1] else ()
    early = call(
        functools.partial(early_kernel, sizes, len(handed)),
        (
            shape((count, width), F32),
            shape((count, width), F32),
            shape((top, 8, count), F32),
            *[shape(array.shape, array.dtype) for array in handed],
        ),
        (4 * moved * count * width, 2 * (10 * count + moved) * width),
    )(tokens, *handed, *[ref for part in range(parts - 1) for ref in (*mixing[part], *backs[part])], *own)
    return tuple(
        call(
            functools.partial(late_kernel, sizes),
            (shape((1, count, width), BF16),) * 2,
            (4 * moved * count * width, 2 * (8 * count + moved) * width),
        )(
            *early,
            *mixing[-1],
            *[backs[-1][d] for d in far_first(len(backs[-1])) if d > 0 or not back[-1]],
        )
    )


def solution(mesh):
    return jax.shard_map(
        on_device,
        mesh=mesh,
        in_specs=(
            P("section", "expert", None),
            P("expert", None),
            P("section", "expert", None),
            P("section", "expert", None),
            P("expert", None),
            P("section", "expert", None),
            P("section", "expert", None),
            P("section", None, "expert", None, None),
            P("section", None),
            P("section", None, None),
            P("expert", None, None),
            P("expert", None, None),
        ),
        out_specs=(P("section", "expert", None), P("section", "expert", None)),
        check_vma=False,
    )
```

```python
import functools

import jax
import jax.numpy as jnp
import numpy as np
from jax import lax
from jax.experimental import pallas as pl
from jax.experimental.pallas import tpu as pltpu
from jax.sharding import PartitionSpec as P

EPS = 1e-06
BF16 = jnp.bfloat16
F32 = jnp.float32
LANES = 128
ROWS = 16
SMALL_VMEM = 16 * 1024 * 1024
EXPERT_VMEM = 28 * 1024 * 1024
LARGE_VMEM = 60 * 1024 * 1024
NT = (((1,), (1,)), ((), ()))
TN = (((0,), (0,)), ((), ()))


def dot(a, b, dims=(((1,), (0,)), ((), ()))):
    return lax.dot_general(a, b, dims, preferred_element_type=F32)


def call(kernel, out_shape, cost, vmem=SMALL_VMEM, **kwargs):
    flops, moved = cost
    return pl.pallas_call(
        kernel,
        out_shape=out_shape,
        compiler_params=pltpu.CompilerParams(vmem_limit_bytes=vmem),
        cost_estimate=pl.CostEstimate(flops=flops, bytes_accessed=moved, transcendentals=0),
        **kwargs,
    )


VMEM = pl.BlockSpec(memory_space=pltpu.VMEM)
HBM = pl.BlockSpec(memory_space=pl.ANY)


def from_behind(block, axis, distance):
    devices = range(lax.axis_size(axis))
    route = [(i - distance, i) for i in devices if i - distance in devices]
    return lax.ppermute(block, axis, route)


def start_order(size):
    near = [d for d in (1, 2) if d < max(2, size // 2)] if size > 1 else []
    far = [d for d in range(max(2, size // 2), size)]
    return near + far + [d for d in range(3, size // 2)] + [0]


def by_block(refs):
    ordered = [None] * len(refs)
    for ref, d in zip(refs, start_order(len(refs))):
        ordered[d] = ref
    return ordered


def exchange(blocks):
    size = lax.axis_size("expert")
    if len(blocks) == 1:
        return [lax.all_to_all(blocks[0], "expert", split_axis=0, concat_axis=0, tiled=True)]
    got = list(blocks)
    for d in start_order(size)[:-1]:
        got[d] = lax.ppermute(blocks[d], "expert", [(i, i ^ d) for i in range(size)])
    return got


def joined(refs):
    if len(refs) == 1:
        return refs[0][...]
    blocks = [ref[...].astype(F32) if ref is not None else None for ref in refs]
    empty = jnp.zeros_like(next(block for block in blocks if block is not None))
    return jnp.concatenate([empty if b is None else b for b in blocks], axis=0).astype(BF16)


def parted(value, refs):
    share = value.shape[0] // len(refs)
    for d, ref in enumerate(refs):
        ref[...] = value[d * share : (d + 1) * share].astype(BF16)


def partners(block, swapped):
    return lax.bitwise_xor(block, jnp.full_like(block, lax.axis_index("expert"))) if swapped else block


def expert_hits(routes, experts):
    top, count = routes.shape
    lane = lax.broadcasted_iota(jnp.int32, (experts, count), 0)
    return [(routes[k : k + 1, :] == lane).astype(F32) for k in range(top)]


def slot_targets(routes, experts, capacity):
    top, count = routes.shape
    hits = expert_hits(routes, experts)
    earlier = lax.broadcasted_iota(jnp.int32, (count, count), 0) < lax.broadcasted_iota(
        jnp.int32, (count, count), 1
    )
    before = dot(sum(hits).astype(BF16), earlier.astype(F32).astype(BF16))
    targets = []
    for k in range(top):
        ranked = jnp.sum((before + sum(hits[:k], jnp.zeros_like(before))) * hits[k], 0, keepdims=True)
        targets.append(routes[k : k + 1, :] * capacity + ranked.astype(jnp.int32))
    return targets, hits


def tables_of(targets, row_keys):
    return [(row_keys == target).astype(F32) for target in targets]


def normalise(tokens, gain):
    widened = tokens.astype(F32)
    inv_rms = lax.rsqrt(jnp.mean(widened * widened, axis=-1, keepdims=True) + EPS)
    return widened, inv_rms, (widened * inv_rms * gain.astype(F32)).astype(BF16)


def route_shares(normed, router, hits):
    logits = dot(router, normed, NT)
    exponents = [jnp.exp(jnp.sum(logits * hit, axis=0, keepdims=True)) for hit in hits]
    total = sum(exponents)
    return [exponent / total for exponent in exponents]


def keys_of_part(sizes, columns, part, swapped):
    device = partners(columns[:, 0:1], swapped)
    return columns[:, 2 + part : 3 + part] + device * sizes["share"]


def rows_to_send(arrived_f, arrived_b, embedded, loss, gain):
    section = lax.axis_index("section")
    last = lax.axis_size("section") - 1
    tokens = jnp.where(section == 0, embedded[...], arrived_f[...])
    upstream = jnp.where(section == last, loss[...], arrived_b[...])
    return tokens, normalise(tokens, gain[...])[2], upstream


def table_kernel(
    sizes, embedded, loss, gain, routes_f, routes_b, columns,
    table, embedded_out, loss_out, gain_out,
):
    experts, capacity = sizes["experts"], sizes["capacity"]
    targets_f, _ = slot_targets(routes_f[...], experts, capacity)
    targets_b, _ = slot_targets(routes_b[...], experts, capacity)
    keys = keys_of_part(sizes, columns, 0, sizes["there"][0])
    table_f = sum(tables_of(targets_f, keys))
    table_b = sum(tables_of([t + experts * capacity for t in targets_b], keys))
    table[...] = jnp.concatenate([table_f, table_b], axis=1).astype(BF16)
    embedded_out[...] = embedded[...]
    loss_out[...] = loss[...]
    gain_out[...] = gain[...]


def first_send_kernel(arrived_f, arrived_b, embedded, loss, gain, table, *send):
    _, normed, upstream = rows_to_send(arrived_f, arrived_b, embedded, loss, gain)
    parted(dot(table[...], jnp.concatenate([normed, upstream], axis=0)), send)


def mixing_kernel(
    sizes, arrived_f, arrived_b, embedded, loss, gain, routes_f, routes_b, columns,
    saved, router, tokens, upstream, shares_b, *refs,
):
    experts, capacity = sizes["experts"], sizes["capacity"]
    parts = len(sizes["back"])
    mixing, sends = refs[: 3 * parts], refs[3 * parts :]
    tokens[...], normed, upstream[...] = rows_to_send(
        arrived_f, arrived_b, embedded, loss, gain
    )
    data = jnp.concatenate([normed, upstream[...]], axis=0)
    targets_f, hits = slot_targets(routes_f[...], experts, capacity)
    shares_f = route_shares(normed, router[...], hits)
    targets_b, hits = slot_targets(routes_b[...], experts, capacity)
    targets_b = [t + experts * capacity for t in targets_b]
    own_shares = route_shares(normalise(saved[...], gain[...])[2], router[...], hits)
    for k, share in enumerate(own_shares):
        shares_b[k] = jnp.broadcast_to(share, shares_b.shape[1:])
    for part in range(parts):
        there, back = sizes["there"][part], sizes["back"][part]
        mixing_f, mixing_b, tables_b = mixing[3 * part : 3 * part + 3]
        keys = keys_of_part(sizes, columns, part, back)
        found_f, found_b = tables_of(targets_f, keys), tables_of(targets_b, keys)
        for out, found, shares in ((mixing_f, found_f, shares_f), (mixing_b, found_b, own_shares)):
            mixed = sum(t * s.astype(BF16).astype(F32) for t, s in zip(found, shares))
            out[...] = jnp.transpose(mixed).astype(BF16)
        for k, table in enumerate(found_b):
            tables_b[k] = table.astype(BF16)
        if part > 0:
            if there != back:
                keys = keys_of_part(sizes, columns, part, there)
                found_f, found_b = tables_of(targets_f, keys), tables_of(targets_b, keys)
            blocks = sizes["sources"] if there else 1
            table = jnp.concatenate([sum(found_f), sum(found_b)], axis=1).astype(BF16)
            parted(dot(table, data), sends[:blocks])
            sends = sends[blocks:]


def row_order(sizes, swapped, shape, axis):
    line = tuple(size if i == axis else 1 for i, size in enumerate(shape))
    row = lax.broadcasted_iota(jnp.int32, line, axis)
    block = sum(
        (row >= k * sizes["block_rows"]).astype(jnp.int32) for k in range(1, sizes["sources"])
    )
    within = row - block * sizes["block_rows"]
    group = sum(
        (within >= k * sizes["capacity"]).astype(jnp.int32)
        for k in range(1, sizes["block_rows"] // sizes["capacity"])
    )
    source = partners(block, swapped)
    place = group * (sizes["padded"] - sizes["capacity"]) + source * sizes["capacity"] + within
    return (place == lax.broadcasted_iota(jnp.int32, shape, 1 - axis)).astype(F32).astype(BF16)


def expert_kernel(sizes, part, held, saved_all, up, down, *refs):
    there, back = sizes["there"][part], sizes["back"][part]
    blocks = sizes["sources"] if there else 1
    got, out = by_block(refs[:blocks]), refs[blocks:-7]
    rows, results, saved_pre, up_held, down_held, saved_sem, sems = refs[-7:]
    moved = blocks * got[0].shape[0]
    width = rows.shape[1]
    slots, halves = sems.shape[:2]
    half = up.shape[2] // halves
    padded = sizes["padded"]

    def copies(expert, piece):
        slot = lax.rem(expert, slots)
        piece_of = pl.ds(piece * half, half)
        return [
            pltpu.make_async_copy(
                up.at[part * held + expert, :, piece_of],
                up_held.at[slot, :, piece_of],
                sems.at[slot, piece, 0],
            ),
            pltpu.make_async_copy(
                down.at[part * held + expert, piece_of, :],
                down_held.at[slot, piece_of, :],
                sems.at[slot, piece, 1],
            ),
        ]

    for expert in range(min(slots, held)):
        for piece in range(halves):
            for copy in copies(jnp.int32(expert), piece):
                copy.start()

        if expert == 0:
            saved_copy = pltpu.make_async_copy(
                saved_all.at[pl.ds(part * held, held)], saved_pre, saved_sem
            )
            saved_copy.start()

    order = row_order(sizes, there, (rows.shape[0], moved), 1)
    rows[...] = dot(order, joined(got)).astype(BF16)
    results[:, width:] = jnp.zeros((results.shape[0], results.shape[1] - width), BF16)

    saved_copy.wait()

    def one_expert(expert, carry):
        slot = lax.rem(expert, slots)
        own_f = pl.ds(pl.multiple_of(expert * padded, ROWS), padded)
        own_b = pl.ds(pl.multiple_of((held + expert) * padded, ROWS), padded)
        hidden, pre_grad, inner = [], [], 0.0
        for piece in range(halves):
            for copy in copies(expert, piece):
                copy.wait()
            span = slice(piece * half, (piece + 1) * half)
            pre_act = dot(rows[own_f, :], up_held[slot, :, span])
            hidden_grad = dot(rows[own_b, :], down_held[slot, span, :], NT)
            hidden.append((pre_act / (1.0 + jnp.exp(-pre_act))).astype(BF16))
            pre = saved_pre[expert, :, span].astype(F32)
            gate = 1.0 / (1.0 + jnp.exp(-pre))
            inner += jnp.sum(
                hidden_grad * (pre * gate).astype(BF16).astype(F32), axis=1, keepdims=True
            )
            pre_grad.append((hidden_grad * gate * (1.0 + pre * (1.0 - gate))).astype(BF16))
        result_f = dot(jnp.concatenate(hidden, axis=1), down_held[slot])
        result_b = dot(jnp.concatenate(pre_grad, axis=1), up_held[slot], NT)
        results[own_f, :width] = result_f.astype(BF16)
        results[own_b, :width] = result_b.astype(BF16)
        results[own_b, width:] = jnp.broadcast_to(inner, (padded, LANES)).astype(BF16)

        @pl.when(expert + slots < held)
        def _():
            for piece in range(halves):
                for copy in copies(expert + slots, piece):
                    copy.start()

        return carry

    lax.fori_loop(0, held, one_expert, 0)
    order = row_order(sizes, back, (moved, rows.shape[0]), 0)
    parted(dot(order, results[...]), out)


def add_up(blocks, mixing_f, mixing_b, tables):
    back = joined(blocks)
    width = back.shape[1] - LANES
    sums = back[:, width:].astype(F32)[:, :1]
    return (
        dot(mixing_f[...], back[:, :width]),
        dot(mixing_b[...], back[:, :width]),
        [jnp.sum(tables[k].astype(F32) * sums, axis=0, keepdims=True) for k in range(tables.shape[0])],
    )


def early_kernel(sizes, handed, tokens, *refs):
    output, gradient, inner, *copies = refs[-3 - handed :]
    for given, copied in zip(refs, copies):
        copied[...] = given[...]
    refs = refs[handed : -3 - handed]
    own = None
    if sizes["back"][-1]:
        refs, own = refs[:-4], refs[-4:]
    sum_f, sum_b, sums = tokens[...].astype(F32), None, None
    for swapped in sizes["back"][:-1]:
        blocks = sizes["sources"] if swapped else 1
        more_f, more_b, more = add_up(refs[3 : 3 + blocks], *refs[:3])
        refs = refs[3 + blocks :]
        sum_f += more_f
        sum_b = more_b if sum_b is None else sum_b + more_b
        sums = more if sums is None else [a + b for a, b in zip(sums, more)]
    if own is not None:
        blocks = [own[3]] + [None] * (sizes["sources"] - 1)
        more_f, more_b, more = add_up(blocks, *own[:3])
        sum_f += more_f
        sum_b = more_b if sum_b is None else sum_b + more_b
        sums = more if sums is None else [a + b for a, b in zip(sums, more)]
    output[...] = sum_f
    if sums is None:
        gradient[...] = jnp.zeros(gradient.shape, F32)
        inner[...] = jnp.zeros(inner.shape, F32)
    else:
        gradient[...] = sum_b
        for k, row in enumerate(sums):
            inner[k] = jnp.broadcast_to(row, inner.shape[1:])


def late_kernel(
    sizes, early_f, early_b, early_inner, saved, upstream, gain, router, routes, shares,
    mixing_f, mixing_b, tables, *refs,
):
    *backs, output, gradient = refs
    if sizes["back"][-1]:
        backs = by_block(backs + [None])
    more_f, more_b, more = add_up(backs, mixing_f, mixing_b, tables)
    widened = saved[...].astype(F32)
    inv_rms = lax.rsqrt(jnp.mean(widened * widened, axis=-1, keepdims=True) + EPS)
    hits = expert_hits(routes[...], sizes["experts"])
    top = len(hits)
    share = [shares[k][:1, :] for k in range(top)]
    inner = [early_inner[k][:1, :] + more[k] for k in range(top)]
    mean = sum(share[k] * inner[k] for k in range(top))
    logit_grad = sum(share[k] * (inner[k] - mean) * hits[k] for k in range(top))
    high = logit_grad.astype(BF16)
    rest = logit_grad - high.astype(F32)
    middle = rest.astype(BF16)
    low = (rest - middle.astype(F32)).astype(BF16)
    output[0] = (early_f[...] + more_f).astype(BF16)
    normed_grad = early_b[...] + more_b
    for piece in (high, middle, low):
        normed_grad += dot(piece, router[...], TN)
    gained = normed_grad * gain[...].astype(F32)
    projected = jnp.mean(widened * gained, axis=-1, keepdims=True)
    grad = inv_rms * gained - widened * (inv_rms * inv_rms * inv_rms * projected)
    gradient[0] = (upstream[...].astype(F32) + grad).astype(BF16)


def exchange_columns(parts, sources, local, capacity):
    held = local // parts
    slots = sources * local * capacity
    block_rows = 2 * held * capacity
    columns = np.zeros((sources * block_rows, 2 + parts), np.int32)
    for source in range(sources):
        for batch in range(2):
            for expert in range(held):
                for slot in range(capacity):
                    within = (batch * held + expert) * capacity + slot
                    row = source * block_rows + within
                    columns[row, :2] = source, within
                    for part in range(parts):
                        own = (part * held + expert) * capacity + slot
                        columns[row, 2 + part] = batch * slots + own
    return columns


def on_device(
    forward_sent,
    embedded,
    forward_routes,
    backward_sent,
    loss_gradient,
    saved_inputs,
    backward_routes,
    pre_activation,
    norm_gain,
    router,
    up_weight,
    down_weight,
):
    sources = lax.axis_size("expert")
    experts = router.shape[2]
    capacity = pre_activation.shape[3]
    local, width, hidden = up_weight.shape
    count = embedded.shape[0]
    top = forward_routes.shape[2]
    slots = experts * capacity
    rows = sources * capacity
    padded = -(-rows // ROWS) * ROWS
    shape = jax.ShapeDtypeStruct
    parts = 2 if local % 2 == 0 else 1
    held = local // parts
    moved = 2 * slots // parts
    few = sources in (2, 4, 8)
    there = [few and part == 0 for part in range(parts)]
    back = [few and part == parts - 1 for part in range(parts)]
    columns = exchange_columns(parts, sources, local, capacity)
    sizes = {
        "experts": experts,
        "capacity": capacity,
        "sources": sources,
        "share": local * capacity,
        "there": there,
        "back": back,
        "padded": padded,
        "block_rows": moved // sources,
    }

    def blocks_of(swapped, columns):
        blocks = sources if swapped else 1
        return [shape((moved // blocks, columns), BF16)] * blocks

    later = [block for swapped in there[1:] for block in blocks_of(swapped, width)]

    router_t = router[0].T
    routes_f, routes_b = forward_routes[0].T, backward_routes[0].T
    arrived_f = from_behind(forward_sent[0], "section", 1)
    arrived_b = from_behind(backward_sent[0], "section", -1)
    row_shape = shape((count, width), BF16)
    table, embedded_held, loss_held, gain_held = call(
        functools.partial(table_kernel, sizes),
        (shape((moved, 2 * count), BF16), row_shape, row_shape, shape((1, width), BF16)),
        (4 * moved * count, 4 * (2 * count + moved) * width),
        in_specs=[VMEM] * 6,
    )(embedded, loss_gradient, norm_gain, routes_f, routes_b, columns)
    given = (arrived_f, arrived_b, embedded_held, loss_held, gain_held)
    send = call(
        first_send_kernel,
        tuple(blocks_of(there[0], width)),
        (4 * moved * count * width, 2 * (4 * count + moved) * width),
        in_specs=[VMEM] * 6,
    )(*given, table)
    mixing_shapes = [
        shape((count, moved), BF16),
        shape((count, moved), BF16),
        shape((top, moved, count), BF16),
    ]
    tokens, upstream, shares_b, *rest = call(
        functools.partial(mixing_kernel, sizes),
        (
            row_shape,
            row_shape,
            shape((top, 8, count), F32),
            *mixing_shapes * parts,
            *later,
        ),
        (4 * moved * count * width, 2 * (8 * count + moved) * width),
        vmem=LARGE_VMEM,
        in_specs=[VMEM] * 10,
    )(
        arrived_f, arrived_b, embedded, loss_gradient, norm_gain, routes_f, routes_b, columns,
        saved_inputs[0], router_t,
    )
    mixing = [rest[3 * part : 3 * part + 3] for part in range(parts)]
    sends = rest[3 * parts :]
    saved_pre = jnp.transpose(pre_activation[0], (1, 0, 2, 3)).reshape(local, rows, hidden)
    saved_pre = jnp.pad(saved_pre, ((0, 0), (0, padded - rows), (0, 0)))
    backs = []
    got = exchange(send)
    for part in range(parts):
        if part + 1 < parts:
            got = [got[d] for d in start_order(len(got))]
            sends, saved_pre, got = lax.optimization_barrier((sends, saved_pre, got))
            got = by_block(got)
            blocks = len(blocks_of(there[part + 1], width))
            coming = exchange(sends[:blocks])
            sends = sends[blocks:]
        result = blocks_of(back[part], width + LANES)
        done = call(
            functools.partial(expert_kernel, sizes, part, held),
            tuple(result),
            (8 * held * padded * width * hidden, 4 * held * width * hidden),
            vmem=EXPERT_VMEM,
            in_specs=[HBM] * 3 + [VMEM] * len(got),
            out_specs=(VMEM,) * len(result),
            scratch_shapes=[
                pltpu.VMEM((2 * held * padded, width), BF16),
                pltpu.VMEM((2 * held * padded, width + LANES), BF16),
                pltpu.VMEM((held, padded, hidden), BF16),
                pltpu.VMEM((min(2, held), width, hidden), BF16),
                pltpu.VMEM((min(2, held), hidden, width), BF16),
                pltpu.SemaphoreType.DMA,
                pltpu.SemaphoreType.DMA((min(2, held), 2, 2)),
            ],
        )(saved_pre, up_weight, down_weight, *[got[d] for d in start_order(len(got))])
        backs.append(exchange(list(done)))
        got = coming if part + 1 < parts else None
    handed = (
        saved_inputs[0], upstream, norm_gain, router_t, routes_b, shares_b,
    )
    own = (*mixing[-1], backs[-1][0]) if back[-1] else ()
    early = call(
        functools.partial(early_kernel, sizes, len(handed)),
        (
            shape((count, width), F32),
            shape((count, width), F32),
            shape((top, 8, count), F32),
            *[shape(array.shape, array.dtype) for array in handed],
        ),
        (4 * moved * count * width, 2 * (10 * count + moved) * width),
    )(tokens, *handed, *[ref for part in range(parts - 1) for ref in (*mixing[part], *backs[part])], *own)
    return tuple(
        call(
            functools.partial(late_kernel, sizes),
            (shape((1, count, width), BF16),) * 2,
            (4 * moved * count * width, 2 * (8 * count + moved) * width),
        )(
            *early,
            *mixing[-1],
            *[backs[-1][d] for d in start_order(len(backs[-1])) if d > 0 or not back[-1]],
        )
    )


def solution(mesh):
    return jax.shard_map(
        on_device,
        mesh=mesh,
        in_specs=(
            P("section", "expert", None),
            P("expert", None),
            P("section", "expert", None),
            P("section", "expert", None),
            P("expert", None),
            P("section", "expert", None),
            P("section", "expert", None),
            P("section", None, "expert", None, None),
            P("section", None),
            P("section", None, None),
            P("expert", None, None),
            P("expert", None, None),
        ),
        out_specs=(P("section", "expert", None), P("section", "expert", None)),
        check_vma=False,
    )
```

```python
import functools

import jax
import jax.numpy as jnp
import numpy as np
from jax import lax
from jax.experimental import pallas as pl
from jax.experimental.pallas import tpu as pltpu
from jax.sharding import PartitionSpec as P

EPS = 1e-06
BF16 = jnp.bfloat16
F32 = jnp.float32
LANES = 128
ROWS = 16
SMALL_VMEM = 16 * 1024 * 1024
EXPERT_VMEM = 28 * 1024 * 1024
LARGE_VMEM = 60 * 1024 * 1024
NT = (((1,), (1,)), ((), ()))
TN = (((0,), (0,)), ((), ()))


def dot(a, b, dims=(((1,), (0,)), ((), ()))):
    return lax.dot_general(a, b, dims, preferred_element_type=F32)


def call(kernel, out_shape, cost, vmem=SMALL_VMEM, **kwargs):
    flops, moved = cost
    return pl.pallas_call(
        kernel,
        out_shape=out_shape,
        compiler_params=pltpu.CompilerParams(vmem_limit_bytes=vmem),
        cost_estimate=pl.CostEstimate(flops=flops, bytes_accessed=moved, transcendentals=0),
        **kwargs,
    )


VMEM = pl.BlockSpec(memory_space=pltpu.VMEM)
HBM = pl.BlockSpec(memory_space=pl.ANY)


def from_behind(block, axis, distance):
    devices = range(lax.axis_size(axis))
    route = [(i - distance, i) for i in devices if i - distance in devices]
    return lax.ppermute(block, axis, route)


def start_order(size):
    near = [d for d in (1, 2) if d < max(2, size // 2)] if size > 1 else []
    far = [d for d in range(max(2, size // 2), size)]
    return near + far + [d for d in range(3, size // 2)] + [0]


def by_block(refs):
    ordered = [None] * len(refs)
    for ref, d in zip(refs, start_order(len(refs))):
        ordered[d] = ref
    return ordered


def exchange(blocks):
    size = lax.axis_size("expert")
    if len(blocks) == 1:
        return [lax.all_to_all(blocks[0], "expert", split_axis=0, concat_axis=0, tiled=True)]
    got = list(blocks)
    for d in start_order(size)[:-1]:
        got[d] = lax.ppermute(blocks[d], "expert", [(i, i ^ d) for i in range(size)])
    return got


def joined(refs):
    if len(refs) == 1:
        return refs[0][...]
    blocks = [ref[...].astype(F32) if ref is not None else None for ref in refs]
    empty = jnp.zeros_like(next(block for block in blocks if block is not None))
    return jnp.concatenate([empty if b is None else b for b in blocks], axis=0).astype(BF16)


def parted(value, refs):
    share = value.shape[0] // len(refs)
    for d, ref in enumerate(refs):
        ref[...] = value[d * share : (d + 1) * share].astype(BF16)


def partners(block, swapped):
    return lax.bitwise_xor(block, jnp.full_like(block, lax.axis_index("expert"))) if swapped else block


def expert_hits(routes, experts):
    top, count = routes.shape
    lane = lax.broadcasted_iota(jnp.int32, (experts, count), 0)
    return [(routes[k : k + 1, :] == lane).astype(F32) for k in range(top)]


def slot_targets(routes, experts, capacity):
    top, count = routes.shape
    hits = expert_hits(routes, experts)
    earlier = lax.broadcasted_iota(jnp.int32, (count, count), 0) < lax.broadcasted_iota(
        jnp.int32, (count, count), 1
    )
    before = dot(sum(hits).astype(BF16), earlier.astype(F32).astype(BF16))
    targets = []
    for k in range(top):
        ranked = jnp.sum((before + sum(hits[:k], jnp.zeros_like(before))) * hits[k], 0, keepdims=True)
        targets.append(routes[k : k + 1, :] * capacity + ranked.astype(jnp.int32))
    return targets, hits


def tables_of(targets, row_keys):
    return [(row_keys == target).astype(F32) for target in targets]


def normalise(tokens, gain):
    widened = tokens.astype(F32)
    inv_rms = lax.rsqrt(jnp.mean(widened * widened, axis=-1, keepdims=True) + EPS)
    return widened, inv_rms, (widened * inv_rms * gain.astype(F32)).astype(BF16)


def route_shares(normed, router, hits):
    logits = dot(router, normed, NT)
    exponents = [jnp.exp(jnp.sum(logits * hit, axis=0, keepdims=True)) for hit in hits]
    total = sum(exponents)
    return [exponent / total for exponent in exponents]


def keys_of_part(sizes, columns, part, swapped):
    device = partners(columns[:, 0:1], swapped)
    return columns[:, 2 + part : 3 + part] + device * sizes["share"]


def rows_to_send(arrived_f, arrived_b, embedded, loss, gain):
    section = lax.axis_index("section")
    last = lax.axis_size("section") - 1
    tokens = jnp.where(section == 0, embedded[...], arrived_f[...])
    upstream = jnp.where(section == last, loss[...], arrived_b[...])
    return tokens, normalise(tokens, gain[...])[2], upstream


def table_kernel(
    sizes, embedded, loss, gain, routes_f, routes_b, columns,
    table, embedded_out, loss_out, gain_out,
):
    experts, capacity = sizes["experts"], sizes["capacity"]
    targets_f, _ = slot_targets(routes_f[...], experts, capacity)
    targets_b, _ = slot_targets(routes_b[...], experts, capacity)
    keys = keys_of_part(sizes, columns, 0, sizes["there"][0])
    table_f = sum(tables_of(targets_f, keys))
    table_b = sum(tables_of([t + experts * capacity for t in targets_b], keys))
    table[...] = jnp.concatenate([table_f, table_b], axis=1).astype(BF16)
    embedded_out[...] = embedded[...]
    loss_out[...] = loss[...]
    gain_out[...] = gain[...]


def first_send_kernel(arrived_f, arrived_b, embedded, loss, gain, table, *send):
    _, normed, upstream = rows_to_send(arrived_f, arrived_b, embedded, loss, gain)
    parted(dot(table[...], jnp.concatenate([normed, upstream], axis=0)), send)


def mixing_kernel(
    sizes, arrived_f, arrived_b, embedded, loss, gain, routes_f, routes_b, columns,
    saved, router, tokens, upstream, shares_b, *refs,
):
    experts, capacity = sizes["experts"], sizes["capacity"]
    parts = len(sizes["back"])
    mixing, sends = refs[: 3 * parts], refs[3 * parts :]
    tokens[...], normed, upstream[...] = rows_to_send(
        arrived_f, arrived_b, embedded, loss, gain
    )
    data = jnp.concatenate([normed, upstream[...]], axis=0)
    targets_f, hits = slot_targets(routes_f[...], experts, capacity)
    shares_f = route_shares(normed, router[...], hits)
    targets_b, hits = slot_targets(routes_b[...], experts, capacity)
    targets_b = [t + experts * capacity for t in targets_b]
    own_shares = route_shares(normalise(saved[...], gain[...])[2], router[...], hits)
    for k, share in enumerate(own_shares):
        shares_b[k] = jnp.broadcast_to(share, shares_b.shape[1:])
    for part in range(parts):
        there, back = sizes["there"][part], sizes["back"][part]
        mixing_f, mixing_b, tables_b = mixing[3 * part : 3 * part + 3]
        keys = keys_of_part(sizes, columns, part, back)
        found_f, found_b = tables_of(targets_f, keys), tables_of(targets_b, keys)
        for out, found, shares in ((mixing_f, found_f, shares_f), (mixing_b, found_b, own_shares)):
            mixed = sum(t * s.astype(BF16).astype(F32) for t, s in zip(found, shares))
            out[...] = jnp.transpose(mixed).astype(BF16)
        for k, table in enumerate(found_b):
            tables_b[k] = table.astype(BF16)
        if part > 0:
            if there != back:
                keys = keys_of_part(sizes, columns, part, there)
                found_f, found_b = tables_of(targets_f, keys), tables_of(targets_b, keys)
            blocks = sizes["sources"] if there else 1
            table = jnp.concatenate([sum(found_f), sum(found_b)], axis=1).astype(BF16)
            parted(dot(table, data), sends[:blocks])
            sends = sends[blocks:]


def row_order(sizes, swapped, shape, axis):
    line = tuple(size if i == axis else 1 for i, size in enumerate(shape))
    row = lax.broadcasted_iota(jnp.int32, line, axis)
    block = sum(
        (row >= k * sizes["block_rows"]).astype(jnp.int32) for k in range(1, sizes["sources"])
    )
    within = row - block * sizes["block_rows"]
    group = sum(
        (within >= k * sizes["capacity"]).astype(jnp.int32)
        for k in range(1, sizes["block_rows"] // sizes["capacity"])
    )
    source = partners(block, swapped)
    place = group * (sizes["padded"] - sizes["capacity"]) + source * sizes["capacity"] + within
    return (place == lax.broadcasted_iota(jnp.int32, shape, 1 - axis)).astype(F32).astype(BF16)


def expert_kernel(sizes, part, held, saved_all, up, down, *refs):
    there, back = sizes["there"][part], sizes["back"][part]
    blocks = sizes["sources"] if there else 1
    got, out = by_block(refs[:blocks]), refs[blocks:-7]
    rows, results, saved_pre, up_held, down_held, saved_sem, sems = refs[-7:]
    moved = blocks * got[0].shape[0]
    width = rows.shape[1]
    slots, halves = sems.shape[:2]
    half = up.shape[2] // halves
    padded = sizes["padded"]

    def copies(expert, piece):
        slot = lax.rem(expert, slots)
        piece_of = pl.ds(piece * half, half)
        return [
            pltpu.make_async_copy(
                up.at[part * held + expert, :, piece_of],
                up_held.at[slot, :, piece_of],
                sems.at[slot, piece, 0],
            ),
            pltpu.make_async_copy(
                down.at[part * held + expert, piece_of, :],
                down_held.at[slot, piece_of, :],
                sems.at[slot, piece, 1],
            ),
        ]

    for expert in range(min(slots, held)):
        for piece in range(halves):
            for copy in copies(jnp.int32(expert), piece):
                copy.start()

        if expert == 0:
            saved_copy = pltpu.make_async_copy(
                saved_all.at[pl.ds(part * held, held)], saved_pre, saved_sem
            )
            saved_copy.start()

    order = row_order(sizes, there, (rows.shape[0], moved), 1)
    rows[...] = dot(order, joined(got)).astype(BF16)
    results[:, width:] = jnp.zeros((results.shape[0], results.shape[1] - width), BF16)

    saved_copy.wait()

    def one_expert(expert, carry):
        slot = lax.rem(expert, slots)
        own_f = pl.ds(pl.multiple_of(expert * padded, ROWS), padded)
        own_b = pl.ds(pl.multiple_of((held + expert) * padded, ROWS), padded)
        hidden, pre_grad, inner = [], [], 0.0
        for piece in range(halves):
            for copy in copies(expert, piece):
                copy.wait()
            span = slice(piece * half, (piece + 1) * half)
            pre_act = dot(rows[own_f, :], up_held[slot, :, span])
            hidden_grad = dot(rows[own_b, :], down_held[slot, span, :], NT)
            hidden.append((pre_act / (1.0 + jnp.exp(-pre_act))).astype(BF16))
            pre = saved_pre[expert, :, span].astype(F32)
            gate = 1.0 / (1.0 + jnp.exp(-pre))
            inner += jnp.sum(
                hidden_grad * (pre * gate).astype(BF16).astype(F32), axis=1, keepdims=True
            )
            pre_grad.append((hidden_grad * gate * (1.0 + pre * (1.0 - gate))).astype(BF16))
        result_f = dot(jnp.concatenate(hidden, axis=1), down_held[slot])
        result_b = dot(jnp.concatenate(pre_grad, axis=1), up_held[slot], NT)
        results[own_f, :width] = result_f.astype(BF16)
        results[own_b, :width] = result_b.astype(BF16)
        results[own_b, width:] = jnp.broadcast_to(inner, (padded, LANES)).astype(BF16)

        @pl.when(expert + slots < held)
        def _():
            for piece in range(halves):
                for copy in copies(expert + slots, piece):
                    copy.start()

        return carry

    lax.fori_loop(0, held, one_expert, 0)
    order = row_order(sizes, back, (moved, rows.shape[0]), 0)
    parted(dot(order, results[...]), out)


def add_up(blocks, mixing_f, mixing_b, tables):
    back = joined(blocks)
    width = back.shape[1] - LANES
    sums = back[:, width:].astype(F32)[:, :1]
    return (
        dot(mixing_f[...], back[:, :width]),
        dot(mixing_b[...], back[:, :width]),
        [jnp.sum(tables[k].astype(F32) * sums, axis=0, keepdims=True) for k in range(tables.shape[0])],
    )


def early_kernel(sizes, handed, tokens, *refs):
    output, gradient, inner, *copies = refs[-3 - handed :]
    for given, copied in zip(refs, copies):
        copied[...] = given[...]
    refs = refs[handed : -3 - handed]
    own = None
    if sizes["back"][-1]:
        refs, own = refs[:-4], refs[-4:]
    sum_f, sum_b, sums = tokens[...].astype(F32), None, None
    for swapped in sizes["back"][:-1]:
        blocks = sizes["sources"] if swapped else 1
        more_f, more_b, more = add_up(refs[3 : 3 + blocks], *refs[:3])
        refs = refs[3 + blocks :]
        sum_f += more_f
        sum_b = more_b if sum_b is None else sum_b + more_b
        sums = more if sums is None else [a + b for a, b in zip(sums, more)]
    if own is not None:
        blocks = [own[3]] + [None] * (sizes["sources"] - 1)
        more_f, more_b, more = add_up(blocks, *own[:3])
        sum_f += more_f
        sum_b = more_b if sum_b is None else sum_b + more_b
        sums = more if sums is None else [a + b for a, b in zip(sums, more)]
    output[...] = sum_f
    if sums is None:
        gradient[...] = jnp.zeros(gradient.shape, F32)
        inner[...] = jnp.zeros(inner.shape, F32)
    else:
        gradient[...] = sum_b
        for k, row in enumerate(sums):
            inner[k] = jnp.broadcast_to(row, inner.shape[1:])


def late_kernel(
    sizes, early_f, early_b, early_inner, upstream, gain, routes, shares, saved, router,
    mixing_f, mixing_b, tables, *refs,
):
    *backs, output, gradient = refs
    if sizes["back"][-1]:
        backs = by_block(backs + [None])
    more_f, more_b, more = add_up(backs, mixing_f, mixing_b, tables)
    widened = saved[...].astype(F32)
    inv_rms = lax.rsqrt(jnp.mean(widened * widened, axis=-1, keepdims=True) + EPS)
    hits = expert_hits(routes[...], sizes["experts"])
    top = len(hits)
    share = [shares[k][:1, :] for k in range(top)]
    inner = [early_inner[k][:1, :] + more[k] for k in range(top)]
    mean = sum(share[k] * inner[k] for k in range(top))
    logit_grad = sum(share[k] * (inner[k] - mean) * hits[k] for k in range(top))
    high = logit_grad.astype(BF16)
    rest = logit_grad - high.astype(F32)
    middle = rest.astype(BF16)
    low = (rest - middle.astype(F32)).astype(BF16)
    output[0] = (early_f[...] + more_f).astype(BF16)
    normed_grad = early_b[...] + more_b
    for piece in (high, middle, low):
        normed_grad += dot(piece, router[...], TN)
    gained = normed_grad * gain[...].astype(F32)
    projected = jnp.mean(widened * gained, axis=-1, keepdims=True)
    grad = inv_rms * gained - widened * (inv_rms * inv_rms * inv_rms * projected)
    gradient[0] = (upstream[...].astype(F32) + grad).astype(BF16)


def exchange_columns(parts, sources, local, capacity):
    held = local // parts
    slots = sources * local * capacity
    block_rows = 2 * held * capacity
    columns = np.zeros((sources * block_rows, 2 + parts), np.int32)
    for source in range(sources):
        for batch in range(2):
            for expert in range(held):
                for slot in range(capacity):
                    within = (batch * held + expert) * capacity + slot
                    row = source * block_rows + within
                    columns[row, :2] = source, within
                    for part in range(parts):
                        own = (part * held + expert) * capacity + slot
                        columns[row, 2 + part] = batch * slots + own
    return columns


def on_device(
    forward_sent,
    embedded,
    forward_routes,
    backward_sent,
    loss_gradient,
    saved_inputs,
    backward_routes,
    pre_activation,
    norm_gain,
    router,
    up_weight,
    down_weight,
):
    sources = lax.axis_size("expert")
    experts = router.shape[2]
    capacity = pre_activation.shape[3]
    local, width, hidden = up_weight.shape
    count = embedded.shape[0]
    top = forward_routes.shape[2]
    slots = experts * capacity
    rows = sources * capacity
    padded = -(-rows // ROWS) * ROWS
    shape = jax.ShapeDtypeStruct
    parts = 2 if local % 2 == 0 else 1
    held = local // parts
    moved = 2 * slots // parts
    few = sources in (2, 4, 8)
    there = [few and part == 0 for part in range(parts)]
    back = [few and part == parts - 1 for part in range(parts)]
    columns = exchange_columns(parts, sources, local, capacity)
    sizes = {
        "experts": experts,
        "capacity": capacity,
        "sources": sources,
        "share": local * capacity,
        "there": there,
        "back": back,
        "padded": padded,
        "block_rows": moved // sources,
    }

    def blocks_of(swapped, columns):
        blocks = sources if swapped else 1
        return [shape((moved // blocks, columns), BF16)] * blocks

    later = [block for swapped in there[1:] for block in blocks_of(swapped, width)]

    router_t = router[0].T
    routes_f, routes_b = forward_routes[0].T, backward_routes[0].T
    arrived_f = from_behind(forward_sent[0], "section", 1)
    arrived_b = from_behind(backward_sent[0], "section", -1)
    row_shape = shape((count, width), BF16)
    table, embedded_held, loss_held, gain_held = call(
        functools.partial(table_kernel, sizes),
        (shape((moved, 2 * count), BF16), row_shape, row_shape, shape((1, width), BF16)),
        (4 * moved * count, 4 * (2 * count + moved) * width),
        in_specs=[VMEM] * 6,
    )(embedded, loss_gradient, norm_gain, routes_f, routes_b, columns)
    given = (arrived_f, arrived_b, embedded_held, loss_held, gain_held)
    send = call(
        first_send_kernel,
        tuple(blocks_of(there[0], width)),
        (4 * moved * count * width, 2 * (4 * count + moved) * width),
        in_specs=[VMEM] * 6,
    )(*given, table)
    mixing_shapes = [
        shape((count, moved), BF16),
        shape((count, moved), BF16),
        shape((top, moved, count), BF16),
    ]
    tokens, upstream, shares_b, *rest = call(
        functools.partial(mixing_kernel, sizes),
        (
            row_shape,
            row_shape,
            shape((top, 8, count), F32),
            *mixing_shapes * parts,
            *later,
        ),
        (4 * moved * count * width, 2 * (8 * count + moved) * width),
        vmem=LARGE_VMEM,
        in_specs=[VMEM] * 10,
    )(
        arrived_f, arrived_b, embedded, loss_gradient, norm_gain, routes_f, routes_b, columns,
        saved_inputs[0], router_t,
    )
    mixing = [rest[3 * part : 3 * part + 3] for part in range(parts)]
    sends = rest[3 * parts :]
    saved_pre = jnp.transpose(pre_activation[0], (1, 0, 2, 3)).reshape(local, rows, hidden)
    saved_pre = jnp.pad(saved_pre, ((0, 0), (0, padded - rows), (0, 0)))
    backs = []
    got = exchange(send)
    for part in range(parts):
        if part + 1 < parts:
            got = [got[d] for d in start_order(len(got))]
            sends, saved_pre, got = lax.optimization_barrier((sends, saved_pre, got))
            got = by_block(got)
            blocks = len(blocks_of(there[part + 1], width))
            coming = exchange(sends[:blocks])
            sends = sends[blocks:]
        result = blocks_of(back[part], width + LANES)
        done = call(
            functools.partial(expert_kernel, sizes, part, held),
            tuple(result),
            (8 * held * padded * width * hidden, 4 * held * width * hidden),
            vmem=EXPERT_VMEM,
            in_specs=[HBM] * 3 + [VMEM] * len(got),
            out_specs=(VMEM,) * len(result),
            scratch_shapes=[
                pltpu.VMEM((2 * held * padded, width), BF16),
                pltpu.VMEM((2 * held * padded, width + LANES), BF16),
                pltpu.VMEM((held, padded, hidden), BF16),
                pltpu.VMEM((min(2, held), width, hidden), BF16),
                pltpu.VMEM((min(2, held), hidden, width), BF16),
                pltpu.SemaphoreType.DMA,
                pltpu.SemaphoreType.DMA((min(2, held), 2, 2)),
            ],
        )(saved_pre, up_weight, down_weight, *[got[d] for d in start_order(len(got))])
        backs.append(exchange(list(done)))
        got = coming if part + 1 < parts else None
    handed = (
        upstream, norm_gain, routes_b, shares_b,
    )
    own = (*mixing[-1], backs[-1][0]) if back[-1] else ()
    early = call(
        functools.partial(early_kernel, sizes, len(handed)),
        (
            shape((count, width), F32),
            shape((count, width), F32),
            shape((top, 8, count), F32),
            *[shape(array.shape, array.dtype) for array in handed],
        ),
        (4 * moved * count * width, 2 * (10 * count + moved) * width),
    )(tokens, *handed, *[ref for part in range(parts - 1) for ref in (*mixing[part], *backs[part])], *own)
    return tuple(
        call(
            functools.partial(late_kernel, sizes),
            (shape((1, count, width), BF16),) * 2,
            (4 * moved * count * width, 2 * (8 * count + moved) * width),
        )(
            *early,
            saved_inputs[0],
            router_t,
            *mixing[-1],
            *[backs[-1][d] for d in start_order(len(backs[-1])) if d > 0 or not back[-1]],
        )
    )


def solution(mesh):
    return jax.shard_map(
        on_device,
        mesh=mesh,
        in_specs=(
            P("section", "expert", None),
            P("expert", None),
            P("section", "expert", None),
            P("section", "expert", None),
            P("expert", None),
            P("section", "expert", None),
            P("section", "expert", None),
            P("section", None, "expert", None, None),
            P("section", None),
            P("section", None, None),
            P("expert", None, None),
            P("expert", None, None),
        ),
        out_specs=(P("section", "expert", None), P("section", "expert", None)),
        check_vma=False,
    )
```
